32 devices in a mesh: wide: 8 (over y, x, core), narrow: 4 (over z).
Axes of the slice: x: 2, y: 2, z: 4, core: 2. Of those that a mesh axis runs over, the one named last changes fastest.
Arguments:
- tokens: bfloat16 [32768, 768], P(('wide', 'narrow')), may hold values from -5.6 to 5.6
- cotangent: bfloat16 [32768, 768], P(('wide', 'narrow')), may hold values from -6 to 6
- qkv_w: bfloat16 [2, 768, 2304], P(None, ('wide', 'narrow'))
- out_w: bfloat16 [2, 768, 768], P(None, ('wide', 'narrow')), may hold values from -0.3125 to 0.3125
- in_w: bfloat16 [2, 768, 3072], P(None, ('wide', 'narrow')), may hold values from -0.21875 to 0.21875
- in_b: bfloat16 [2, 3072], P(None, ('wide', 'narrow')), may hold values from -3 to 3
- out2_w: bfloat16 [2, 3072, 768], P(None, ('wide', 'narrow')), may hold values from -0.109375 to 0.109375
- bias_rows: bfloat16 [2, 6, 768], P(None, None, ('wide', 'narrow')), may hold values from -3 to 3
- gain_rows: bfloat16 [2, 2, 768], P(None, None, ('wide', 'narrow')), may hold values from 0.25 to 1.75
- conv_w: bfloat16 [2, 12, 33], replicated, may hold values from -1 to 1
Outputs:
- output: bfloat16 [32768, 768], P(('wide', 'narrow'))
- grad_input: float32 [32768, 768], P(('wide', 'narrow'))
- grad_qkv_w: float32 [2, 768, 2304], P(None, ('wide', 'narrow'))
- grad_out_w: float32 [2, 768, 768], P(None, ('wide', 'narrow'))
- grad_in_w: float32 [2, 768, 3072], P(None, ('wide', 'narrow'))
- grad_in_b: float32 [2, 3072], P(None, ('wide', 'narrow'))
- grad_out2_w: float32 [2, 3072, 768], P(None, ('wide', 'narrow'))
- grad_bias_rows: float32 [2, 6, 768], P(None, None, ('wide', 'narrow'))
- grad_gain_rows: float32 [2, 2, 768], P(None, None, ('wide', 'narrow'))
- grad_conv_w: float32 [2, 12, 33], replicated
The draws below stay inside these ranges and needn't reach their ends.
All inputs are finite; a program needn't handle non-finite values.
Results may differ from the reference program's by a relative error of at most 0.02.
Values may be sent and summed in bfloat16 or wider, within the bound.
A program may use at most 384 MiB of HBM per device.

```python
import jax
import jax.numpy as jnp
from jax import lax

MODEL_WIDTH = 768
HEADS = 12
HEAD_DIM = 64
FF = 3072
LANDMARKS = 64
KSIZE = 33
NS_ITERS = 6
LAYERS = 2
SEQ = 1024
TOKENS = 32768


def draw_tokens(key, part):
    seg_len = SEQ // LANDMARKS
    first_key, second_key = jax.random.split(key)
    noise = jnp.clip(jax.random.normal(first_key, (TOKENS, MODEL_WIDTH), jnp.float32), -4.0, 4.0)
    slower = jnp.clip(jax.random.normal(second_key, (TOKENS // seg_len, MODEL_WIDTH), jnp.float32), -4.0, 4.0)
    slower = jnp.repeat(slower, seg_len, axis=0)
    return (0.7 * noise + 0.7 * slower).astype(jnp.bfloat16)


def draw_qkv_w(key, part):
    shape = (LAYERS, MODEL_WIDTH, MODEL_WIDTH)
    scale = (MODEL_WIDTH // 2) ** (-0.5)
    query_key, key_key, value_key = jax.random.split(jax.random.fold_in(key, 11), 3)
    query_part = jnp.clip(jax.random.normal(query_key, shape, jnp.float32), -4.0, 4.0)
    key_part = jnp.clip(jax.random.normal(key_key, shape, jnp.float32), -4.0, 4.0)
    value_part = jnp.clip(jax.random.normal(value_key, shape, jnp.float32), -4.0, 4.0)
    key_part = 0.55 * query_part + 0.83 * key_part
    whole = jnp.concatenate([query_part, key_part, value_part], axis=2) * scale
    return whole.astype(jnp.bfloat16)


def block_levels(rng, shape, cuts, least, high):
    factor_of, own = 1.0, jax.random.fold_in(rng, 6)
    for position, shards_of in cuts:
        steps = jnp.exp(jax.random.uniform(jax.random.fold_in(own, position), (shards_of,), jnp.float32, least / len(cuts), high / len(cuts)))
        factor_of = factor_of * jnp.repeat(steps, shape[position] // shards_of).reshape([-1 if axis == position else 1 for axis in range(len(shape))])
    return factor_of


def gaussian(rng, dims, width, bound, cuts=(), held_as=jnp.bfloat16):
    level = block_levels(rng, dims, cuts, -0.22, 0.18) if cuts else 1.0
    entries = jax.random.normal(rng, dims, jnp.float32) * width * level
    return jnp.minimum(jnp.maximum(entries, -bound), bound).astype(held_as)


def setup_inputs(seed: int = 0) -> dict:
    streams_of = jax.random.split(jax.random.key(seed), 11)
    tokens = draw_tokens(jax.random.fold_in(streams_of[10], 71), 0)
    cotangent = gaussian(streams_of[1], (TOKENS, MODEL_WIDTH), 1.0, 6.0, ((0, 32),))
    qkv_w = draw_qkv_w(jax.random.fold_in(streams_of[10], 71), 0)
    out_w = gaussian(streams_of[3], (LAYERS, MODEL_WIDTH, MODEL_WIDTH), (MODEL_WIDTH // 2) ** -0.5, 0.3125, ((1, 32),))
    in_w = gaussian(streams_of[4], (LAYERS, MODEL_WIDTH, FF), MODEL_WIDTH ** -0.5, 0.21875, ((1, 32),))
    in_b = gaussian(streams_of[5], (LAYERS, FF), 0.5, 3.0, ((1, 32),))
    out2_w = gaussian(streams_of[6], (LAYERS, FF, MODEL_WIDTH), FF ** -0.5, 0.109375, ((1, 32),))
    bias_rows = gaussian(streams_of[7], (LAYERS, 6, MODEL_WIDTH), 0.5, 3.0, ((2, 32),))
    gain_rows = jnp.clip(1.0 + 0.15 * jax.random.normal(streams_of[8], (LAYERS, 2, MODEL_WIDTH), jnp.float32), 0.25, 1.75).astype(jnp.bfloat16)
    conv_w = gaussian(streams_of[9], (LAYERS, HEADS, KSIZE), KSIZE ** -0.5, 1.0)
    return {"tokens": tokens, "cotangent": cotangent, "qkv_w": qkv_w, "out_w": out_w, "in_w": in_w, "in_b": in_b, "out2_w": out2_w, "bias_rows": bias_rows, "gain_rows": gain_rows, "conv_w": conv_w}


HIGH_ACCURACY = lax.Precision.HIGHEST
EPSILON = 1e-05

@jax.custom_vjp
def low(v):
    return lax.optimization_barrier(v.astype(jnp.bfloat16)).astype(jnp.float32)

@jax.custom_vjp
def low_back(v):
    return v

def low_keep(v):
    return (low(v), None)

def low_pass(kept, grad):
    return (grad,)

def back_keep(v):
    return (v, None)

def back_low(kept, grad):
    return (low(grad),)
low.defvjp(low_keep, low_pass)
low_back.defvjp(back_keep, back_low)

def matmul_high(left, right):
    return jnp.dot(left, right, precision=HIGH_ACCURACY)

def layer_norm(values_in, gain_row, shift_row):
    center = values_in - lax.optimization_barrier(jnp.mean(values_in, axis=-1, keepdims=True))
    spread = lax.optimization_barrier(jnp.mean(center * center, axis=-1, keepdims=True))
    return center * lax.rsqrt(spread + EPSILON) * gain_row + shift_row

def newton(adjacent):
    identity = jnp.eye(adjacent.shape[-1], dtype=jnp.float32)
    score_scale = 1.0 / lax.optimization_barrier(jnp.sum(adjacent * adjacent, axis=(1, 2), keepdims=True))
    pseudo_inverse = jnp.swapaxes(adjacent, 1, 2) * score_scale
    for repeat in range(NS_ITERS):
        product = jnp.einsum('hij,hjk->hik', adjacent, pseudo_inverse, precision=HIGH_ACCURACY)
        bracket = 7.0 * identity - product
        bracket = 15.0 * identity - jnp.einsum('hij,hjk->hik', product, bracket, precision=HIGH_ACCURACY)
        bracket = 13.0 * identity - jnp.einsum('hij,hjk->hik', product, bracket, precision=HIGH_ACCURACY)
        pseudo_inverse = 0.25 * jnp.einsum('hij,hjk->hik', pseudo_inverse, bracket, precision=HIGH_ACCURACY)
    return pseudo_inverse

def attention(inputs, qkv_full, bias_query, bias_value, kernel):
    sequence_length = inputs.shape[0]
    seg_len = sequence_length // LANDMARKS
    score_scale = HEAD_DIM ** (-0.5)
    inputs_low = low(inputs)
    mixed_rows = matmul_high(inputs_low, qkv_full)
    queries = low(low_back(mixed_rows[:, :MODEL_WIDTH] + bias_query))
    key_rows = low(low_back(mixed_rows[:, MODEL_WIDTH:2 * MODEL_WIDTH]))
    value_rows = low(low_back(mixed_rows[:, 2 * MODEL_WIDTH:] + bias_value))
    query_per_head = queries.reshape(sequence_length, HEADS, HEAD_DIM)
    key_per_head = key_rows.reshape(sequence_length, HEADS, HEAD_DIM)
    value_per_head = value_rows.reshape(sequence_length, HEADS, HEAD_DIM)
    query_anchors = low(lax.optimization_barrier(jnp.mean(query_per_head.reshape(LANDMARKS, seg_len, HEADS, HEAD_DIM), axis=1)))
    key_anchors = low(lax.optimization_barrier(jnp.mean(key_per_head.reshape(LANDMARKS, seg_len, HEADS, HEAD_DIM), axis=1)))
    softmax_query_anchors = jax.nn.softmax(jnp.einsum('yfb,rfb->fry', query_per_head, key_anchors, precision=HIGH_ACCURACY) * score_scale, axis=1)
    softmax_anchor_pairs = jax.nn.softmax(jnp.einsum('xow,zow->oxz', query_anchors, key_anchors, precision=HIGH_ACCURACY) * score_scale, axis=2)
    softmax_key_anchors = jax.nn.softmax(jnp.einsum('prb,irb->rpi', query_anchors, key_per_head, precision=HIGH_ACCURACY) * score_scale, axis=2)
    pseudo_inverse = newton(softmax_anchor_pairs)
    anchor_summary = low_back(jnp.einsum('ika,aip->ikp', low(softmax_key_anchors), value_per_head, precision=HIGH_ACCURACY))
    small_product = low(jnp.einsum('ies,isr->ier', pseudo_inverse, anchor_summary, precision=HIGH_ACCURACY))
    attended_output = jnp.einsum('oer,oel->rol', low(softmax_query_anchors), small_product, precision=HIGH_ACCURACY).reshape(sequence_length, MODEL_WIDTH)
    kernel_cols = jnp.repeat(kernel, HEAD_DIM, axis=0)
    radius = KSIZE // 2
    padded = jnp.pad(value_rows, ((radius, radius), (0, 0)))
    conv_out = jnp.zeros_like(attended_output)
    for offset in range(KSIZE):
        conv_out = conv_out + kernel_cols[:, offset] * padded[offset:offset + sequence_length]
    return low(low_back(attended_output + conv_out))

def layer(inputs, qkv_full, out_full, in_full, in_bias, out2_full, bias_rows, gain_rows, kernel):
    context = attention(inputs, qkv_full, bias_rows[0], bias_rows[1], kernel)
    projected = low_back(matmul_high(context, out_full) + bias_rows[2])
    normed = layer_norm(projected + inputs, gain_rows[0], bias_rows[3])
    hidden = low_back(matmul_high(low(normed), in_full) + in_bias)
    active = low(jax.nn.gelu(hidden, approximate=False))
    branch = low_back(matmul_high(active, out2_full) + bias_rows[4])
    return layer_norm(branch + normed, gain_rows[1], bias_rows[5])

def forward(inputs, params):
    current = inputs
    for layer_id in range(LAYERS):
        current = layer(current, *[param[layer_id] for param in params])
    return current

def reference(tokens, cotangent, qkv_w, out_w, in_w, in_b, out2_w, bias_rows, gain_rows, conv_w):
    params = tuple((param.astype(jnp.float32) for param in (qkv_w, out_w, in_w, in_b, out2_w, bias_rows, gain_rows, conv_w)))
    seq_count = TOKENS // SEQ
    seq_inputs = tokens.astype(jnp.float32).reshape(seq_count, SEQ, MODEL_WIDTH)
    seq_cots = cotangent.astype(jnp.float32).reshape(seq_count, SEQ, MODEL_WIDTH)

    def one_sequence(running, seq_item):
        seq_input, seq_cot = seq_item
        result, pull_back = jax.vjp(forward, seq_input, params)
        grad_seq, grad_params = pull_back(seq_cot)
        return (jax.tree.map(jnp.add, running, grad_params), (result.astype(jnp.bfloat16), grad_seq))
    zero_grads = jax.tree.map(jnp.zeros_like, params)
    totals, (outputs, grads_seq) = lax.scan(one_sequence, zero_grads, (seq_inputs, seq_cots))
    return (outputs.reshape(TOKENS, MODEL_WIDTH), grads_seq.reshape(TOKENS, MODEL_WIDTH), totals[0], totals[1], totals[2], totals[3], totals[4], totals[5], totals[6], totals[7])
```

```python
import functools
import jax
import jax.numpy as jnp
import numpy as np
from jax import lax
from jax.experimental import pallas as pl
from jax.experimental.pallas import tpu as pltpu
from jax.sharding import PartitionSpec as P

D = 768
HEADS = 12
HD = 64
FF = 3072
LM = 64
KSIZE = 33
RADIUS = KSIZE // 2
NS_ITERS = 6
T = 1024
SEG = T // LM
SCALE = HD ** -0.5
EPS = 1e-05
CONV_N = 256
CONV_K = 512
CONV_BLOCKS = T // CONV_N
LEAD = 128
f32 = jnp.float32
bf16 = jnp.bfloat16
AXES = ("wide", "narrow")
NN = (((1,), (0,)), ((), ()))
NT = (((1,), (1,)), ((), ()))
TN = (((0,), (0,)), ((), ()))
VMEM_LIMIT = 60 * 1024 * 1024


def dot(a, b, dims):
    return lax.dot_general(a, b, dims, preferred_element_type=f32)


def split(a):
    high = a.astype(bf16)
    return high, (a - high.astype(f32)).astype(bf16)


def dot3(a, b, dims):
    return dot(a[0], b[0], dims) + (dot(a[0], b[1], dims) + dot(a[1], b[0], dims))


def rows(start, size):
    if isinstance(start, int):
        return pl.ds(start, size)
    return pl.ds(pl.multiple_of(start, size), size)


def segment_mean():
    token = lax.broadcasted_iota(jnp.int32, (T, LM), 0)
    seg = lax.broadcasted_iota(jnp.int32, (T, LM), 1)
    return jnp.where(token // SEG == seg, 1.0 / SEG, 0.0).astype(bf16)


def segment_spread():
    token = lax.broadcasted_iota(jnp.int32, (LM, T), 1)
    seg = lax.broadcasted_iota(jnp.int32, (LM, T), 0)
    return jnp.where(token // SEG == seg, 1.0, 0.0).astype(bf16)


def eye(value):
    i = lax.broadcasted_iota(jnp.int32, (LM, LM), 0)
    j = lax.broadcasted_iota(jnp.int32, (LM, LM), 1)
    return jnp.where(i == j, value, 0.0).astype(f32)


def toeplitz(row):
    full = jnp.broadcast_to(row, (CONV_N, CONV_K))
    return pltpu.roll(full, 0, 1, stride=1, stride_axis=0).astype(bf16)


def windows(ref, base):
    return jnp.concatenate(
        [ref[rows(base, HD), CONV_N * b : CONV_N * b + CONV_K] for b in range(CONV_BLOCKS)], axis=0
    )


def stack_blocks(value):
    return jnp.concatenate(
        [value[:, CONV_N * b : CONV_N * (b + 1)] for b in range(CONV_BLOCKS)], axis=0
    )


def unstack_blocks(value):
    return jnp.concatenate(
        [value[HD * b : HD * (b + 1), :] for b in range(CONV_BLOCKS)], axis=1
    )


def norm_forward(r_ref, xhat_ref, rstd_ref, width=128):
    for c in range(0, T, width):
        r = r_ref[:, c : c + width]
        center = r - jnp.mean(r, axis=0, keepdims=True)
        rstd = lax.rsqrt(jnp.mean(center * center, axis=0, keepdims=True) + EPS)
        xhat_ref[:, c : c + width] = center * rstd
        rstd_ref[:, c : c + width] = jnp.broadcast_to(rstd, (8, width))


def attention_forward_kernel(
    n_pieces, p, starts_ref, x_ref, par_ref, conv_ref, *rest
):
    pieces = rest[:n_pieces]
    (xl_ref, mix_ref, ctx_ref, f_ref, b_ref, lm_ref, a_ref, ns_ref, small_ref, xhat_ref, rstd_ref,
     w_ref, vpad_ref, z_ref, sem) = rest[n_pieces:]
    r = pieces[0].shape[0]
    loads = []
    for i in range(n_pieces):
        copy = pltpu.make_async_copy(
            pieces[i].at[:, pl.ds(0, 4 * D)], w_ref.at[pl.ds(pl.multiple_of(starts_ref[i] * r, r), r), :], sem.at[i])
        copy.start()
        loads.append(copy)
    vpad_ref[:, 0:LEAD] = jnp.zeros((D, LEAD), bf16)
    vpad_ref[:, LEAD + T :] = jnp.zeros((D, LEAD), bf16)
    xl_ref[...] = x_ref[...].astype(bf16)
    for copy in loads:
        copy.wait()

    for part, column in ((0, p), (1, None), (2, p + 1)):

        def mix_step(i, _):
            at = rows(part * D + i * 256, 256)
            got = dot(w_ref[:, at], xl_ref[...], TN)
            if column is not None:
                got = got + par_ref[rows(i * 256, 256), column : column + 1]
            mix_ref[at, :] = got.astype(bf16)
            return 0

        lax.fori_loop(0, 3, mix_step, 0)
    vpad_ref[:, LEAD : LEAD + T] = mix_ref[2 * D :, :]
    mean = segment_mean()
    lm_ref[...] = dot(mix_ref[0 : 2 * D, :], mean, NN).astype(bf16)

    for h in range(HEADS):
        ql = lm_ref[h * HD : (h + 1) * HD, :]
        kl = lm_ref[D + h * HD : D + (h + 1) * HD, :]
        s = dot(ql, kl, TN) * SCALE
        e = jnp.exp(s - jnp.max(s, axis=1, keepdims=True))
        a = e / jnp.sum(e, axis=1, keepdims=True)
        a_ref[h] = a
        z_ref[h] = a.T / jnp.sum(a * a)

    def ns_step(k, _):
        ps, rs = [], []
        for h in range(HEADS):
            z = z_ref[h]
            ns_ref[k, 0, h] = z
            p = dot3(split(a_ref[h]), split(z), NN)
            ns_ref[k, 1, h] = p
            ps.append(split(p))
            rs.append(split(eye(7.0) - p))
        for h in range(HEADS):
            r2 = eye(15.0) - dot3(ps[h], rs[h], NN)
            ns_ref[k, 2, h] = r2
            rs[h] = split(r2)
        for h in range(HEADS):
            r3 = eye(13.0) - dot3(ps[h], rs[h], NN)
            ns_ref[k, 3, h] = r3
            rs[h] = split(r3)
        for h in range(HEADS):
            z_ref[h] = 0.25 * dot3(split(z_ref[h]), rs[h], NN)
        return 0

    lax.fori_loop(0, NS_ITERS, ns_step, 0)

    def head_step(h, _):
        base = h * HD
        q = mix_ref[rows(base, HD), :]
        k = mix_ref[rows(D + base, HD), :]
        v = mix_ref[rows(2 * D + base, HD), :]
        ql = lm_ref[rows(base, HD), :]
        kl = lm_ref[rows(D + base, HD), :]
        s = dot(kl, q, TN) * SCALE
        e = jnp.exp(s - jnp.max(s, axis=0, keepdims=True))
        f = (e / jnp.sum(e, axis=0, keepdims=True)).astype(bf16)
        f_ref[rows(base, HD), :] = f
        s = dot(ql, k, TN) * SCALE
        e = jnp.exp(s - jnp.max(s, axis=1, keepdims=True))
        b = (e / jnp.sum(e, axis=1, keepdims=True)).astype(bf16)
        b_ref[rows(base, HD), :] = b
        bv = dot(b, v, NT)
        z = z_ref[h]
        w = dot3(split(z), split(bv), NN)
        small_ref[0, h] = z
        small_ref[1, h] = bv
        small_ref[2, h] = w
        attended = dot(w.astype(bf16), f, TN)
        conv = dot(windows(vpad_ref, base), toeplitz(conv_ref[h, 0:1]), NT)
        ctx_ref[rows(base, HD), :] = (attended + unstack_blocks(conv)).astype(bf16)
        return 0

    lax.fori_loop(0, HEADS, head_step, 0)

    def out_step(i, _):
        base = i * 256
        got = dot(w_ref[:, pl.ds(pl.multiple_of(3 * D + base, 256), 256)], ctx_ref[...], TN)
        xhat_ref[rows(base, 256), :] = got + par_ref[rows(base, 256), p + 2 : p + 3] + x_ref[rows(base, 256), :]
        return 0

    lax.fori_loop(0, 3, out_step, 0)
    norm_forward(xhat_ref, xhat_ref, rstd_ref)


def vm():
    return pl.BlockSpec(memory_space=pltpu.VMEM)


def attention_forward(x, pieces, starts, par, conv, layer):
    n = len(pieces)
    sd = jax.ShapeDtypeStruct
    return pl.pallas_call(
        functools.partial(attention_forward_kernel, n, 8 * layer),
        out_shape=[
            sd((D, T), bf16), sd((3 * D, T), bf16), sd((D, T), bf16), sd((D, T), bf16), sd((D, T), bf16),
            sd((2 * D, LM), bf16), sd((HEADS, LM, LM), f32), sd((NS_ITERS, 4, HEADS, LM, LM), f32),
            sd((3, HEADS, LM, LM), f32), sd((D, T), f32), sd((8, T), f32),
        ],
        in_specs=[pl.BlockSpec(memory_space=pltpu.SMEM), vm(), vm(), vm()]
        + [pl.BlockSpec(memory_space=pl.ANY)] * n,
        out_specs=[vm()] * 11,
        scratch_shapes=[
            pltpu.VMEM((D, 4 * D), bf16),
            pltpu.VMEM((D, T + 2 * LEAD), bf16),
            pltpu.VMEM((HEADS, LM, LM), f32),
            pltpu.SemaphoreType.DMA((n,)),
        ],
        compiler_params=pltpu.CompilerParams(vmem_limit_bytes=VMEM_LIMIT),
        cost_estimate=pl.CostEstimate(flops=6_500_000_000, bytes_accessed=30_000_000, transcendentals=2_000_000),
        name="attention_forward",
    )(starts, x, par, conv, *pieces)


CHUNK = 768
STEPS = FF // CHUNK
SUB = 256


def feed_forward_kernel(n_in, n_out, p, last, in_starts, out_starts, xhat_ref, par_ref, inb_ref, *rest):
    in_pieces, rest = rest[:n_in], rest[n_in:]
    out_pieces, rest = rest[:n_out], rest[n_out:]
    (a_ref, g_ref, xhat2_ref, rstd2_ref, next_ref, w1_ref, w2_ref, hl_ref, sem1, sem2) = rest
    j = pl.program_id(0)
    r1, r2 = in_pieces[0].shape[0], out_pieces[0].shape[0]

    def load1(i):
        return pltpu.make_async_copy(
            in_pieces[i], w1_ref.at[pl.ds(pl.multiple_of(in_starts[i] * r1, r1), r1), :], sem1.at[i])

    def load2(i):
        return pltpu.make_async_copy(
            out_pieces[i], w2_ref.at[pl.ds(pl.multiple_of(out_starts[i] * r2, r2), r2), :], sem2.at[i])

    @pl.when(j == 0)
    def _():
        for i in range(n_in):
            load1(i).start()
        for i in range(n_out):
            load2(i).start()
        h = xhat_ref[...] * par_ref[:, p + 6 : p + 7] + par_ref[:, p + 3 : p + 4]
        hl_ref[...] = h.astype(bf16)
        xhat2_ref[...] = h + par_ref[:, p + 4 : p + 5]
        for i in range(n_in):
            load1(i).wait()
        for i in range(n_out):
            load2(i).wait()

    def up_step(i, _):
        base = i * SUB
        at = j * CHUNK + base
        u = dot(w1_ref[:, pl.ds(pl.multiple_of(at, SUB), SUB)], hl_ref[...], TN)
        u = u + inb_ref[rows(at, SUB), 0:1]
        cdf = 0.5 + 0.5 * lax.erf(u * (2.0 ** -0.5))
        pdf = jnp.exp(-0.5 * u * u) * ((2.0 * np.pi) ** -0.5)
        a_ref[rows(base, SUB), :] = (u * cdf).astype(bf16)
        g_ref[rows(base, SUB), :] = (cdf + u * pdf).astype(bf16)
        return 0

    lax.fori_loop(0, CHUNK // SUB, up_step, 0)

    def down_step(i, _):
        base = i * SUB
        xhat2_ref[rows(base, SUB), :] += dot(
            w2_ref[rows(j * CHUNK, CHUNK), pl.ds(pl.multiple_of(base, SUB), SUB)], a_ref[...], TN)
        return 0

    lax.fori_loop(0, D // SUB, down_step, 0)

    @pl.when(j == STEPS - 1)
    def _():
        norm_forward(xhat2_ref, xhat2_ref, rstd2_ref)
        y = xhat2_ref[...] * par_ref[:, p + 7 : p + 8] + par_ref[:, p + 5 : p + 6]
        if last:
            next_ref[...] = y.T.astype(bf16)
        else:
            next_ref[...] = y


def feed_forward(xhat, in_pieces, out_pieces, in_starts, out_starts, par, inb, layer, last):
    n1, n2 = len(in_pieces), len(out_pieces)
    sd = jax.ShapeDtypeStruct
    smem = pl.BlockSpec(memory_space=pltpu.SMEM)
    anyspec = pl.BlockSpec(memory_space=pl.ANY)
    whole = lambda *s: pl.BlockSpec(s, lambda j: (0,) * len(s))
    next_shape = (T, D) if last else (D, T)
    return pl.pallas_call(
        functools.partial(feed_forward_kernel, n1, n2, 8 * layer, last),
        grid=(STEPS,),
        out_shape=[
            sd((FF, T), bf16), sd((FF, T), bf16), sd((D, T), f32), sd((8, T), f32),
            sd(next_shape, bf16 if last else f32),
        ],
        in_specs=[smem, smem, whole(D, T), whole(D, 128), whole(FF, 1)] + [anyspec] * (n1 + n2),
        out_specs=[
            pl.BlockSpec((CHUNK, T), lambda j: (j, 0)), pl.BlockSpec((CHUNK, T), lambda j: (j, 0)),
            whole(D, T), whole(8, T), whole(*next_shape),
        ],
        scratch_shapes=[
            pltpu.VMEM((D, FF), bf16), pltpu.VMEM((FF, D), bf16), pltpu.VMEM((D, T), bf16),
            pltpu.SemaphoreType.DMA((n1,)), pltpu.SemaphoreType.DMA((n2,)),
        ],
        compiler_params=pltpu.CompilerParams(vmem_limit_bytes=VMEM_LIMIT),
        cost_estimate=pl.CostEstimate(flops=9_700_000_000, bytes_accessed=30_000_000, transcendentals=6_000_000),
        name="feed_forward",
    )(in_starts, out_starts, xhat, par, inb, *in_pieces, *out_pieces)


def norm_backward(dy_ref, xhat_ref, rstd_ref, gain, out_ref, grads_ref, gain_col, shift_col, width=128):
    total_gain = jnp.zeros((D, width), f32)
    total_shift = jnp.zeros((D, width), f32)
    for c in range(0, T, width):
        dy = dy_ref[:, c : c + width]
        xhat = xhat_ref[:, c : c + width]
        total_shift = total_shift + dy
        total_gain = total_gain + dy * xhat
        dxhat = dy * gain
        m1 = jnp.mean(dxhat, axis=0, keepdims=True)
        m2 = jnp.mean(dxhat * xhat, axis=0, keepdims=True)
        out_ref[:, c : c + width] = rstd_ref[0:1, c : c + width] * (dxhat - m1 - xhat * m2)
    grads_ref[:, gain_col : gain_col + 1] = jnp.sum(total_gain, axis=1, keepdims=True)
    grads_ref[:, shift_col : shift_col + 1] = jnp.sum(total_shift, axis=1, keepdims=True)


def lane_sum(value):
    return jnp.sum(value.astype(f32), axis=1, keepdims=True)


def permute_rows(dst_ref, src_ref, order_ref, offset, block):
    for i in range(D // block):
        dst_ref[i * block : (i + 1) * block, :] = src_ref[
            pl.ds(pl.multiple_of(order_ref[offset + i] * block, block), block), :]


def feed_backward_kernel(
    n_in, n_out, p, first, order_ref, dy_ref, xhat2_ref, rstd2_ref, xhat1_ref, rstd1_ref, par_ref, a_ref, g_ref, *rest
):
    in_pieces, rest = rest[:n_in], rest[n_in:]
    out_pieces, rest = rest[:n_out], rest[n_out:]
    (keep2_ref, send2_ref, keep1_ref, send1_ref, inb_ref, dr1_ref, cols_ref,
     w1_ref, w2_ref, hl_ref, dz_ref, du_ref, acc_ref, sem1, sem2) = rest
    j = pl.program_id(0)
    r1, r2 = in_pieces[0].shape[0], out_pieces[0].shape[0]

    def load1(i):
        return pltpu.make_async_copy(
            in_pieces[i], w1_ref.at[pl.ds(pl.multiple_of(order_ref[IN_AT + i] * r1, r1), r1), :], sem1.at[i])

    def load2(i):
        return pltpu.make_async_copy(
            out_pieces[i], w2_ref.at[pl.ds(pl.multiple_of(order_ref[IN_AT + i] * r2, r2), r2), :], sem2.at[i])

    @pl.when(j == 0)
    def _():
        for i in range(n_out):
            load2(i).start()
        for i in range(n_in):
            load1(i).start()
        if first:
            acc_ref[...] = dy_ref[...].astype(f32).T
            dy = acc_ref
        else:
            dy = dy_ref
        cols_ref[...] = jnp.zeros_like(cols_ref)
        norm_backward(dy, xhat2_ref, rstd2_ref, par_ref[:, p + 7 : p + 8], acc_ref, cols_ref, 7, 5)
        dz_ref[...] = acc_ref[...].astype(bf16)
        cols_ref[:, 4:5] = lane_sum(dz_ref[...])
        block = D // 8
        for i in range(8):
            at = pl.ds(pl.multiple_of(order_ref[ROW_AT + i] * block, block), block)
            hl_ref[i * block : (i + 1) * block, :] = (
                xhat1_ref[at, :] * par_ref[at, p + 6 : p + 7] + par_ref[at, p + 3 : p + 4]).astype(bf16)
        for i in range(n_out):
            load2(i).wait()
        for i in range(n_in):
            load1(i).wait()

    def du_step(i, _):
        base = i * SUB
        da = dot(w2_ref[rows(j * CHUNK + base, SUB), :], dz_ref[...], NN)
        du = (da * g_ref[rows(base, SUB), :].astype(f32)).astype(bf16)
        du_ref[rows(base, SUB), :] = du
        inb_ref[rows(base, SUB), :] = lane_sum(du)
        return 0

    lax.fori_loop(0, CHUNK // SUB, du_step, 0)
    half = CHUNK // 2
    core = order_ref[CORE_AT]
    keep2_ref[0] = dot(a_ref[rows(core * half, half), :], dz_ref[...], NT).astype(bf16)
    send2_ref[0] = dot(a_ref[rows((1 - core) * half, half), :], dz_ref[...], NT).astype(bf16)

    for i, out_ref in enumerate((keep1_ref, send1_ref)):
        out_ref[...] = dot(hl_ref[i * (D // 2) : (i + 1) * (D // 2), :], du_ref[...], NT).astype(bf16)

    def dh_step(i, _):
        acc_ref[rows(i * SUB, SUB), :] += dot(
            w1_ref[rows(i * SUB, SUB), rows(j * CHUNK, CHUNK)], du_ref[...], NN)
        return 0

    lax.fori_loop(0, D // SUB, dh_step, 0)

    @pl.when(j == STEPS - 1)
    def _():
        norm_backward(acc_ref, xhat1_ref, rstd1_ref, par_ref[:, p + 6 : p + 7], dr1_ref, cols_ref, 6, 3)
        cols_ref[:, 2:3] = lane_sum(dr1_ref[...].astype(bf16))


IN_AT = 0
ROW_AT = 8
KEEP_AT = 16
SEND_AT = 20
CORE_AT = 24


def feed_backward(dy, xhat2, rstd2, xhat1, rstd1, par, a, g, in_pieces, out_pieces, order, layer, first):
    n1, n2 = len(in_pieces), len(out_pieces)
    sd = jax.ShapeDtypeStruct
    anyspec = pl.BlockSpec(memory_space=pl.ANY)
    whole = lambda *s: pl.BlockSpec(s, lambda j, o: (0,) * len(s))
    chunk = pl.BlockSpec((CHUNK, T), lambda j, o: (j, 0))
    half = CHUNK // 2
    return pl.pallas_call(
        functools.partial(feed_backward_kernel, n1, n2, 8 * layer, first),
        grid_spec=pltpu.PrefetchScalarGridSpec(
            num_scalar_prefetch=1,
            grid=(STEPS,),
            in_specs=[whole(*dy.shape), whole(D, T), whole(8, T), whole(D, T), whole(8, T), whole(D, 128), chunk, chunk]
            + [anyspec] * (n1 + n2),
            out_specs=[
                pl.BlockSpec((1, half, D), lambda j, o: (o[KEEP_AT + j], 0, 0)),
                pl.BlockSpec((1, half, D), lambda j, o: (o[SEND_AT + j], 0, 0)),
                pl.BlockSpec((D // 2, CHUNK), lambda j, o: (0, j)), pl.BlockSpec((D // 2, CHUNK), lambda j, o: (0, j)),
                pl.BlockSpec((CHUNK, 1), lambda j, o: (j, 0)),
                whole(D, T), whole(D, 8),
            ],
            scratch_shapes=[
                pltpu.VMEM((D, FF), bf16), pltpu.VMEM((FF, D), bf16), pltpu.VMEM((D, T), bf16),
                pltpu.VMEM((D, T), bf16), pltpu.VMEM((CHUNK, T), bf16), pltpu.VMEM((D, T), f32),
                pltpu.SemaphoreType.DMA((n1,)), pltpu.SemaphoreType.DMA((n2,)),
            ],
        ),
        out_shape=[
            sd((STEPS, half, D), bf16), sd((STEPS, half, D), bf16), sd((D // 2, FF), bf16), sd((D // 2, FF), bf16), sd((FF, 1), f32),
            sd((D, T), f32), sd((D, 8), f32),
        ],
        compiler_params=pltpu.CompilerParams(vmem_limit_bytes=VMEM_LIMIT),
        cost_estimate=pl.CostEstimate(flops=19_400_000_000, bytes_accessed=50_000_000, transcendentals=0),
        name="feed_backward",
    )(order, dy, xhat2, rstd2, xhat1, rstd1, par, a, g, *in_pieces, *out_pieces)


def attention_backward_kernel(
    n_pieces, first, order_ref, dr1_ref, xl_ref, mix_ref, ctx_ref, f_ref, b_ref, lm_ref, a_ref, ns_ref, small_ref,
    conv_ref, *rest
):
    pieces = rest[:n_pieces]
    (keep_ref, send_ref, dx_ref, cols_ref, taps_ref,
     w_ref, dp_ref, perm_ref, dctx_ref, dmix_ref, vpad_ref, dpad_ref, dz_ref, da_ref, sem) = rest[n_pieces:]
    r = pieces[0].shape[0]
    loads = []
    for i in range(n_pieces):
        copy = pltpu.make_async_copy(
            pieces[i].at[:, pl.ds(0, 4 * D)], w_ref.at[pl.ds(pl.multiple_of(order_ref[IN_AT + i] * r, r), r), :], sem.at[i])
        copy.start()
        loads.append(copy)
    for ref in (vpad_ref, dpad_ref):
        ref[:, 0:LEAD] = jnp.zeros((D, LEAD), bf16)
        ref[:, LEAD + T :] = jnp.zeros((D, LEAD), bf16)
    vpad_ref[:, LEAD : LEAD + T] = mix_ref[2 * D :, :]
    dp_ref[...] = dr1_ref[...].astype(bf16)
    permute_rows(perm_ref, ctx_ref, order_ref, ROW_AT, D // 8)

    for i, out_ref in enumerate((keep_ref, send_ref)):
        out_ref[:, 3 * D :] = dot(perm_ref[i * (D // 2) : (i + 1) * (D // 2), :], dp_ref[...], NT).astype(bf16)
    for copy in loads:
        copy.wait()

    def dctx_step(i, _):
        got = dot(w_ref[rows(i * SUB, SUB), 3 * D :], dp_ref[...], NN).astype(bf16)
        dctx_ref[rows(i * SUB, SUB), :] = got
        dpad_ref[rows(i * SUB, SUB), LEAD : LEAD + T] = got
        return 0

    lax.fori_loop(0, D // SUB, dctx_step, 0)
    spread = segment_spread()
    flip = jnp.where(
        lax.broadcasted_iota(jnp.int32, (CONV_N, CONV_N), 0)
        + lax.broadcasted_iota(jnp.int32, (CONV_N, CONV_N), 1) == CONV_N - 1, 1.0, 0.0).astype(bf16)

    def value_step(h, _):
        base = h * HD
        dctx = dctx_ref[rows(base, HD), :]
        f = f_ref[rows(base, HD), :]
        dw = split(dot(f, dctx, NT))
        dz_ref[h] = dot3(dw, split(small_ref[1, h]), NT)
        dbv = dot3(split(small_ref[0, h]), dw, TN)
        da_ref[h] = dbv
        vw = windows(vpad_ref, base)
        dw_ = windows(dpad_ref, base)
        dv = dot(dbv.astype(bf16), b_ref[rows(base, HD), :], TN)
        conv = dot(dw_, toeplitz(conv_ref[h, 1:2]), NT)
        dmix_ref[rows(2 * D + base, HD), :] = (dv + unstack_blocks(conv)).astype(bf16)
        flipped = dot(stack_blocks(dctx), flip, NN).astype(bf16)
        g = dot(flipped, vw, TN)
        g = pltpu.roll(g, CONV_K - CONV_N + 1, 1, stride=1, stride_axis=0)
        taps_ref[h] = jnp.sum(g, axis=0, keepdims=True)
        return 0

    lax.fori_loop(0, HEADS, value_step, 0)

    def score_b_step(h, _):
        base = h * HD
        b = b_ref[rows(base, HD), :].astype(f32)
        db = dot(da_ref[h].astype(bf16), mix_ref[rows(2 * D + base, HD), :], NN)
        ds = SCALE * b * (db - jnp.sum(b * db, axis=1, keepdims=True))
        b_out = ds.astype(bf16)
        dmix_ref[rows(D + base, HD), :] = b_out
        return 0

    lax.fori_loop(0, HEADS, score_b_step, 0)

    for h in range(HEADS):
        da_ref[h] = jnp.zeros((LM, LM), f32)

    def ns_step(i, _):
        k = NS_ITERS - 1 - i
        d3, dzs, dps, d2 = [], [], [], []
        for h in range(HEADS):
            dzn = split(0.25 * dz_ref[h])
            d3.append(split(dot3(split(ns_ref[k, 0, h]), dzn, TN)))
            dz_ref[h] = dot3(dzn, split(ns_ref[k, 3, h]), NT)
        for h in range(HEADS):
            p = split(ns_ref[k, 1, h])
            d2.append(split(-dot3(p, d3[h], TN)))
            dps.append(dot3(d3[h], split(ns_ref[k, 2, h]), NT))
        for h in range(HEADS):
            p = ns_ref[k, 1, h]
            d1 = dot3(split(p), d2[h], TN)
            dp = d1 - dps[h] - dot3(d2[h], split(eye(7.0) - p), NT)
            dps[h] = split(dp)
        for h in range(HEADS):
            da_ref[h] += dot3(dps[h], split(ns_ref[k, 0, h]), NT)
            dz_ref[h] += dot3(split(a_ref[h]), dps[h], TN)
        return 0

    lax.fori_loop(0, NS_ITERS, ns_step, 0)

    def score_step(h, _):
        base = h * HD
        a = a_ref[h]
        dz0 = dz_ref[h].T
        s = 1.0 / jnp.sum(a * a)
        da = da_ref[h] + s * dz0 - (2.0 * s * s * jnp.sum(dz0 * a)) * a
        dsa = (SCALE * a * (da - jnp.sum(a * da, axis=1, keepdims=True))).astype(bf16)
        ql = lm_ref[rows(base, HD), :]
        kl = lm_ref[rows(D + base, HD), :]
        q = mix_ref[rows(base, HD), :]
        k = mix_ref[rows(D + base, HD), :]
        f = f_ref[rows(base, HD), :].astype(f32)
        df = dot(small_ref[2, h].astype(bf16), dctx_ref[rows(base, HD), :], NN)
        dsf = (SCALE * f * (df - jnp.sum(f * df, axis=0, keepdims=True))).astype(bf16)
        dsb = dmix_ref[rows(D + base, HD), :]
        dkl = dot(q, dsf, NT) + dot(ql, dsa, NN)
        dql = dot(kl, dsa, NT) + dot(k, dsb, NT)
        dq = dot(kl, dsf, NN) + dot((dql * (1.0 / SEG)).astype(bf16), spread, NN)
        dk = dot(ql, dsb, NN) + dot((dkl * (1.0 / SEG)).astype(bf16), spread, NN)
        dmix_ref[rows(base, HD), :] = dq.astype(bf16)
        dmix_ref[rows(D + base, HD), :] = dk.astype(bf16)
        return 0

    lax.fori_loop(0, HEADS, score_step, 0)
    cols_ref[...] = jnp.zeros_like(cols_ref)
    cols_ref[:, 0:1] = lane_sum(dmix_ref[0:D, :])
    cols_ref[:, 1:2] = lane_sum(dmix_ref[2 * D :, :])
    permute_rows(perm_ref, xl_ref, order_ref, ROW_AT, D // 8)

    def gqkv_step(i, _):
        at = rows(i * D, D)
        for part, out_ref in enumerate((keep_ref, send_ref)):
            out_ref[:, at] = dot(
                perm_ref[part * (D // 2) : (part + 1) * (D // 2), :], dmix_ref[at, :], NT).astype(bf16)
        return 0

    lax.fori_loop(0, 3, gqkv_step, 0)

    def dx_step(i, _):
        got = dr1_ref[rows(i * SUB, SUB), :] + dot(w_ref[rows(i * SUB, SUB), 0 : 3 * D], dmix_ref[...], NN)
        if first:
            dx_ref[:, rows(i * SUB, SUB)] = got.T
        else:
            dx_ref[rows(i * SUB, SUB), :] = got
        return 0

    lax.fori_loop(0, D // SUB, dx_step, 0)


def attention_backward(dr1, saved, conv, pieces, order, first):
    n = len(pieces)
    sd = jax.ShapeDtypeStruct
    return pl.pallas_call(
        functools.partial(attention_backward_kernel, n, first),
        out_shape=[
            sd((D // 2, 4 * D), bf16), sd((D // 2, 4 * D), bf16), sd((T, D) if first else (D, T), f32), sd((D, 8), f32),
            sd((HEADS, 1, CONV_K), f32),
        ],
        in_specs=[pl.BlockSpec(memory_space=pltpu.SMEM)] + [vm()] * 11 + [pl.BlockSpec(memory_space=pl.ANY)] * n,
        out_specs=[vm()] * 5,
        scratch_shapes=[
            pltpu.VMEM((D, 4 * D), bf16), pltpu.VMEM((D, T), bf16), pltpu.VMEM((D, T), bf16), pltpu.VMEM((D, T), bf16),
            pltpu.VMEM((3 * D, T), bf16), pltpu.VMEM((D, T + 2 * LEAD), bf16), pltpu.VMEM((D, T + 2 * LEAD), bf16),
            pltpu.VMEM((HEADS, LM, LM), f32), pltpu.VMEM((HEADS, LM, LM), f32), pltpu.SemaphoreType.DMA((n,)),
        ],
        compiler_params=pltpu.CompilerParams(vmem_limit_bytes=VMEM_LIMIT),
        cost_estimate=pl.CostEstimate(flops=15_000_000_000, bytes_accessed=40_000_000, transcendentals=0),
        name="attention_backward",
    )(order, dr1, *saved, conv, *pieces)


class Ring:
    def __init__(self, wide, narrow):
        self.wide, self.narrow = wide, narrow
        self.bits = wide.bit_length() - 1
        up = list(range(1, self.bits))
        self.gather_order = (up, up[::-1])
        self.scatter_order = (up[::-1], up)
        self.exact = wide == 8

    def pairs(self, flip):
        n = self.narrow
        out = []
        for w in range(self.wide):
            for z in range(n):
                to_w, to_z = flip(w, z)
                out.append((w * n + z, to_w * n + to_z))
        return out

    def narrow_pairs(self, k):
        return self.pairs(lambda w, z: (w, z ^ k))

    def step_pairs(self, order, s):
        return self.pairs(lambda w, z: (w ^ (1 << order[w & 1][s]), z))

    def core_pairs(self):
        return self.pairs(lambda w, z: (w ^ 1, z))

    def gathered(self, w):
        out = []
        for other in (0, 1):
            v = w ^ other
            for code in range(self.wide // 2):
                t = v
                for s in range(self.bits - 1):
                    if code >> s & 1:
                        t ^= 1 << self.gather_order[v & 1][s]
                out.append(t)
        return out

    def slots(self, w):
        out = []
        for other in (0, 1):
            v = w ^ other
            for code in range(self.wide // 2):
                t = v
                for s in range(self.bits - 1):
                    if code >> (self.bits - 2 - s) & 1:
                        t ^= 1 << self.scatter_order[v & 1][s]
                out.append(t)
        return out

    def table(self):
        out = np.zeros((self.wide, 32), np.int32)
        for w in range(self.wide):
            if self.exact:
                got, slots = self.gathered(w), self.slots(w)
                out[w, IN_AT : IN_AT + 8] = got
                out[w, ROW_AT : ROW_AT + 8] = slots
                for slot in range(4):
                    out[w, KEEP_AT + (slots[slot] >> 1)] = slot
                    out[w, SEND_AT + (slots[4 + slot] >> 1)] = slot
                out[w, CORE_AT] = w & 1
            else:
                out[w, ROW_AT : ROW_AT + 8] = range(8)
                out[w, KEEP_AT : KEEP_AT + 4] = range(4)
                out[w, SEND_AT : SEND_AT + 4] = range(4)
        return out

    def mine(self, table):
        return lax.dynamic_index_in_dim(jnp.asarray(table), lax.axis_index("wide"), 0, keepdims=False)

    def gather(self, shard):
        z = lax.axis_index("narrow")
        parts = [shard] + [lax.ppermute(shard, AXES, self.narrow_pairs(k)) for k in range(1, self.narrow)]
        bit = 1
        while bit < self.narrow:
            swap = (z & bit) != 0
            parts = [jnp.where(swap, parts[k ^ bit], parts[k]) for k in range(self.narrow)]
            bit *= 2
        held = [jnp.concatenate(parts, axis=0)]
        for s in range(self.bits - 1):
            pairs = self.step_pairs(self.gather_order, s)
            held = held + [lax.ppermute(h, AXES, pairs) for h in held]
        pairs = self.core_pairs()
        return held + [lax.ppermute(h, AXES, pairs) for h in held]

    def join(self, pieces):
        inverse = np.stack([np.argsort(self.gathered(w)) for w in range(self.wide)]).astype(np.int32)
        stacked = jnp.stack(pieces)
        return jnp.take(stacked, self.mine(inverse), axis=0).reshape(-1, stacked.shape[-1])

    def pieces(self, shard):
        got = self.gather(shard)
        return got if self.exact else [self.join(got)]

    def scatter(self, keep, send):
        half = self.wide // 2
        if not self.exact:
            slots = np.stack([self.slots(w) for w in range(self.wide)]).astype(np.int32)
            whole = jnp.concatenate([keep, send], axis=0)
            whole = whole.reshape(self.wide, -1, whole.shape[-1])
            whole = jnp.take(whole, self.mine(slots), axis=0)
            keep, send = whole[:half], whole[half:]
        total = keep.astype(f32) + lax.ppermute(send, AXES, self.core_pairs()).astype(f32)
        for s in range(self.bits - 1):
            half //= 2
            away = total[half:].astype(bf16)
            total = total[:half] + lax.ppermute(away, AXES, self.step_pairs(self.scatter_order, s)).astype(f32)
        total = total[0]
        size = total.shape[0] // self.narrow
        z = lax.axis_index("narrow")
        own = lax.dynamic_slice_in_dim(total, z * size, size, axis=0)
        low = total.astype(bf16)
        for k in range(1, self.narrow):
            part = lax.dynamic_slice_in_dim(low, (z ^ k) * size, size, axis=0)
            own = own + lax.ppermute(part, AXES, self.narrow_pairs(k)).astype(f32)
        return own

    def total(self, value):
        bit = 1
        while bit < self.narrow:
            value = value + lax.ppermute(value, AXES, self.narrow_pairs(bit))
            bit *= 2
        for s in range(self.bits - 1):
            value = value + lax.ppermute(value, AXES, self.pairs(lambda w, z: (w ^ (2 << s), z)))
        return value + lax.ppermute(value, AXES, self.core_pairs())


def natural_halves(keep, send):
    both = jnp.stack([keep, send], axis=1)
    both = both.reshape(2, -1, both.shape[-1])
    return both[0], both[1]


def conv_rows(conv):
    at = LEAD - RADIUS
    tail = CONV_K - at - KSIZE
    both = jnp.stack([conv, conv[:, ::-1]], axis=1)
    return jnp.pad(both.astype(f32), ((0, 0), (0, 0), (at, tail)))


def body(ring, tokens, cotangent, qkv_w, out_w, in_w, in_b, out2_w, bias_rows, gain_rows, conv_w):
    layers = qkv_w.shape[0]
    size = qkv_w.shape[1]
    order = ring.mine(ring.table())
    columns = jnp.concatenate([bias_rows, gain_rows], axis=1)
    columns = columns.transpose(2, 0, 1).reshape(size, 8 * layers)
    hidden = in_b.reshape(layers, size, -1).transpose(1, 0, 2).reshape(size, -1)
    per = hidden.shape[1] // layers
    small = jnp.concatenate([columns, hidden], axis=1)
    small = jnp.pad(small, ((0, 0), (0, 128 - small.shape[1])))
    attention, feed_in, feed_out = [], [], []
    for layer in range(layers):
        parts = [qkv_w[layer], out_w[layer]] + ([small] if layer == 0 else [])
        attention.append(ring.gather(jnp.concatenate(parts, axis=1)))
        feed_in.append(ring.pieces(in_w[layer]))
        feed_out.append(ring.pieces(out2_w[layer]))
    par = ring.join([piece[:, 4 * D :] for piece in attention[0]]).astype(f32)
    if not ring.exact:
        attention = [[ring.join(pieces)] for pieces in attention]

    x = tokens.T.astype(f32)
    kept = []
    for layer in range(layers):
        conv = conv_rows(conv_w[layer])
        at = 8 * layers + per * layer
        inb = par[:, at : at + per].reshape(FF, 1)
        *saved, xhat1, rstd1 = attention_forward(x, attention[layer], order, par, conv, layer)
        a, g, xhat2, rstd2, x = feed_forward(
            xhat1, feed_in[layer], feed_out[layer], order, order, par, inb, layer, layer == layers - 1)
        kept.append((saved, xhat1, rstd1, a, g, xhat2, rstd2, conv))
    output = x
    dy = cotangent
    results = [None] * layers
    for layer in reversed(range(layers)):
        saved, xhat1, rstd1, a, g, xhat2, rstd2, conv = kept[layer]
        keep2, send2, keep1, send1, inb, dr1, cols = feed_backward(
            dy, xhat2, rstd2, xhat1, rstd1, par, a, g, feed_in[layer], feed_out[layer], order, layer,
            layer == layers - 1)
        if not ring.exact:
            keep2, send2 = natural_halves(keep2, send2)
        grad_out2 = ring.scatter(keep2.reshape(ring.wide // 2, -1, D), send2.reshape(ring.wide // 2, -1, D))
        grad_in = ring.scatter(keep1.reshape(ring.wide // 2, -1, FF), send1.reshape(ring.wide // 2, -1, FF))
        keep, send, dy, cols2, taps = attention_backward(dr1, saved, conv, attention[layer], order, layer == 0)
        grad_att = ring.scatter(keep.reshape(ring.wide // 2, -1, 4 * D), send.reshape(ring.wide // 2, -1, 4 * D))
        at = LEAD - RADIUS
        taps = taps[:, 0, at : at + KSIZE]
        flat = jnp.concatenate(
            [cols2[:, :2].T.reshape(-1), cols[:, 2:].T.reshape(-1), inb.reshape(-1), taps.reshape(-1)])
        flat = jnp.pad(flat, (0, -flat.shape[0] % 1024)).reshape(-1, 128)
        flat = ring.total(flat).reshape(-1)
        rest = flat[8 * D :]
        here = lax.axis_index("wide") * ring.narrow + lax.axis_index("narrow")
        mine = lax.dynamic_slice_in_dim(flat[: 8 * D].reshape(8, D), here * size, size, axis=1)
        results[layer] = (
            grad_att[:, : 3 * D], grad_att[:, 3 * D :], grad_in,
            lax.dynamic_slice_in_dim(rest[:FF], here * in_b.shape[1], in_b.shape[1], axis=0),
            grad_out2, mine[:6], mine[6:], rest[FF : FF + HEADS * KSIZE].reshape(HEADS, KSIZE))
    grads = [jnp.stack([results[layer][i] for layer in range(layers)]) for i in range(8)]
    return (output, dy, *grads)


def solution(mesh):
    ring = Ring(mesh.shape["wide"], mesh.shape["narrow"])
    rows3 = P(None, AXES, None)
    columns3 = P(None, None, AXES)
    weights = (rows3, rows3, rows3, P(None, AXES), rows3, columns3, columns3, P())
    return jax.shard_map(
        functools.partial(body, ring),
        mesh=mesh,
        in_specs=(P(AXES, None), P(AXES, None)) + weights,
        out_specs=(P(AXES, None), P(AXES, None)) + weights,
        check_vma=False,
    )
```

```python
import functools
import jax
import jax.numpy as jnp
import numpy as np
from jax import lax
from jax.experimental import pallas as pl
from jax.experimental.pallas import tpu as pltpu
from jax.sharding import PartitionSpec as P

D = 768
HEADS = 12
HD = 64
FF = 3072
LM = 64
KSIZE = 33
RADIUS = KSIZE // 2
NS_ITERS = 6
T = 1024
SEG = T // LM
SCALE = HD ** -0.5
EPS = 1e-05
CONV_N = 256
CONV_K = 512
CONV_BLOCKS = T // CONV_N
LEAD = 128
f32 = jnp.float32
bf16 = jnp.bfloat16
AXES = ("wide", "narrow")
NN = (((1,), (0,)), ((), ()))
NT = (((1,), (1,)), ((), ()))
TN = (((0,), (0,)), ((), ()))
VMEM_LIMIT = 60 * 1024 * 1024


def dot(a, b, dims):
    return lax.dot_general(a, b, dims, preferred_element_type=f32)


def split(a):
    high = a.astype(bf16)
    return high, (a - high.astype(f32)).astype(bf16)


def dot3(a, b, dims):
    return dot(a[0], b[0], dims) + (dot(a[0], b[1], dims) + dot(a[1], b[0], dims))


def rows(start, size):
    if isinstance(start, int):
        return pl.ds(start, size)
    return pl.ds(pl.multiple_of(start, size), size)


def segment_mean():
    token = lax.broadcasted_iota(jnp.int32, (T, LM), 0)
    seg = lax.broadcasted_iota(jnp.int32, (T, LM), 1)
    return jnp.where(token // SEG == seg, 1.0 / SEG, 0.0).astype(bf16)


def segment_spread():
    token = lax.broadcasted_iota(jnp.int32, (LM, T), 1)
    seg = lax.broadcasted_iota(jnp.int32, (LM, T), 0)
    return jnp.where(token // SEG == seg, 1.0, 0.0).astype(bf16)


def eye(value):
    i = lax.broadcasted_iota(jnp.int32, (LM, LM), 0)
    j = lax.broadcasted_iota(jnp.int32, (LM, LM), 1)
    return jnp.where(i == j, value, 0.0).astype(f32)


def toeplitz(row):
    full = jnp.broadcast_to(row, (CONV_N, CONV_K))
    return pltpu.roll(full, 0, 1, stride=1, stride_axis=0).astype(bf16)


def windows(ref, base):
    return jnp.concatenate(
        [ref[rows(base, HD), CONV_N * b : CONV_N * b + CONV_K] for b in range(CONV_BLOCKS)], axis=0
    )


def stack_blocks(value):
    return jnp.concatenate(
        [value[:, CONV_N * b : CONV_N * (b + 1)] for b in range(CONV_BLOCKS)], axis=0
    )


def unstack_blocks(value):
    return jnp.concatenate(
        [value[HD * b : HD * (b + 1), :] for b in range(CONV_BLOCKS)], axis=1
    )


def norm_forward(r_ref, xhat_ref, rstd_ref, width=128):
    for c in range(0, T, width):
        r = r_ref[:, c : c + width]
        center = r - jnp.mean(r, axis=0, keepdims=True)
        rstd = lax.rsqrt(jnp.mean(center * center, axis=0, keepdims=True) + EPS)
        xhat_ref[:, c : c + width] = center * rstd
        rstd_ref[:, c : c + width] = jnp.broadcast_to(rstd, (8, width))


def vm():
    return pl.BlockSpec(memory_space=pltpu.VMEM)


def anywhere(n):
    return [pl.BlockSpec(memory_space=pl.ANY)] * n


def whole(*s):
    return pl.BlockSpec(s, lambda *_: (0,) * len(s))


def sd(*s, t=f32):
    return jax.ShapeDtypeStruct(s, t)


def loader(pieces, dst, sem, columns=None):
    r = pieces[0].shape[0]
    order = Order(len(pieces))
    out = []
    for i, piece in enumerate(pieces):
        src = piece if columns is None else piece.at[:, pl.ds(*columns)]
        at = rows(order.target(i) * r, r)
        out.append(pltpu.make_async_copy(src, dst.at[at, :], sem.at[i]))
    return out


def call(kernel, name, out_shape, in_specs, out_specs, scratch, args, lanes, flops, size, grid=None, trans=0):
    identity, lanes = lanes
    ins, outs = len(args), len(out_shape)
    lane_args = [a for lane in lanes for a in lane.args]
    lane_outs = [o for lane in lanes for o in lane.outs]
    lane_scratch = [o for lane in lanes for o in lane.scratch]

    def run(*refs):
        refs = list(refs)

        def take(n):
            got = refs[:n]
            del refs[:n]
            return got

        own = take(ins)
        lane_in = [take(len(lane.args)) for lane in lanes]
        own += take(outs)
        lane_out = [take(len(lane.outs)) for lane in lanes]
        own += take(len(scratch))
        for lane, a, o in zip(lanes, lane_in, lane_out):
            lane.bind(a, o, take(len(lane.scratch)))

        def hook(i):
            if lanes and i == 0:
                near = Near()
                names = sorted({p for lane in lanes for p in lane.partners})
                barrier = pltpu.get_barrier_semaphore()
                for p in names:
                    pl.semaphore_signal(barrier, inc=1, device_id=near.at(p), device_id_type=pl.DeviceIdType.MESH)
                pl.semaphore_wait(barrier, len(names))
            for lane in lanes:
                lane.turn(i)

        kernel(*own, hook=hook)

    params = {"collective_id": identity, "has_side_effects": True} if lanes else {}
    got = pl.pallas_call(
        run,
        out_shape=list(out_shape) + [o for o, _ in lane_outs],
        in_specs=list(in_specs) + [spec for lane in lanes for spec in lane.specs],
        out_specs=list(out_specs) + [spec for _, spec in lane_outs],
        scratch_shapes=list(scratch) + lane_scratch,
        **({} if grid is None else {"grid": grid}),
        compiler_params=pltpu.CompilerParams(vmem_limit_bytes=VMEM_LIMIT, **params),
        cost_estimate=pl.CostEstimate(flops=flops, bytes_accessed=size, transcendentals=trans),
        name=name,
    )(*args, *lane_args)
    own, rest = list(got[:outs]), list(got[outs:])
    for lane in lanes:
        n = len(lane.outs)
        lane.done(rest[:n])
        rest = rest[n:]
    return own


class Near:
    def __init__(self):
        self.w, self.z = lax.axis_index("wide"), lax.axis_index("narrow")

    def over(self, k):
        z = self.z
        if k == 1:
            return z + 1 - 2 * (z % 2)
        if k == 2:
            return z + 2 - 4 * (z // 2)
        return 3 - z

    def at(self, name):
        w, core = self.w, self.w % 2
        if name[0] == "z":
            return (w, self.over(int(name[1])))
        if name == "core":
            return (w + 1 - 2 * core, self.z)
        step = {"a": 2 + 2 * core, "b": 4 - 2 * core, "x": 2, "y": 4}[name]
        return (w + step - 2 * step * ((w // step) % 2), self.z)


def remote(src, dst, send, recv, name):
    return pltpu.make_async_remote_copy(
        src_ref=src, dst_ref=dst, send_sem=send, recv_sem=recv, device_id=Near().at(name),
        device_id_type=pl.DeviceIdType.MESH)


DMA = pltpu.SemaphoreType.DMA
ANY = pl.BlockSpec(memory_space=pl.ANY)


class Move:
    def __init__(self, source, name, start, wait):
        self.chained = isinstance(source, Move)
        self.source, self.name, self.start, self.wait = source, name, start, wait
        self.shape = source.shape
        self.args = [] if self.chained else [source]
        self.specs = [ANY] * len(self.args)
        self.outs = [(sd(*self.shape, t=bf16), ANY)]
        self.scratch = [DMA((2,))]
        self.partners = [name]

    def bind(self, args, outs, scratch):
        self.src = self.source.dst if self.chained else args[0]
        self.dst, self.sem = outs[0], scratch[0]

    def copy(self):
        return remote(self.src, self.dst, self.sem.at[0], self.sem.at[1], self.name)

    def turn(self, i):
        if i == self.wait:
            self.copy().wait()
        if i == self.start:
            self.copy().start()

    def done(self, got):
        self.value = got[0]


class Spread:
    def __init__(self, shard, start, wait):
        self.start, self.wait = start, wait
        self.args, self.specs = [shard], [ANY]
        self.outs = [(sd(4, *shard.shape, t=bf16), ANY)]
        self.scratch = [DMA((7,))]
        self.partners = ["z1", "z2", "z3"]

    def bind(self, args, outs, scratch):
        self.src, self.dst, self.sem = args[0], outs[0], scratch[0]

    def copies(self):
        z = lax.axis_index("narrow")
        out = [pltpu.make_async_copy(self.src, self.dst.at[z], self.sem.at[6])]
        for k in (1, 2, 3):
            out.append(remote(self.src, self.dst.at[z], self.sem.at[2 * k - 2], self.sem.at[2 * k - 1], f"z{k}"))
        return out

    def turn(self, i):
        if i == self.wait:
            for copy in self.copies():
                copy.wait()
        if i == self.start:
            for copy in self.copies():
                copy.start()

    def done(self, got):
        value = got[0]
        self.value = value.reshape(-1, value.shape[-1])


def strips(columns):
    width = 384 if columns % 384 == 0 else columns
    return [slice(c, c + width) for c in range(0, columns, width)]


class ReduceFirst:
    def __init__(self, keep, send, turns, chained=False, columns=None):
        self.turns, self.chained, self.at = turns, chained, columns
        rows4 = D // 2 if columns is not None else send.shape[0]
        self.columns = columns.stop - columns.start if columns is not None else send.shape[1]
        self.r = r = rows4 // 4
        self.partners = ["core", "b"]
        shape = (r, self.columns)
        self.args = [] if columns is not None else [keep, send]
        self.specs = [ANY] * len(self.args)
        self.outs = [] if chained else [(sd(*shape, t=bf16), whole(*shape)), (sd(*shape), whole(*shape))]
        self.scratch = [pltpu.VMEM((2 * r, self.columns), bf16), pltpu.VMEM((2 * r, self.columns), bf16),
                        pltpu.VMEM((4 * r, self.columns), bf16), DMA((5,))]
        if chained:
            self.scratch += [pltpu.VMEM(shape, bf16), pltpu.VMEM(shape, f32)]
        if columns is None:
            self.scratch += [pltpu.VMEM((4 * r, self.columns), bf16)]

    def bind(self, args, outs, scratch):
        self.away1, self.got1, self.got0, self.sem = scratch[:4]
        rest = scratch[4:]
        if self.chained:
            self.away2, self.own2 = rest[:2]
            rest = rest[2:]
        else:
            self.away2, self.own2 = outs
        if self.at is None:
            self.keep_from, self.send = args
            self.keep = rest[0]

    def use(self, keep, send):
        self.keep, self.send = keep.at[:, self.at], send.at[:, self.at]

    def load(self):
        return pltpu.make_async_copy(self.keep_from, self.keep, self.sem.at[4])

    def first(self):
        return remote(self.send, self.got0, self.sem.at[0], self.sem.at[1], "core")

    def second(self):
        return remote(self.away1, self.got1, self.sem.at[2], self.sem.at[3], "b")

    def turn(self, i):
        r = self.r
        if i == self.turns[0]:
            self.first().start()
            if self.at is None:
                self.load().start()
        if i == self.turns[1]:
            if self.at is None:
                self.load().wait()
            self.first().wait()
            for at in strips(self.columns):
                self.away1[:, at] = self.keep[2 * r :, at] + self.got0[2 * r :, at]
            self.second().start()
        if i == self.turns[2]:
            self.second().wait()
            for at in strips(self.columns):
                for k, out in ((0, self.own2), (1, self.away2)):
                    block = slice(k * r, (k + 1) * r)
                    value = self.keep[block, at].astype(f32) + self.got0[block, at].astype(f32)
                    out[:, at] = (value + self.got1[block, at].astype(f32)).astype(out.dtype)

    def done(self, got):
        self.value = got


class ReduceLast:
    def __init__(self, away, own, turns, inside=None):
        self.turns, self.inside = turns, inside
        r, columns = (inside.r, inside.columns) if inside else away.shape
        size = r // 4
        self.r, self.columns, self.size = r, columns, size
        self.partners = ["a", "z1", "z2", "z3"]
        self.args = [] if inside else [away, own]
        self.specs = [] if inside else [ANY, whole(r, columns)]
        self.outs = [(sd(size, columns), whole(size, columns))]
        self.scratch = [pltpu.VMEM((r, columns), bf16), pltpu.VMEM((4, size, columns), bf16),
                        pltpu.VMEM((4, size, columns), bf16), pltpu.VMEM((4, size, columns), f32), DMA((8,))]

    def bind(self, args, outs, scratch):
        self.got2, self.parts, self.got3, self.sums, self.sem = scratch
        self.out = outs[0]
        self.away, self.own = (self.inside.away2, self.inside.own2) if self.inside else args

    def third(self):
        return remote(self.away, self.got2, self.sem.at[0], self.sem.at[1], "a")

    def last(self):
        near = Near()
        return [
            remote(self.parts.at[near.over(k)], self.got3.at[near.z], self.sem.at[2 * k], self.sem.at[2 * k + 1], f"z{k}")
            for k in (1, 2, 3)]

    def turn(self, i):
        if i == self.turns[0]:
            self.third().start()
        if i == self.turns[1]:
            self.third().wait()
            for at in strips(self.columns):
                for k in range(4):
                    block = slice(k * self.size, (k + 1) * self.size)
                    self.sums[k, :, at] = self.own[block, at]
                whole_block = self.got2[:, at].astype(f32)
                for k in range(4):
                    value = self.sums[k, :, at] + whole_block[k * self.size : (k + 1) * self.size]
                    self.sums[k, :, at] = value
                    self.parts[k, :, at] = value.astype(bf16)
            for copy in self.last():
                copy.start()
        if i == self.turns[2]:
            for copy in self.last():
                copy.wait()
            near = Near()
            for at in strips(self.columns):
                value = self.sums[near.z, :, at]
                for k in (1, 2, 3):
                    value = value + self.got3[near.over(k), :, at].astype(f32)
                self.out[:, at] = value

    def done(self, got):
        self.value = got[0]


SMALL = 24


class Total:
    def __init__(self, sums, taps, turns):
        self.turns = turns
        self.args = [sums, *taps]
        self.specs = [whole(*a.shape) for a in self.args]
        shape = (SMALL, D + 128)
        self.outs = [(sd(*shape), whole(*shape))]
        self.scratch = [pltpu.VMEM((5, *shape), f32), pltpu.VMEM((5, *shape), f32), DMA((10,))]
        self.partners = ["core", "x", "y", "z1", "z2"]

    def bind(self, args, outs, scratch):
        self.small, self.out = args, outs[0]
        self.held, self.got, self.sem = scratch

    def copy(self, s):
        return remote(self.held.at[s], self.got.at[s], self.sem.at[2 * s], self.sem.at[2 * s + 1], self.partners[s])

    def turn(self, i):
        for s in range(6):
            if i == self.turns[s]:
                if s:
                    self.copy(s - 1).wait()
                    value = self.held[s - 1] + self.got[s - 1]
                    if s < 5:
                        self.held[s] = value
                    else:
                        self.out[...] = value
                else:
                    self.held[0, :, 0:D] = self.small[0][...].T[0:SMALL, :]
                    self.held[0, 0:HEADS, D:] = self.small[1][...]
                    self.held[0, HEADS : 2 * HEADS, D:] = self.small[2][...]
                if s < 5:
                    self.copy(s).start()

    def done(self, got):
        self.value = got[0]


CHUNK = 768
STEPS = FF // CHUNK
SUB = 256


def flip(t, stride):
    return t + stride - 2 * stride * ((t // stride) % 2)


class Order:
    def __init__(self, n):
        self.exact = n == 8
        self.core = 0
        if self.exact:
            self.w = lax.axis_index("wide")
            self.core = self.w % 2

    def target(self, i):
        if not self.exact:
            return i
        other, code = i // 4, i % 4
        t = self.w + other * (1 - 2 * self.core)
        core = t % 2
        if code % 2:
            t = flip(t, 2 + 2 * core)
        if code // 2:
            t = flip(t, 4 - 2 * core)
        return t

    def slot(self, j, other):
        if not self.exact:
            return j
        plane = self.w // 2
        core = self.core if other == 0 else 1 - self.core
        dx, dy = (j + plane) % 2, (j // 2 + plane // 2) % 2
        return dx * (1 + core) + dy * (2 - core)


def exchange(lanes, turns):
    def kernel(hook):
        for i in range(turns):
            hook(i)

    call(kernel, "exchange", [], [], [], [], (), lanes, 0, 10_000_000)


def project_kernel(n, p, x_ref, *rest, hook):
    if p:
        par_ref, *rest = rest
    pieces, rest = rest[:n], rest[n:]
    if p:
        xl_ref, mix_ref, lm_ref, w_ref, sem = rest
        loads = []
    else:
        xl_ref, mix_ref, lm_ref, par_ref, w_ref, sem, low_ref, low_sem = rest
        loads = loader(pieces, low_ref, low_sem, (4 * D, 128))
    loads += loader(pieces, w_ref, sem, (0, 3 * D))
    for copy in loads:
        copy.start()
    xl_ref[...] = x_ref[...].astype(bf16)
    hook(0)
    for copy in loads:
        copy.wait()
    if not p:
        par_ref[...] = low_ref[...].astype(f32)
    for part, column in ((0, p), (1, None), (2, p + 1)):

        def mix_step(i, _):
            at = rows(part * D + i * 256, 256)
            got = dot(w_ref[:, at], xl_ref[...], TN)
            if column is not None:
                got = got + par_ref[rows(i * 256, 256), column : column + 1]
            mix_ref[at, :] = got.astype(bf16)
            return 0

        lax.fori_loop(0, 3, mix_step, 0)
        hook(part + 1)
    lm_ref[...] = dot(mix_ref[0 : 2 * D, :], segment_mean(), NN).astype(bf16)
    hook(4)


def project(x, pieces, par, layer, lanes=(None, ())):
    n = len(pieces)
    first = layer == 0
    got = call(
        functools.partial(project_kernel, n, 8 * layer), "project",
        [sd(D, T, t=bf16), sd(3 * D, T, t=bf16), sd(2 * D, LM, t=bf16)] + [sd(D, 128)] * first,
        [vm()] + [vm()] * (not first) + anywhere(n), [vm()] * (3 + first),
        [pltpu.VMEM((D, 3 * D), bf16), DMA((n,))] + [pltpu.VMEM((D, 128), bf16), DMA((n,))] * first,
        (x, *([] if first else [par]), *pieces), lanes, 3_800_000_000, 14_000_000)
    return got if first else [*got, par]


def attend_kernel(n, p, x_ref, mix_ref, lm_ref, par_ref, conv_ref, *rest, hook):
    pieces = rest[:n]
    (ctx_ref, f_ref, b_ref, a_ref, ns_ref, small_ref, xhat_ref, rstd_ref,
     w_ref, vpad_ref, z_ref, sem) = rest[n:]
    loads = loader(pieces, w_ref, sem, (3 * D, D))
    for copy in loads:
        copy.start()
    vpad_ref[:, 0:LEAD] = jnp.zeros((D, LEAD), bf16)
    vpad_ref[:, LEAD + T :] = jnp.zeros((D, LEAD), bf16)
    vpad_ref[:, LEAD : LEAD + T] = mix_ref[2 * D :, :]
    hook(0)
    for h in range(HEADS):
        ql = lm_ref[h * HD : (h + 1) * HD, :]
        kl = lm_ref[D + h * HD : D + (h + 1) * HD, :]
        s = dot(ql, kl, TN) * SCALE
        e = jnp.exp(s - jnp.max(s, axis=1, keepdims=True))
        a = e / jnp.sum(e, axis=1, keepdims=True)
        a_ref[h] = a
        z_ref[h] = a.T / jnp.sum(a * a)

    def ns_step(k, _):
        ps, rs = [], []
        for h in range(HEADS):
            z = z_ref[h]
            ns_ref[k, 0, h] = z
            p = dot3(split(a_ref[h]), split(z), NN)
            ns_ref[k, 1, h] = p
            ps.append(split(p))
            rs.append(split(eye(7.0) - p))
        for h in range(HEADS):
            r2 = eye(15.0) - dot3(ps[h], rs[h], NN)
            ns_ref[k, 2, h] = r2
            rs[h] = split(r2)
        for h in range(HEADS):
            r3 = eye(13.0) - dot3(ps[h], rs[h], NN)
            ns_ref[k, 3, h] = r3
            rs[h] = split(r3)
        for h in range(HEADS):
            z_ref[h] = 0.25 * dot3(split(z_ref[h]), rs[h], NN)
        return 0

    lax.fori_loop(0, NS_ITERS, ns_step, 0)
    hook(1)

    def head_step(h, _):
        base = h * HD
        q = mix_ref[rows(base, HD), :]
        k = mix_ref[rows(D + base, HD), :]
        v = mix_ref[rows(2 * D + base, HD), :]
        ql = lm_ref[rows(base, HD), :]
        kl = lm_ref[rows(D + base, HD), :]
        s = dot(kl, q, TN) * SCALE
        e = jnp.exp(s - jnp.max(s, axis=0, keepdims=True))
        f = (e / jnp.sum(e, axis=0, keepdims=True)).astype(bf16)
        f_ref[rows(base, HD), :] = f
        s = dot(ql, k, TN) * SCALE
        e = jnp.exp(s - jnp.max(s, axis=1, keepdims=True))
        b = (e / jnp.sum(e, axis=1, keepdims=True)).astype(bf16)
        b_ref[rows(base, HD), :] = b
        bv = dot(b, v, NT)
        z = z_ref[h]
        w = dot3(split(z), split(bv), NN)
        small_ref[0, h] = z
        small_ref[1, h] = bv
        small_ref[2, h] = w
        attended = dot(w.astype(bf16), f, TN)
        conv = dot(windows(vpad_ref, base), toeplitz(conv_ref[h, 0:1]), NT)
        ctx_ref[rows(base, HD), :] = (attended + unstack_blocks(conv)).astype(bf16)
        return 0

    lax.fori_loop(0, HEADS // 2, head_step, 0)
    hook(2)
    lax.fori_loop(HEADS // 2, HEADS, head_step, 0)
    hook(3)
    for copy in loads:
        copy.wait()

    def out_step(i, _):
        base = i * 256
        got = dot(w_ref[:, rows(base, 256)], ctx_ref[...], TN)
        xhat_ref[rows(base, 256), :] = got + par_ref[rows(base, 256), p + 2 : p + 3] + x_ref[rows(base, 256), :]
        return 0

    lax.fori_loop(0, 3, out_step, 0)
    norm_forward(xhat_ref, xhat_ref, rstd_ref)
    hook(4)


def attend(x, mix, lm, pieces, par, conv, layer, lanes=(None, ())):
    n = len(pieces)
    return call(
        functools.partial(attend_kernel, n, 8 * layer), "attend",
        [
            sd(D, T, t=bf16), sd(D, T, t=bf16), sd(D, T, t=bf16), sd(HEADS, LM, LM),
            sd(NS_ITERS, 4, HEADS, LM, LM), sd(3, HEADS, LM, LM), sd(D, T), sd(8, T),
        ],
        [vm()] * 5 + anywhere(n), [vm()] * 8,
        [
            pltpu.VMEM((D, D), bf16), pltpu.VMEM((D, T + 2 * LEAD), bf16), pltpu.VMEM((HEADS, LM, LM), f32),
            pltpu.SemaphoreType.DMA((n,)),
        ],
        (x, mix, lm, par, conv, *pieces), lanes, 3_000_000_000, 30_000_000, trans=2_000_000)


def up_kernel(n, p, xhat_ref, par_ref, inb_ref, *rest, hook):
    pieces, (a_ref, g_ref, w_ref, hl_ref, sem) = rest[:n], rest[n:]
    j = pl.program_id(0)

    @pl.when(j == 0)
    def _():
        loads = loader(pieces, w_ref, sem)
        for copy in loads:
            copy.start()
        hook(0)
        h = xhat_ref[...] * par_ref[:, p + 6 : p + 7] + par_ref[:, p + 3 : p + 4]
        hl_ref[...] = h.astype(bf16)
        for copy in loads:
            copy.wait()

    def up_step(i, _):
        base = i * SUB
        at = j * CHUNK + base
        u = dot(w_ref[:, pl.ds(pl.multiple_of(at, SUB), SUB)], hl_ref[...], TN)
        u = u + inb_ref[rows(at, SUB), 0:1]
        cdf = 0.5 + 0.5 * lax.erf(u * (2.0 ** -0.5))
        pdf = jnp.exp(-0.5 * u * u) * ((2.0 * np.pi) ** -0.5)
        a_ref[rows(base, SUB), :] = (u * cdf).astype(bf16)
        g_ref[rows(base, SUB), :] = (cdf + u * pdf).astype(bf16)
        return 0

    lax.fori_loop(0, CHUNK // SUB, up_step, 0)
    for i in range(STEPS):

        @pl.when(j == i)
        def _():
            hook(i + 1)


def up(xhat, pieces, par, inb, layer, lanes=(None, ())):
    n = len(pieces)
    chunk = pl.BlockSpec((CHUNK, T), lambda j: (j, 0))
    return call(
        functools.partial(up_kernel, n, 8 * layer), "up",
        [sd(FF, T, t=bf16), sd(FF, T, t=bf16)],
        [whole(D, T), whole(D, 128), whole(FF, 1)] + anywhere(n), [chunk, chunk],
        [pltpu.VMEM((D, FF), bf16), pltpu.VMEM((D, T), bf16), pltpu.SemaphoreType.DMA((n,))],
        (xhat, par, inb, *pieces), lanes, 4_900_000_000, 24_000_000, (STEPS,), 6_000_000)


def down_kernel(n, p, last, xhat_ref, par_ref, a_ref, *rest, hook):
    pieces, (xhat2_ref, rstd2_ref, next_ref, w_ref, sem) = rest[:n], rest[n:]
    j = pl.program_id(0)

    @pl.when(j == 0)
    def _():
        loads = loader(pieces, w_ref, sem)
        for copy in loads:
            copy.start()
        hook(0)
        h = xhat_ref[...] * par_ref[:, p + 6 : p + 7] + par_ref[:, p + 3 : p + 4]
        xhat2_ref[...] = h + par_ref[:, p + 4 : p + 5]
        for copy in loads:
            copy.wait()

    def down_step(i, _):
        base = i * SUB
        xhat2_ref[rows(base, SUB), :] += dot(
            w_ref[rows(j * CHUNK, CHUNK), pl.ds(pl.multiple_of(base, SUB), SUB)], a_ref[...], TN)
        return 0

    lax.fori_loop(0, D // SUB, down_step, 0)

    @pl.when(j == STEPS - 1)
    def _():
        norm_forward(xhat2_ref, xhat2_ref, rstd2_ref)
        y = xhat2_ref[...] * par_ref[:, p + 7 : p + 8] + par_ref[:, p + 5 : p + 6]
        if last:
            next_ref[...] = y.T.astype(bf16)
        else:
            next_ref[...] = y
    for i in range(STEPS):

        @pl.when(j == i)
        def _():
            hook(i + 1)


def down(xhat, a, pieces, par, layer, last, lanes=(None, ())):
    n = len(pieces)
    next_shape = (T, D) if last else (D, T)
    return call(
        functools.partial(down_kernel, n, 8 * layer, last), "down",
        [sd(D, T), sd(8, T), sd(*next_shape, t=bf16 if last else f32)],
        [whole(D, T), whole(D, 128), pl.BlockSpec((CHUNK, T), lambda j: (j, 0))] + anywhere(n),
        [whole(D, T), whole(8, T), whole(*next_shape)],
        [pltpu.VMEM((FF, D), bf16), pltpu.SemaphoreType.DMA((n,))],
        (xhat, par, a, *pieces), lanes, 4_900_000_000, 24_000_000, (STEPS,))


def norm_backward(dy_ref, xhat_ref, rstd_ref, gain, out_ref, grads_ref, gain_col, shift_col, width=128):
    total_gain = jnp.zeros((D, width), f32)
    total_shift = jnp.zeros((D, width), f32)
    for c in range(0, T, width):
        dy = dy_ref[:, c : c + width]
        xhat = xhat_ref[:, c : c + width]
        total_shift = total_shift + dy
        total_gain = total_gain + dy * xhat
        dxhat = dy * gain
        m1 = jnp.mean(dxhat, axis=0, keepdims=True)
        m2 = jnp.mean(dxhat * xhat, axis=0, keepdims=True)
        out_ref[:, c : c + width] = rstd_ref[0:1, c : c + width] * (dxhat - m1 - xhat * m2)
    grads_ref[:, gain_col : gain_col + 1] = jnp.sum(total_gain, axis=1, keepdims=True)
    grads_ref[:, shift_col : shift_col + 1] = jnp.sum(total_shift, axis=1, keepdims=True)


def lane_sum(value):
    return jnp.sum(value.astype(f32), axis=1, keepdims=True)


def permute_rows(dst_ref, src_ref, order, block):
    for i in range(D // block):
        dst_ref[i * block : (i + 1) * block, :] = src_ref[
            rows(order.target(i) * block, block), :]


def hidden_kernel(n, p, first, sums_in, dy_ref, xhat_ref, rstd_ref, par_ref, a_ref, g_ref, *rest, hook):
    order = Order(n)
    pieces, (keep_ref, send_ref, du_ref, dr_ref, cols_ref, w_ref, dz_ref, inb_ref, sem) = rest[:n], rest[n:]
    j = pl.program_id(0)

    @pl.when(j == 0)
    def _():
        loads = loader(pieces, w_ref, sem)
        for copy in loads:
            copy.start()
        hook(0)
        if first:
            dr_ref[...] = dy_ref[...].astype(f32).T
            dy = dr_ref
        else:
            dy = dy_ref
        cols_ref[...] = sums_in[...]
        norm_backward(dy, xhat_ref, rstd_ref, par_ref[:, p + 7 : p + 8], dr_ref, cols_ref, p + 7, p + 5)
        dz_ref[...] = dr_ref[...].astype(bf16)
        cols_ref[:, p + 4 : p + 5] = lane_sum(dz_ref[...])
        for copy in loads:
            copy.wait()

    def du_step(i, _):
        base = i * SUB
        da = dot(w_ref[rows(j * CHUNK + base, SUB), :], dz_ref[...], NN)
        du = (da * g_ref[rows(base, SUB), :].astype(f32)).astype(bf16)
        du_ref[rows(base, SUB), :] = du
        inb_ref[rows(base, SUB), :] = lane_sum(du)
        return 0

    lax.fori_loop(0, CHUNK // SUB, du_step, 0)
    half = CHUNK // 2
    core = order.core

    def own(start):
        return a_ref[rows(start, half), :]

    keep_ref[order.slot(j, 0)] = dot(own(core * half), dz_ref[...], NT).astype(bf16)
    send_ref[order.slot(j, 1)] = dot(own((1 - core) * half), dz_ref[...], NT).astype(bf16)
    for i in range(STEPS):

        @pl.when(j == i)
        def _():
            column = 2 * 8 + p // 2 + i
            cols_ref[:, column : column + 1] = inb_ref[...]
            hook(i + 1)


def hidden(sums, dy, xhat, rstd, par, a, g, pieces, layer, first, lanes=(None, ())):
    n = len(pieces)
    chunk = pl.BlockSpec((CHUNK, T), lambda j: (j, 0))
    half = CHUNK // 2
    return call(
        functools.partial(hidden_kernel, n, 8 * layer, first), "hidden",
        [
            sd(STEPS, half, D, t=bf16), sd(STEPS, half, D, t=bf16), sd(FF, T, t=bf16), sd(D, T), sd(D, 128),
        ],
        [whole(D, 128), whole(*dy.shape), whole(D, T), whole(8, T), whole(D, 128), chunk, chunk] + anywhere(n),
        [
            whole(STEPS, half, D), whole(STEPS, half, D), chunk, whole(D, T), whole(D, 128),
        ],
        [pltpu.VMEM((FF, D), bf16), pltpu.VMEM((D, T), bf16), pltpu.VMEM((CHUNK, 1), f32), pltpu.SemaphoreType.DMA((n,))],
        (sums, dy, xhat, rstd, par, a, g, *pieces), lanes, 9_700_000_000, 40_000_000, (STEPS,))


def inner_kernel(n, p, sums_in, du_ref, dr_ref, xhat_ref, rstd_ref, par_ref, *rest, hook):
    order = Order(n)
    pieces, (keep_ref, send_ref, out_ref, cols_ref, w_ref, hl_ref, acc_ref, sem) = rest[:n], rest[n:]
    j = pl.program_id(0)

    @pl.when(j == 0)
    def _():
        loads = loader(pieces, w_ref, sem)
        for copy in loads:
            copy.start()
        hook(0)
        block = D // 8
        for i in range(8):
            at = rows(order.target(i) * block, block)
            hl_ref[i * block : (i + 1) * block, :] = (
                xhat_ref[at, :] * par_ref[at, p + 6 : p + 7] + par_ref[at, p + 3 : p + 4]).astype(bf16)
        acc_ref[...] = dr_ref[...]
        for copy in loads:
            copy.wait()

    for i, ref in enumerate((keep_ref, send_ref)):
        ref[...] = dot(hl_ref[i * (D // 2) : (i + 1) * (D // 2), :], du_ref[...], NT).astype(bf16)

    def dh_step(i, _):
        acc_ref[rows(i * SUB, SUB), :] += dot(
            w_ref[rows(i * SUB, SUB), rows(j * CHUNK, CHUNK)], du_ref[...], NN)
        return 0

    lax.fori_loop(0, D // SUB, dh_step, 0)

    @pl.when(j == STEPS - 1)
    def _():
        cols_ref[...] = sums_in[...]
        norm_backward(acc_ref, xhat_ref, rstd_ref, par_ref[:, p + 6 : p + 7], out_ref, cols_ref, p + 6, p + 3)
        cols_ref[:, p + 2 : p + 3] = lane_sum(out_ref[...].astype(bf16))
    for i in range(STEPS):

        @pl.when(j == i)
        def _():
            hook(i + 1)


def inner(sums, du, dr, xhat, rstd, par, pieces, layer, lanes=(None, ())):
    n = len(pieces)
    return call(
        functools.partial(inner_kernel, n, 8 * layer), "inner",
        [sd(D // 2, FF, t=bf16), sd(D // 2, FF, t=bf16), sd(D, T), sd(D, 128)],
        [whole(D, 128), pl.BlockSpec((CHUNK, T), lambda j: (j, 0)), whole(D, T), whole(D, T), whole(8, T), whole(D, 128)]
        + anywhere(n),
        [
            pl.BlockSpec((D // 2, CHUNK), lambda j: (0, j)), pl.BlockSpec((D // 2, CHUNK), lambda j: (0, j)),
            whole(D, T), whole(D, 128),
        ],
        [pltpu.VMEM((D, FF), bf16), pltpu.VMEM((D, T), bf16), pltpu.VMEM((D, T), f32), pltpu.SemaphoreType.DMA((n,))],
        (sums, du, dr, xhat, rstd, par, *pieces), lanes, 9_700_000_000, 35_000_000, (STEPS,))


def values_kernel(n, p, sums_in, dr1_ref, v_ref, ctx_ref, f_ref, b_ref, small_ref, conv_ref, *rest, hook):
    order = Order(n)
    pieces = rest[:n]
    (keep_ref, send_ref, dctx_ref, dv_ref, dz_ref, dbv_ref, taps_ref, cols_ref,
     w_ref, dp_ref, perm_ref, vpad_ref, dpad_ref, sem) = rest[n:]
    loads = loader(pieces, w_ref, sem, (3 * D, D))
    for copy in loads:
        copy.start()
    for ref in (vpad_ref, dpad_ref):
        ref[:, 0:LEAD] = jnp.zeros((D, LEAD), bf16)
        ref[:, LEAD + T :] = jnp.zeros((D, LEAD), bf16)
    vpad_ref[:, LEAD : LEAD + T] = v_ref[...]
    dp_ref[...] = dr1_ref[...].astype(bf16)
    permute_rows(perm_ref, ctx_ref, order, D // 8)
    hook(0)
    for i, ref in enumerate((keep_ref, send_ref)):
        ref[...] = dot(perm_ref[i * (D // 2) : (i + 1) * (D // 2), :], dp_ref[...], NT).astype(bf16)
    for copy in loads:
        copy.wait()

    def dctx_step(i, _):
        got = dot(w_ref[rows(i * SUB, SUB), :], dp_ref[...], NN).astype(bf16)
        dctx_ref[rows(i * SUB, SUB), :] = got
        dpad_ref[rows(i * SUB, SUB), LEAD : LEAD + T] = got
        return 0

    lax.fori_loop(0, D // SUB, dctx_step, 0)
    hook(1)
    flip = jnp.where(
        lax.broadcasted_iota(jnp.int32, (CONV_N, CONV_N), 0)
        + lax.broadcasted_iota(jnp.int32, (CONV_N, CONV_N), 1) == CONV_N - 1, 1.0, 0.0).astype(bf16)

    def value_step(h, _):
        base = h * HD
        dctx = dctx_ref[rows(base, HD), :]
        f = f_ref[rows(base, HD), :]
        dw = split(dot(f, dctx, NT))
        dz_ref[h] = dot3(dw, split(small_ref[1, h]), NT)
        dbv = dot3(split(small_ref[0, h]), dw, TN).astype(bf16)
        dbv_ref[h] = dbv
        dv = dot(dbv, b_ref[rows(base, HD), :], TN)
        conv = dot(windows(dpad_ref, base), toeplitz(conv_ref[h, 1:2]), NT)
        dv_ref[rows(base, HD), :] = (dv + unstack_blocks(conv)).astype(bf16)
        flipped = dot(stack_blocks(dctx), flip, NN).astype(bf16)
        g = dot(flipped, windows(vpad_ref, base), TN)
        g = pltpu.roll(g, CONV_K - CONV_N + 1 - (LEAD - RADIUS), 1, stride=1, stride_axis=0)
        taps_ref[pl.ds(h, 1), :] = jnp.sum(g[:, 0:128], axis=0, keepdims=True)
        return 0

    lax.fori_loop(0, HEADS // 2, value_step, 0)
    hook(2)
    lax.fori_loop(HEADS // 2, HEADS, value_step, 0)
    cols_ref[...] = sums_in[...]
    cols_ref[:, p + 1 : p + 2] = lane_sum(dv_ref[...])
    hook(3)
    hook(4)


def values(sums, dr1, mix, ctx, f, b, small, conv, pieces, layer, lanes=(None, ())):
    n = len(pieces)
    return call(
        functools.partial(values_kernel, n, 8 * layer), "values",
        [
            sd(D // 2, D, t=bf16), sd(D // 2, D, t=bf16), sd(D, T, t=bf16), sd(D, T, t=bf16),
            sd(HEADS, LM, LM), sd(HEADS, LM, LM, t=bf16), sd(HEADS, 128), sd(D, 128),
        ],
        [whole(D, 128), whole(D, T), pl.BlockSpec((D, T), lambda *_: (2, 0)), whole(D, T), whole(D, T), whole(D, T),
         whole(*small.shape), whole(*conv.shape)] + anywhere(n),
        [whole(D // 2, D), whole(D // 2, D), whole(D, T), whole(D, T), whole(HEADS, LM, LM), whole(HEADS, LM, LM),
         whole(HEADS, 128), whole(D, 128)],
        [
            pltpu.VMEM((D, D), bf16), pltpu.VMEM((D, T), bf16), pltpu.VMEM((D, T), bf16),
            pltpu.VMEM((D, T + 2 * LEAD), bf16), pltpu.VMEM((D, T + 2 * LEAD), bf16), pltpu.SemaphoreType.DMA((n,)),
        ],
        (sums, dr1, mix, ctx, f, b, small, conv, *pieces), lanes, 5_000_000_000, 25_000_000, (1,))


def scores_kernel(p, sums_in, mix_ref, dctx_ref, f_ref, b_ref, lm_ref, a_ref, ns_ref, small_ref, dz0_ref, dbv_ref,
                  dqk_ref, cols_ref, dz_ref, da_ref, *, hook):
    hook(0)
    spread = segment_spread()
    for h in range(HEADS):
        da_ref[h] = jnp.zeros((LM, LM), f32)
        dz_ref[h] = dz0_ref[h]

    def ns_step(i, _):
        k = NS_ITERS - 1 - i
        d3, dzs, dps, d2 = [], [], [], []
        for h in range(HEADS):
            dzn = split(0.25 * dz_ref[h])
            d3.append(split(dot3(split(ns_ref[k, 0, h]), dzn, TN)))
            dz_ref[h] = dot3(dzn, split(ns_ref[k, 3, h]), NT)
        for h in range(HEADS):
            p = split(ns_ref[k, 1, h])
            d2.append(split(-dot3(p, d3[h], TN)))
            dps.append(dot3(d3[h], split(ns_ref[k, 2, h]), NT))
        for h in range(HEADS):
            p = ns_ref[k, 1, h]
            d1 = dot3(split(p), d2[h], TN)
            dp = d1 - dps[h] - dot3(d2[h], split(eye(7.0) - p), NT)
            dps[h] = split(dp)
        for h in range(HEADS):
            da_ref[h] += dot3(dps[h], split(ns_ref[k, 0, h]), NT)
            dz_ref[h] += dot3(split(a_ref[h]), dps[h], TN)
        return 0

    lax.fori_loop(0, NS_ITERS // 2, ns_step, 0)
    hook(1)
    lax.fori_loop(NS_ITERS // 2, NS_ITERS, ns_step, 0)
    hook(2)

    def score_step(h, _):
        base = h * HD
        a = a_ref[h]
        dz0 = dz_ref[h].T
        s = 1.0 / jnp.sum(a * a)
        da = da_ref[h] + s * dz0 - (2.0 * s * s * jnp.sum(dz0 * a)) * a
        dsa = (SCALE * a * (da - jnp.sum(a * da, axis=1, keepdims=True))).astype(bf16)
        ql = lm_ref[rows(base, HD), :]
        kl = lm_ref[rows(D + base, HD), :]
        q = mix_ref[rows(base, HD), :]
        k = mix_ref[rows(D + base, HD), :]
        f = f_ref[rows(base, HD), :].astype(f32)
        df = dot(small_ref[2, h].astype(bf16), dctx_ref[rows(base, HD), :], NN)
        dsf = (SCALE * f * (df - jnp.sum(f * df, axis=0, keepdims=True))).astype(bf16)
        b = b_ref[rows(base, HD), :].astype(f32)
        db = dot(dbv_ref[h], mix_ref[rows(2 * D + base, HD), :], NN)
        dsb = (SCALE * b * (db - jnp.sum(b * db, axis=1, keepdims=True))).astype(bf16)
        dkl = dot(q, dsf, NT) + dot(ql, dsa, NN)
        dql = dot(kl, dsa, NT) + dot(k, dsb, NT)
        dq = dot(kl, dsf, NN) + dot((dql * (1.0 / SEG)).astype(bf16), spread, NN)
        dk = dot(ql, dsb, NN) + dot((dkl * (1.0 / SEG)).astype(bf16), spread, NN)
        dqk_ref[rows(base, HD), :] = dq.astype(bf16)
        dqk_ref[rows(D + base, HD), :] = dk.astype(bf16)
        return 0

    lax.fori_loop(0, HEADS // 2, score_step, 0)
    hook(3)
    lax.fori_loop(HEADS // 2, HEADS, score_step, 0)
    cols_ref[...] = sums_in[...]
    cols_ref[:, p : p + 1] = lane_sum(dqk_ref[0:D, :])
    hook(4)


def scores(sums, mix, dctx, f, b, lm, a, ns, small, dz0, dbv, layer, lanes=(None, ())):
    return call(
        functools.partial(scores_kernel, 8 * layer), "scores", [sd(2 * D, T, t=bf16), sd(D, 128)], [vm()] * 11,
        [vm()] * 2, [pltpu.VMEM((HEADS, LM, LM), f32), pltpu.VMEM((HEADS, LM, LM), f32)],
        (sums, mix, dctx, f, b, lm, a, ns, small, dz0, dbv), lanes, 3_000_000_000, 30_000_000)


def inputs_kernel(n, first, tail, dr1_ref, xl_ref, dqk_ref, dv_ref, *rest, hook):
    order = Order(n)
    pieces, (keep_ref, send_ref, dx_ref, w_ref, perm_ref, sem) = rest[:n], rest[n:]
    loads = loader(pieces, w_ref, sem, (0, 3 * D))
    for copy in loads:
        copy.start()
    permute_rows(perm_ref, xl_ref, order, D // 8)
    for lane in tail:
        lane.use(keep_ref, send_ref)
    hook(0)
    for i in range(3):
        d = dqk_ref[i * D : (i + 1) * D, :] if i < 2 else dv_ref[...]
        for part, ref in enumerate((send_ref, keep_ref)):
            mine = perm_ref[(1 - part) * (D // 2) : (2 - part) * (D // 2), :]
            ref[:, i * D : (i + 1) * D] = dot(mine, d, NT).astype(bf16)
        hook(i + 1)
    for copy in loads:
        copy.wait()

    def dx_step(i, _):
        at = rows(i * SUB, SUB)
        got = dr1_ref[at, :] + dot(w_ref[at, 0 : 2 * D], dqk_ref[...], NN)
        got = got + dot(w_ref[at, 2 * D :], dv_ref[...], NN)
        if first:
            dx_ref[:, at] = got.T
        else:
            dx_ref[at, :] = got
        return 0

    for i in range(D // SUB):
        dx_step(i, 0)
        hook(i + 4)
    for i in range(7, TURNS):
        hook(i)


TURNS = 16


def inputs(dr1, xl, dqk, dv, pieces, first, lanes=(None, ()), tail=()):
    n = len(pieces)
    return call(
        functools.partial(inputs_kernel, n, first, tail), "inputs",
        [sd(D // 2, 3 * D, t=bf16), sd(D // 2, 3 * D, t=bf16), sd(*((T, D) if first else (D, T)))],
        [vm()] * 4 + anywhere(n), [vm()] * 3,
        [pltpu.VMEM((D, 3 * D), bf16), pltpu.VMEM((D, T), bf16), pltpu.SemaphoreType.DMA((n,))],
        (dr1, xl, dqk, dv, *pieces), lanes, 7_400_000_000, 25_000_000)


class Ring:
    def __init__(self, wide, narrow):
        self.wide, self.narrow = wide, narrow
        self.bits = wide.bit_length() - 1
        up = list(range(1, self.bits))
        self.gather_order = (up, up[::-1])
        self.scatter_order = (up[::-1], up)
        self.exact = wide == 8 and narrow == 4

    def pairs(self, flip):
        n = self.narrow
        out = []
        for w in range(self.wide):
            for z in range(n):
                to_w, to_z = flip(w, z)
                out.append((w * n + z, to_w * n + to_z))
        return out

    def narrow_pairs(self, k):
        return self.pairs(lambda w, z: (w, z ^ k))

    def step_pairs(self, order, s):
        return self.pairs(lambda w, z: (w ^ (1 << order[w & 1][s]), z))

    def core_pairs(self):
        return self.pairs(lambda w, z: (w ^ 1, z))

    def gathered(self, w):
        out = []
        for other in (0, 1):
            v = w ^ other
            for code in range(self.wide // 2):
                t = v
                for s in range(self.bits - 1):
                    if code >> s & 1:
                        t ^= 1 << self.gather_order[v & 1][s]
                out.append(t)
        return out

    def slots(self, w):
        out = []
        for other in (0, 1):
            v = w ^ other
            for code in range(self.wide // 2):
                t = v
                for s in range(self.bits - 1):
                    if code >> (self.bits - 2 - s) & 1:
                        t ^= 1 << self.scatter_order[v & 1][s]
                out.append(t)
        return out

    def mine(self, table):
        return lax.dynamic_index_in_dim(jnp.asarray(table), lax.axis_index("wide"), 0, keepdims=False)

    def gather(self, shard):
        z = lax.axis_index("narrow")
        parts = [shard] + [lax.ppermute(shard, AXES, self.narrow_pairs(k)) for k in range(1, self.narrow)]
        yield []
        bit = 1
        while bit < self.narrow:
            swap = (z & bit) != 0
            parts = [jnp.where(swap, parts[k ^ bit], parts[k]) for k in range(self.narrow)]
            bit *= 2
        held = [jnp.concatenate(parts, axis=0)]
        got = held
        for s in range(self.bits - 1):
            pairs = self.step_pairs(self.gather_order, s)
            fresh, got = got, [lax.ppermute(h, AXES, pairs) for h in held]
            held = held + got
            yield fresh
        other = [lax.ppermute(h, AXES, self.core_pairs()) for h in held]
        yield got
        held = held + other
        return held if self.exact else [self.join(held)]

    def join(self, pieces):
        inverse = np.stack([np.argsort(self.gathered(w)) for w in range(self.wide)]).astype(np.int32)
        stacked = jnp.stack(pieces)
        return jnp.take(stacked, self.mine(inverse), axis=0).reshape(-1, stacked.shape[-1])

    def scatter(self, keep, send):
        half = self.wide // 2
        if not self.exact:
            slots = np.stack([self.slots(w) for w in range(self.wide)]).astype(np.int32)
            whole = jnp.concatenate([keep, send], axis=0)
            whole = whole.reshape(self.wide, -1, whole.shape[-1])
            whole = jnp.take(whole, self.mine(slots), axis=0)
            keep, send = whole[:half], whole[half:]
        got = lax.ppermute(send, AXES, self.core_pairs())
        yield [send]
        total = keep.astype(f32) + got.astype(f32)
        for s in range(self.bits - 1):
            half //= 2
            away = total[half:].astype(bf16)
            got = lax.ppermute(away, AXES, self.step_pairs(self.scatter_order, s))
            yield [away]
            total = total[:half] + got.astype(f32)
        total = total[0]
        size = total.shape[0] // self.narrow
        z = lax.axis_index("narrow")
        own = lax.dynamic_slice_in_dim(total, z * size, size, axis=0)
        low = total.astype(bf16)
        parts = [lax.dynamic_slice_in_dim(low, (z ^ k) * size, size, axis=0) for k in range(1, self.narrow)]
        got = [lax.ppermute(parts[k - 1], AXES, self.narrow_pairs(k)) for k in range(1, self.narrow)]
        yield parts
        for part in got:
            own = own + part.astype(f32)
        return own

    def sum(self, keep, send):
        blocks = self.wide // 2
        return finish(self.scatter(
            keep.reshape(blocks, -1, keep.shape[-1]), send.reshape(blocks, -1, send.shape[-1])))

    def total(self, value):
        bit = 1
        while bit < self.narrow:
            value = value + lax.ppermute(value, AXES, self.narrow_pairs(bit))
            bit *= 2
        for s in range(self.bits - 1):
            value = value + lax.ppermute(value, AXES, self.pairs(lambda w, z: (w ^ (2 << s), z)))
        return value + lax.ppermute(value, AXES, self.core_pairs())


def natural_halves(keep, send):
    both = jnp.stack([keep, send], axis=1)
    both = both.reshape(2, -1, both.shape[-1])
    return both[0], both[1]


def conv_rows(conv):
    at = LEAD - RADIUS
    tail = CONV_K - at - KSIZE
    both = jnp.stack([conv, conv[:, ::-1]], axis=1)
    return jnp.pad(both.astype(f32), ((0, 0), (0, 0), (at, tail)))


def finish(steps):
    while True:
        try:
            next(steps)
        except StopIteration as end:
            return end.value


def small_outputs(ring, total, size, hidden_size):
    layers = total.shape[0] // (8 + STEPS)
    here = lax.axis_index("wide") * ring.narrow + lax.axis_index("narrow")
    lines = total[: 8 * layers, :D].reshape(layers, 8, D)
    lines = lax.dynamic_slice_in_dim(lines, here * size, size, axis=2)
    inb = total[8 * layers :, :D].reshape(layers, FF)
    inb = lax.dynamic_slice_in_dim(inb, here * hidden_size, hidden_size, axis=1)
    taps = total[:, D : D + KSIZE].reshape(layers, HEADS, KSIZE)
    return lines[:, :6], lines[:, 6:], inb, taps


def small_shard(in_b, bias_rows, gain_rows):
    layers, size = bias_rows.shape[0], bias_rows.shape[2]
    columns = jnp.concatenate([bias_rows, gain_rows], axis=1).transpose(2, 0, 1).reshape(size, 8 * layers)
    inner_bias = in_b.reshape(layers, size, -1).transpose(1, 0, 2).reshape(size, -1)
    small = jnp.concatenate([columns, inner_bias], axis=1)
    return jnp.pad(small, ((0, 0), (0, 128 - small.shape[1])))


def gather_all(ring, attention_shards, in_w, out2_w):
    layers = in_w.shape[0]
    return (
        [finish(ring.gather(shard)) for shard in attention_shards],
        [finish(ring.gather(in_w[layer])) for layer in range(layers)],
        [finish(ring.gather(out2_w[layer])) for layer in range(layers)],
    )


class Plan:
    def __init__(self):
        self.count = 0

    def lanes(self, *lanes):
        self.count += 1
        return (self.count, list(lanes))


def pieces_of(block, a, b, c):
    return [block, a.value] + [m.value for m in b] + [m.value for m in c]


def body(ring, tokens, cotangent, qkv_w, out_w, in_w, in_b, out2_w, bias_rows, gain_rows, conv_w):
    layers = qkv_w.shape[0]
    size = qkv_w.shape[1]
    small = small_shard(in_b, bias_rows, gain_rows)
    shards = [
        jnp.concatenate([qkv_w[layer], out_w[layer]] + ([small] if layer == 0 else []), axis=1)
        for layer in range(layers)]
    plan = Plan()
    none = (None, ())
    on = ring.exact and layers == 2
    x = tokens.T.astype(f32)
    conv = [conv_rows(conv_w[layer]) for layer in range(layers)]
    lanes = {name: [none] * layers for name in ("project", "attend", "up", "down")}

    if on:
        spread = Spread(shards[0], 0, 1)
        exchange(plan.lanes(spread), 2)
        u1 = spread.value
        a1 = Move(u1, "a", 0, 1)
        b1 = [Move(u1, "b", 1, 2), Move(a1, "b", 1, 2)]
        c1 = [Move(u1, "core", 0, 3), Move(a1, "core", 1, 3)] + [Move(b, "core", 2, 3) for b in b1]
        s2, s3 = Spread(in_w[0], 0, 3), Spread(out2_w[0], 0, 3)
        exchange(plan.lanes(a1, *b1, *c1, s2, s3), 4)
        att = [pieces_of(u1, a1, b1, c1), None]
        win, wout = [None, None], [None, None]
    else:
        att, win, wout = gather_all(ring, shards, in_w, out2_w)

    kept = []
    par = None
    for layer in range(layers):
        final = layer == layers - 1
        if on and layer == 0:
            u2, u3 = s2.value, s3.value
            a2, a3 = Move(u2, "a", 0, 4), Move(u3, "a", 0, 4)
            c2, c3 = [Move(u2, "core", 0, 4)], [Move(u3, "core", 0, 4)]
            lanes["project"][0] = plan.lanes(a2, c2[0], a3, c3[0])
        if on and layer == 1:
            b5 = [Move(u5, "b", 0, 4), Move(a5.value, "b", 0, 4)]
            c5 = [Move(u5, "core", 0, 4), Move(a5.value, "core", 0, 4)]
            lanes["project"][1] = plan.lanes(*b5, *c5)
        xl, mix, lm, par = project(x, att[layer], par, layer, lanes["project"][layer])
        if on and layer == 0:
            b2 = [Move(u2, "b", 0, 1), Move(a2.value, "b", 0, 1)]
            b3 = [Move(u3, "b", 1, 3), Move(a3.value, "b", 1, 3)]
            c2 += [Move(a2.value, "core", 0, 1)] + [Move(b, "core", 1, 4) for b in b2]
            c3 += [Move(a3.value, "core", 0, 1)] + [Move(b, "core", 3, 4) for b in b3]
            s4 = Spread(shards[1], 0, 4)
            lanes["attend"][0] = plan.lanes(*b2, *b3, *c2[1:], *c3[1:], s4)
        if on and layer == 1:
            b6 = [Move(u6, "b", 0, 2), Move(a6.value, "b", 0, 2)]
            c6 = [Move(u6, "core", 0, 1), Move(a6.value, "core", 0, 1)] + [Move(b, "core", 2, 4) for b in b6]
            c5 += [Move(b.value, "core", 0, 4) for b in b5]
            lanes["attend"][1] = plan.lanes(*b6, *c6, *c5[2:])
        ctx, f, b, a, ns, sm, xhat1, rstd1 = attend(
            x, mix, lm, att[layer], par, conv[layer], layer, lanes["attend"][layer])
        if on and layer == 0:
            win[0], wout[0] = pieces_of(u2, a2, b2, c2), pieces_of(u3, a3, b3, c3)
            u4 = s4.value
            a4 = Move(u4, "a", 0, 1)
            b4 = [Move(u4, "b", 1, 4), Move(a4, "b", 1, 4)]
            c4 = [Move(u4, "core", 0, 1), Move(a4, "core", 1, 4)]
            s5, s6 = Spread(in_w[1], 0, 4), Spread(out2_w[1], 0, 4)
            lanes["up"][0] = plan.lanes(a4, *b4, *c4, s5, s6)
        if on and layer == 1:
            win[1], wout[1] = pieces_of(u5, a5, b5, c5), pieces_of(u6, a6, b6, c6)
        at = 8 * layers + FF // D * layer
        inb = par[:, at : at + FF // D].reshape(FF, 1)
        act, slope = up(xhat1, win[layer], par, inb, layer, lanes["up"][layer])
        if on and layer == 0:
            c4 += [Move(b.value, "core", 0, 4) for b in b4]
            u5, u6 = s5.value, s6.value
            a5, a6 = Move(u5, "a", 0, 4), Move(u6, "a", 0, 4)
            lanes["down"][0] = plan.lanes(*c4[2:], a5, a6)
        xhat2, rstd2, x = down(xhat1, act, wout[layer], par, layer, final, lanes["down"][layer])
        if on and layer == 0:
            att[1] = pieces_of(u4, a4, b4, c4)
        kept.append((xl, mix, lm, ctx, f, b, a, ns, sm, xhat1, rstd1, act, slope, xhat2, rstd2))
    output = x

    dy = cotangent
    sums = jnp.zeros((D, 128), f32)
    taps = [None] * layers
    grads = [[None] * 4 for _ in range(layers)]
    waiting = []

    def sum_first(keep, send, turns, layer, place, **more):
        lane = ReduceFirst(keep, send, turns, **more)
        waiting.append((lane, layer, place))
        return lane

    def sum_last(turns, chained=False):
        lane, layer, place = waiting.pop(0)
        if chained:
            last = ReduceLast(None, None, turns, inside=lane)
        else:
            last = ReduceLast(*lane.value, turns)
        ends.append((last, layer, place))
        return last

    ends = []
    halves = None
    for layer in reversed(range(layers)):
        xl, mix, lm, ctx, f, b, a, ns, sm, xhat1, rstd1, act, slope, xhat2, rstd2 = kept[layer]
        lane = plan.lanes(sum_first(*halves, (0, 1, 4), 1, 0)) if on and halves else none
        keep, send, du, dr2, sums = hidden(
            sums, dy, xhat2, rstd2, par, act, slope, wout[layer], layer, layer == layers - 1, lane)
        if on:
            out2 = (keep.reshape(-1, D), send.reshape(-1, D))
            lane = [sum_last((0, 1, 4))] if waiting else []
            lane = plan.lanes(*lane, sum_first(*out2, (0, 1, 4), layer, 3))
        else:
            keep, send = natural_halves(keep, send)
            grads[layer][3] = ring.sum(keep, send)
        keep, send, dr1, sums = inner(sums, du, dr2, xhat1, rstd1, par, win[layer], layer, lane)
        if on:
            lane = plan.lanes(sum_last((0, 1, 4)), sum_first(keep, send, (0, 1, 4), layer, 2))
        else:
            grads[layer][2] = ring.sum(keep, send)
        keep, send, dctx, dv, dz, dbv, taps[layer], sums = values(
            sums, dr1, mix, ctx, f, b, sm, conv[layer], att[layer], layer, lane)
        if on:
            last = sum_last((0, 1, 4))
            lead = sum_first(keep, send, (0, 1, 2), layer, 1, chained=True)
            lane = plan.lanes(last, lead, sum_last((2, 3, 4), chained=True))
        else:
            grads[layer][1] = ring.sum(keep, send)
        dqk, sums = scores(sums, mix, dctx, f, b, lm, a, ns, sm, dz, dbv, layer, lane)
        tail = []
        if on and layer == 0:
            turns = [(1, 4, 7), (2, 5, 9), (3, 6, 11)]
            lane = []
            for part in range(3):
                lead = ReduceFirst(
                    None, None, turns[part], chained=True, columns=slice(part * D, (part + 1) * D))
                after = turns[part][2]
                last = ReduceLast(None, None, (after, after + 2, after + 4), inside=lead)
                tail.append(lead)
                ends.append((last, 0, part))
                lane += [lead, last]
            total = Total(sums, taps, (0, 1, 2, 3, 4, 5))
            lane = plan.lanes(*lane, total)
        else:
            lane = none
        keep, send, dy = inputs(dr1, xl, dqk, dv, att[layer], layer == 0, lane, tuple(tail))
        halves = (keep, send)
        if not on:
            grads[layer][0] = ring.sum(keep, send)
    if on:
        qkv = [None] * 3
        for lane, layer, place in ends:
            if layer == 0 and lane.columns == D and lane.inside is not None and lane.inside.at is not None:
                qkv[place] = lane.value
            else:
                grads[layer][place] = lane.value
        grads[0][0] = jnp.concatenate(qkv, axis=1)
        total = total.value
    else:
        flat = jnp.concatenate([sums.T[:SMALL], jnp.concatenate(taps, axis=0)], axis=1)
        total = ring.total(flat)
    gbias, ggain, ginb, gtaps = small_outputs(ring, total, size, in_b.shape[1])
    stacked = [jnp.stack([grads[layer][i] for layer in range(layers)]) for i in range(4)]
    return (output, dy, stacked[0], stacked[1], stacked[2], ginb, stacked[3], gbias, ggain, gtaps)


def solution(mesh):
    ring = Ring(mesh.shape["wide"], mesh.shape["narrow"])
    rows3 = P(None, AXES, None)
    columns3 = P(None, None, AXES)
    weights = (rows3, rows3, rows3, P(None, AXES), rows3, columns3, columns3, P())
    return jax.shard_map(
        functools.partial(body, ring),
        mesh=mesh,
        in_specs=(P(AXES, None), P(AXES, None)) + weights,
        out_specs=(P(AXES, None), P(AXES, None)) + weights,
        check_vma=False,
    )
```

```python
import functools
import jax
import jax.numpy as jnp
import numpy as np
from jax import lax
from jax.experimental import pallas as pl
from jax.experimental.pallas import tpu as pltpu
from jax.sharding import PartitionSpec as P

D = 768
HEADS = 12
HD = 64
FF = 3072
LM = 64
KSIZE = 33
RADIUS = KSIZE // 2
NS_ITERS = 6
T = 1024
SEG = T // LM
SCALE = HD ** -0.5
EPS = 1e-05
CONV_N = 256
CONV_K = 512
CONV_BLOCKS = T // CONV_N
LEAD = 128
f32 = jnp.float32
bf16 = jnp.bfloat16
AXES = ("wide", "narrow")
NN = (((1,), (0,)), ((), ()))
NT = (((1,), (1,)), ((), ()))
TN = (((0,), (0,)), ((), ()))
VMEM_LIMIT = 60 * 1024 * 1024


def dot(a, b, dims):
    return lax.dot_general(a, b, dims, preferred_element_type=f32)


def split(a):
    high = a.astype(bf16)
    return high, (a - high.astype(f32)).astype(bf16)


def dot3(a, b, dims):
    return dot(a[0], b[0], dims) + (dot(a[0], b[1], dims) + dot(a[1], b[0], dims))


def rows(start, size):
    if isinstance(start, int):
        return pl.ds(start, size)
    return pl.ds(pl.multiple_of(start, size), size)


def segment_mean():
    token = lax.broadcasted_iota(jnp.int32, (T, LM), 0)
    seg = lax.broadcasted_iota(jnp.int32, (T, LM), 1)
    return jnp.where(token // SEG == seg, 1.0 / SEG, 0.0).astype(bf16)


def segment_spread():
    token = lax.broadcasted_iota(jnp.int32, (LM, T), 1)
    seg = lax.broadcasted_iota(jnp.int32, (LM, T), 0)
    return jnp.where(token // SEG == seg, 1.0, 0.0).astype(bf16)


def eye(value):
    i = lax.broadcasted_iota(jnp.int32, (LM, LM), 0)
    j = lax.broadcasted_iota(jnp.int32, (LM, LM), 1)
    return jnp.where(i == j, value, 0.0).astype(f32)


def toeplitz(row):
    full = jnp.broadcast_to(row, (CONV_N, CONV_K))
    return pltpu.roll(full, 0, 1, stride=1, stride_axis=0).astype(bf16)


def windows(ref, base):
    return jnp.concatenate(
        [ref[rows(base, HD), CONV_N * b : CONV_N * b + CONV_K] for b in range(CONV_BLOCKS)], axis=0
    )


def stack_blocks(value):
    return jnp.concatenate(
        [value[:, CONV_N * b : CONV_N * (b + 1)] for b in range(CONV_BLOCKS)], axis=0
    )


def unstack_blocks(value):
    return jnp.concatenate(
        [value[HD * b : HD * (b + 1), :] for b in range(CONV_BLOCKS)], axis=1
    )


def norm_forward(r_ref, xhat_ref, rstd_ref, width=128):
    for c in range(0, T, width):
        r = r_ref[:, c : c + width]
        center = r - jnp.mean(r, axis=0, keepdims=True)
        rstd = lax.rsqrt(jnp.mean(center * center, axis=0, keepdims=True) + EPS)
        xhat_ref[:, c : c + width] = center * rstd
        rstd_ref[:, c : c + width] = jnp.broadcast_to(rstd, (8, width))


def vm():
    return pl.BlockSpec(memory_space=pltpu.VMEM)


def anywhere(n):
    return [pl.BlockSpec(memory_space=pl.ANY)] * n


def whole(*s):
    return pl.BlockSpec(s, lambda *_: (0,) * len(s))


def sd(*s, t=f32):
    return jax.ShapeDtypeStruct(s, t)


def loader(pieces, dst, sem, columns=None):
    r = pieces[0].shape[0]
    order = Order(len(pieces))
    out = []
    for i, piece in enumerate(pieces):
        src = piece if columns is None else piece.at[:, pl.ds(*columns)]
        at = rows(order.target(i) * r, r)
        out.append(pltpu.make_async_copy(src, dst.at[at, :], sem.at[i]))
    return out


def sizes_of(groups, layer):
    return [(len(g), g[0].shape[1] - (128 if layer == 0 and i == 0 else 0)) for i, g in enumerate(groups)]


def grouped(refs, sizes):
    groups = []
    for n, _ in sizes:
        groups.append(refs[:n])
        refs = refs[n:]
    return groups, refs


def column_loader(groups, sizes, dst, sem, low, high):
    out = []
    at = 0
    for g, (n, width) in enumerate(sizes):
        a, b = max(low, at), min(high, at + width)
        if b > a:
            out += loader(groups[g], dst.at[:, pl.ds(a - low, b - a)], sem.at[g], (a - at, b - a))
        at += width
    return out


def call(kernel, name, out_shape, in_specs, out_specs, scratch, args, lanes, flops, size, grid=None, trans=0):
    identity, lanes = lanes
    ins, outs = len(args), len(out_shape)
    lane_args = [a for lane in lanes for a in lane.args]
    lane_outs = [o for lane in lanes for o in lane.outs]
    lane_scratch = [o for lane in lanes for o in lane.scratch]

    def run(*refs):
        refs = list(refs)

        def take(n):
            got = refs[:n]
            del refs[:n]
            return got

        own = take(ins)
        lane_in = [take(len(lane.args)) for lane in lanes]
        own += take(outs)
        lane_out = [take(len(lane.outs)) for lane in lanes]
        own += take(len(scratch))
        for lane, a, o in zip(lanes, lane_in, lane_out):
            lane.bind(a, o, take(len(lane.scratch)))

        def hook(i):
            if lanes and i == 0:
                near = Near()
                names = sorted({p for lane in lanes for p in lane.partners})
                barrier = pltpu.get_barrier_semaphore()
                for p in names:
                    pl.semaphore_signal(barrier, inc=1, device_id=near.at(p), device_id_type=pl.DeviceIdType.MESH)
                pl.semaphore_wait(barrier, len(names))
            for lane in lanes:
                lane.turn(i)

        kernel(*own, hook=hook)

    params = {"collective_id": identity, "has_side_effects": True} if lanes else {}
    got = pl.pallas_call(
        run,
        out_shape=list(out_shape) + [o for o, _ in lane_outs],
        in_specs=list(in_specs) + [spec for lane in lanes for spec in lane.specs],
        out_specs=list(out_specs) + [spec for _, spec in lane_outs],
        scratch_shapes=list(scratch) + lane_scratch,
        **({} if grid is None else {"grid": grid}),
        compiler_params=pltpu.CompilerParams(vmem_limit_bytes=VMEM_LIMIT, **params),
        cost_estimate=pl.CostEstimate(flops=flops, bytes_accessed=size, transcendentals=trans),
        name=name,
    )(*args, *lane_args)
    own, rest = list(got[:outs]), list(got[outs:])
    for lane in lanes:
        n = len(lane.outs)
        lane.done(rest[:n])
        rest = rest[n:]
    return own


class Near:
    def __init__(self):
        self.w, self.z = lax.axis_index("wide"), lax.axis_index("narrow")

    def over(self, k):
        z = self.z
        if k == 1:
            return z + 1 - 2 * (z % 2)
        if k == 2:
            return z + 2 - 4 * (z // 2)
        return 3 - z

    def at(self, name):
        w, core = self.w, self.w % 2
        if name[0] == "z":
            return (w, self.over(int(name[1])))
        if name == "core":
            return (w + 1 - 2 * core, self.z)
        step = {"a": 2 + 2 * core, "b": 4 - 2 * core, "x": 2, "y": 4}[name]
        return (w + step - 2 * step * ((w // step) % 2), self.z)


def remote(src, dst, send, recv, name):
    return pltpu.make_async_remote_copy(
        src_ref=src, dst_ref=dst, send_sem=send, recv_sem=recv, device_id=Near().at(name),
        device_id_type=pl.DeviceIdType.MESH)


DMA = pltpu.SemaphoreType.DMA
ANY = pl.BlockSpec(memory_space=pl.ANY)


class Move:
    def __init__(self, source, name, start, wait):
        self.chained = not hasattr(source, "dtype")
        self.source, self.name, self.start, self.wait = source, name, start, wait
        self.shape = source.shape
        self.args = [] if self.chained else [source]
        self.specs = [ANY] * len(self.args)
        self.outs = [(sd(*self.shape, t=bf16), ANY)]
        self.scratch = [DMA((2,))]
        self.partners = [name]

    def bind(self, args, outs, scratch):
        self.src = self.source.dst if self.chained else args[0]
        self.dst, self.sem = outs[0], scratch[0]

    def copy(self):
        return remote(self.src, self.dst, self.sem.at[0], self.sem.at[1], self.name)

    def turn(self, i):
        if i == self.wait:
            self.copy().wait()
        if i == self.start:
            self.copy().start()

    def done(self, got):
        self.value = got[0].reshape(-1, self.shape[-1])


class Spread:
    def __init__(self, shard, start, wait):
        self.start, self.wait = start, wait
        self.shape = (4, *shard.shape)
        self.args, self.specs = [shard], [ANY]
        self.outs = [(sd(*self.shape, t=bf16), ANY)]
        self.scratch = [DMA((7,))]
        self.partners = ["z1", "z2", "z3"]

    def bind(self, args, outs, scratch):
        self.src, self.dst, self.sem = args[0], outs[0], scratch[0]

    def copies(self):
        z = lax.axis_index("narrow")
        out = [pltpu.make_async_copy(self.src, self.dst.at[z], self.sem.at[6])]
        for k in (1, 2, 3):
            out.append(remote(self.src, self.dst.at[z], self.sem.at[2 * k - 2], self.sem.at[2 * k - 1], f"z{k}"))
        return out

    def turn(self, i):
        if i == self.wait:
            for copy in self.copies():
                copy.wait()
        if i == self.start:
            for copy in self.copies():
                copy.start()

    def done(self, got):
        self.value = got[0].reshape(-1, self.shape[-1])


class Gather:
    def __init__(self, block):
        self.block, self.moves = block, {}

    def at(self, name):
        if name == "own":
            return self.block
        return self.moves[name]

    def go(self, **turns):
        out = []
        fresh = {}
        value = lambda k: fresh[k] if k in fresh else (
            self.moves[k].value if k in self.moves else
            self.block.value if hasattr(self.block, "value") else self.block)
        for key, turn in turns.items():
            if key == "a":
                todo = [("a", "own", "a")]
            elif key == "b":
                todo = [("b0", "own", "b"), ("b1", "a", "b")]
            else:
                todo = {"core0": [("c0", "own", "core")], "core1": [("c1", "a", "core")],
                        "core2": [("c2", "b0", "core"), ("c3", "b1", "core")]}[key]
            for name, source, partner in todo:
                fresh[name] = Move(value(source), partner, *turn)
                out.append(fresh[name])
        self.moves.update(fresh)
        return sorted(out, key=lambda m: m.start)

    def pieces(self):
        block = self.block.value if hasattr(self.block, "value") else self.block
        return [block] + [self.moves[k].value for k in ("a", "b0", "b1", "c0", "c1", "c2", "c3")]


def strips(columns):
    width = 384 if columns % 384 == 0 else columns
    return [slice(c, c + width) for c in range(0, columns, width)]


class ReduceFirst:
    def __init__(self, keep, send, turns, chained=False, columns=None):
        self.turns, self.chained, self.at = turns, chained, columns
        rows4 = D // 2 if columns is not None else send.shape[0]
        self.columns = columns.stop - columns.start if columns is not None else send.shape[1]
        self.r = r = rows4 // 4
        self.partners = ["core", "b"]
        shape = (r, self.columns)
        self.args = [] if columns is not None else [keep, send]
        self.specs = [ANY] * len(self.args)
        self.outs = [] if chained else [(sd(*shape, t=bf16), whole(*shape)), (sd(*shape), whole(*shape))]
        self.scratch = [pltpu.VMEM((2 * r, self.columns), bf16), pltpu.VMEM((2 * r, self.columns), bf16),
                        pltpu.VMEM((4 * r, self.columns), bf16), DMA((5,))]
        if chained:
            self.scratch += [pltpu.VMEM(shape, bf16), pltpu.VMEM(shape, f32)]
        if columns is None:
            self.scratch += [pltpu.VMEM((4 * r, self.columns), bf16)]

    def bind(self, args, outs, scratch):
        self.away1, self.got1, self.got0, self.sem = scratch[:4]
        rest = scratch[4:]
        if self.chained:
            self.away2, self.own2 = rest[:2]
            rest = rest[2:]
        else:
            self.away2, self.own2 = outs
        if self.at is None:
            self.keep_from, self.send = args
            self.keep = rest[0]

    def use(self, keep, send, sums):
        self.keep, self.send = keep.at[:, self.at], send.at[:, self.at]

    def load(self):
        return pltpu.make_async_copy(self.keep_from, self.keep, self.sem.at[4])

    def first(self):
        return remote(self.send, self.got0, self.sem.at[0], self.sem.at[1], "core")

    def second(self):
        return remote(self.away1, self.got1, self.sem.at[2], self.sem.at[3], "b")

    def turn(self, i):
        r = self.r
        if i == self.turns[0]:
            self.first().start()
            if self.at is None:
                self.load().start()
        if i == self.turns[1]:
            if self.at is None:
                self.load().wait()
            self.first().wait()
            for at in strips(self.columns):
                self.away1[:, at] = self.keep[2 * r :, at] + self.got0[2 * r :, at]
            self.second().start()
        if i == self.turns[2]:
            self.second().wait()
            for at in strips(self.columns):
                for k, out in ((0, self.own2), (1, self.away2)):
                    block = slice(k * r, (k + 1) * r)
                    value = self.keep[block, at].astype(f32) + self.got0[block, at].astype(f32)
                    out[:, at] = (value + self.got1[block, at].astype(f32)).astype(out.dtype)

    def done(self, got):
        self.value = got


class ReduceLast:
    def __init__(self, away, own, turns, inside=None):
        self.turns, self.inside = turns, inside
        r, columns = (inside.r, inside.columns) if inside else away.shape
        size = r // 4
        self.r, self.columns, self.size = r, columns, size
        self.partners = ["a", "z1", "z2", "z3"]
        self.args = [] if inside else [away, own]
        self.specs = [] if inside else [ANY, whole(r, columns)]
        self.outs = [(sd(size, columns), whole(size, columns))]
        self.scratch = [pltpu.VMEM((r, columns), bf16), pltpu.VMEM((4, size, columns), bf16),
                        pltpu.VMEM((4, size, columns), bf16), pltpu.VMEM((4, size, columns), f32), DMA((8,))]

    def bind(self, args, outs, scratch):
        self.got2, self.parts, self.got3, self.sums, self.sem = scratch
        self.out = outs[0]
        self.away, self.own = (self.inside.away2, self.inside.own2) if self.inside else args

    def third(self):
        return remote(self.away, self.got2, self.sem.at[0], self.sem.at[1], "a")

    def last(self):
        near = Near()
        return [
            remote(self.parts.at[near.over(k)], self.got3.at[near.z], self.sem.at[2 * k], self.sem.at[2 * k + 1], f"z{k}")
            for k in (1, 2, 3)]

    def turn(self, i):
        if i == self.turns[0]:
            self.third().start()
        if i == self.turns[1]:
            self.third().wait()
            for at in strips(self.columns):
                value = self.own[:, at] + self.got2[:, at].astype(f32)
                for k in range(4):
                    block = value[k * self.size : (k + 1) * self.size]
                    self.sums[k, :, at] = block
                    self.parts[k, :, at] = block.astype(bf16)
            for copy in self.last():
                copy.start()
        if i == self.turns[2]:
            for copy in self.last():
                copy.wait()
            near = Near()
            for at in strips(self.columns):
                value = self.sums[near.z, :, at]
                for k in (1, 2, 3):
                    value = value + self.got3[near.over(k), :, at].astype(f32)
                self.out[:, at] = value

    def done(self, got):
        self.value = got[0]


class Third:
    def __init__(self, away, own, turns):
        self.turns = turns
        r, columns = away.shape
        self.columns, self.size = columns, r // 4
        self.partners = ["a"]
        self.args, self.specs = [away, own], [ANY, whole(r, columns)]
        shape = (4, self.size, columns)
        self.outs = [(sd(*shape, t=bf16), whole(*shape)), (sd(*shape), whole(*shape))]
        self.scratch = [pltpu.VMEM((r, columns), bf16), DMA((2,))]

    def bind(self, args, outs, scratch):
        self.away, self.own = args
        self.parts, self.sums = outs
        self.got, self.sem = scratch

    def copy(self):
        return remote(self.away, self.got, self.sem.at[0], self.sem.at[1], "a")

    def turn(self, i):
        if i == self.turns[0]:
            self.copy().start()
        if i == self.turns[1]:
            self.copy().wait()
            for at in strips(self.columns):
                value = self.own[:, at] + self.got[:, at].astype(f32)
                for k in range(4):
                    block = value[k * self.size : (k + 1) * self.size]
                    self.sums[k, :, at] = block
                    self.parts[k, :, at] = block.astype(bf16)

    def done(self, got):
        self.value = got


class Final:
    def __init__(self, parts, sums, turns):
        self.turns = turns
        _, self.size, self.columns = shape = parts.shape
        self.partners = ["z1", "z2", "z3"]
        self.args, self.specs = [parts, sums], [ANY, whole(*shape)]
        self.outs = [(sd(*shape[1:]), whole(*shape[1:]))]
        self.scratch = [pltpu.VMEM(shape, bf16), DMA((8,))]

    def bind(self, args, outs, scratch):
        self.parts, self.sums = args
        self.out = outs[0]
        self.got, self.sem = scratch

    def copies(self):
        near = Near()
        return [
            remote(self.parts.at[near.over(k)], self.got.at[near.z], self.sem.at[2 * k], self.sem.at[2 * k + 1], f"z{k}")
            for k in (1, 2, 3)]

    def turn(self, i):
        if i == self.turns[0]:
            for copy in self.copies():
                copy.start()
        if i == self.turns[1]:
            for copy in self.copies():
                copy.wait()
            near = Near()
            for at in strips(self.columns):
                value = self.sums[near.z, :, at]
                for k in (1, 2, 3):
                    value = value + self.got[near.over(k), :, at].astype(f32)
                self.out[:, at] = value

    def done(self, got):
        self.value = got[0]


SMALL = 24


class Total:
    def __init__(self, taps, turns):
        self.turns = turns
        self.args = list(taps)
        self.specs = [whole(*a.shape) for a in self.args]
        shape = (SMALL, D + 128)
        self.outs = [(sd(*shape), whole(*shape))]
        self.scratch = [pltpu.VMEM((5, *shape), f32), pltpu.VMEM((5, *shape), f32), DMA((10,))]
        self.partners = ["core", "x", "y", "z1", "z2"]

    def bind(self, args, outs, scratch):
        self.taps, self.out = args, outs[0]
        self.held, self.got, self.sem = scratch

    def use(self, keep, send, sums):
        self.sums = sums

    def copy(self, s):
        return remote(self.held.at[s], self.got.at[s], self.sem.at[2 * s], self.sem.at[2 * s + 1], self.partners[s])

    def turn(self, i):
        for s in range(6):
            if i == self.turns[s]:
                if s:
                    self.copy(s - 1).wait()
                    value = self.held[s - 1] + self.got[s - 1]
                    if s < 5:
                        self.held[s] = value
                    else:
                        self.out[...] = value
                else:
                    self.held[0, :, 0:D] = self.sums[...].T[0:SMALL, :]
                    self.held[0, 0:HEADS, D:] = self.taps[0][...]
                    self.held[0, HEADS : 2 * HEADS, D:] = self.taps[1][...]
                if s < 5:
                    self.copy(s).start()

    def done(self, got):
        self.value = got[0]


CHUNK = 768
STEPS = FF // CHUNK
SUB = 768


def flip(t, stride):
    return t + stride - 2 * stride * ((t // stride) % 2)


class Order:
    def __init__(self, n):
        self.exact = n == 8
        self.core = 0
        if self.exact:
            self.w = lax.axis_index("wide")
            self.core = self.w % 2

    def target(self, i):
        if not self.exact:
            return i
        other, code = i // 4, i % 4
        t = self.w + other * (1 - 2 * self.core)
        core = t % 2
        if code % 2:
            t = flip(t, 2 + 2 * core)
        if code // 2:
            t = flip(t, 4 - 2 * core)
        return t

    def slot(self, j, other):
        if not self.exact:
            return j
        plane = self.w // 2
        core = self.core if other == 0 else 1 - self.core
        dx, dy = (j + plane) % 2, (j // 2 + plane // 2) % 2
        return dx * (1 + core) + dy * (2 - core)


def exchange(lanes, turns):
    def kernel(hook):
        for i in range(turns):
            hook(i)

    call(kernel, "exchange", [], [], [], [], (), lanes, 0, 10_000_000)


def attention_kernel(sizes, p, x_ref, *rest, hook):
    if p:
        par_ref, *rest = rest
    conv_ref, *rest = rest
    groups, rest = grouped(rest, sizes)
    xl_out, mix_out, lm_ref, *rest = rest
    if not p:
        par_ref, *rest = rest
    (ctx_out, f_out, b_out, a_ref, ns_out, small_ref, xhat_ref, rstd_ref,
     w_ref, vpad_ref, z_ref, sem, xl_ref, mix_ref, ctx_ref, f_ref, b_ref, ns_ref, out_sem, ns_sem, *rest) = rest
    leaving = []

    def leave(src, dst):
        copy = pltpu.make_async_copy(src, dst, out_sem.at[len(leaving)])
        copy.start()
        leaving.append(copy)

    loads = column_loader(groups, sizes, w_ref, sem, 0, 4 * D)
    if not p:
        low_ref, low_sem = rest
        loads += loader(groups[0], low_ref, low_sem, (sizes[0][1], 128))
    for copy in loads:
        copy.start()
    xl_ref[...] = x_ref[...].astype(bf16)
    leave(xl_ref, xl_out)
    vpad_ref[:, 0:LEAD] = jnp.zeros((D, LEAD), bf16)
    vpad_ref[:, LEAD + T :] = jnp.zeros((D, LEAD), bf16)
    hook(0)
    for copy in loads:
        copy.wait()
    if not p:
        par_ref[...] = low_ref[...].astype(f32)
    for part, column in ((0, p), (1, None), (2, p + 1)):

        def mix_step(i, _):
            at = rows(part * D + i * 384, 384)
            got = dot(w_ref[:, at], xl_ref[...], TN)
            if column is not None:
                got = got + par_ref[rows(i * 384, 384), column : column + 1]
            mix_ref[at, :] = got.astype(bf16)
            return 0

        lax.fori_loop(0, 2, mix_step, 0)
        leave(mix_ref.at[pl.ds(part * D, D), :], mix_out.at[pl.ds(part * D, D), :])
        hook(part + 1)
    vpad_ref[:, LEAD : LEAD + T] = mix_ref[2 * D :, :]
    lm_ref[...] = dot(mix_ref[0 : 2 * D, :], segment_mean(), NN).astype(bf16)

    for h in range(HEADS):
        ql = lm_ref[h * HD : (h + 1) * HD, :]
        kl = lm_ref[D + h * HD : D + (h + 1) * HD, :]
        s = dot(ql, kl, TN) * SCALE
        e = jnp.exp(s - jnp.max(s, axis=1, keepdims=True))
        a = e / jnp.sum(e, axis=1, keepdims=True)
        a_ref[h] = a
        z_ref[h] = a.T / jnp.sum(a * a)

    def ns_step(k, _):
        ps, rs = [], []
        for h in range(HEADS):
            z = z_ref[h]
            ns_ref[k, 0, h] = z
            p = dot3(split(a_ref[h]), split(z), NN)
            ns_ref[k, 1, h] = p
            ps.append(split(p))
            rs.append(split(eye(7.0) - p))
        for h in range(HEADS):
            r2 = eye(15.0) - dot3(ps[h], rs[h], NN)
            ns_ref[k, 2, h] = r2
            rs[h] = split(r2)
        for h in range(HEADS):
            r3 = eye(13.0) - dot3(ps[h], rs[h], NN)
            ns_ref[k, 3, h] = r3
            rs[h] = split(r3)
        for h in range(HEADS):
            z_ref[h] = 0.25 * dot3(split(z_ref[h]), rs[h], NN)
        pltpu.make_async_copy(ns_ref.at[k], ns_out.at[k], ns_sem.at[k]).start()
        return 0

    lax.fori_loop(0, NS_ITERS // 2, ns_step, 0)
    hook(4)
    lax.fori_loop(NS_ITERS // 2, NS_ITERS, ns_step, 0)
    hook(5)

    def head_step(h, _):
        base = h * HD
        q = mix_ref[rows(base, HD), :]
        k = mix_ref[rows(D + base, HD), :]
        v = mix_ref[rows(2 * D + base, HD), :]
        ql = lm_ref[rows(base, HD), :]
        kl = lm_ref[rows(D + base, HD), :]
        s = dot(kl, q, TN) * SCALE
        e = jnp.exp(s - jnp.max(s, axis=0, keepdims=True))
        f = (e / jnp.sum(e, axis=0, keepdims=True)).astype(bf16)
        f_ref[rows(base, HD), :] = f
        s = dot(ql, k, TN) * SCALE
        e = jnp.exp(s - jnp.max(s, axis=1, keepdims=True))
        b = (e / jnp.sum(e, axis=1, keepdims=True)).astype(bf16)
        b_ref[rows(base, HD), :] = b
        bv = dot(b, v, NT)
        z = z_ref[h]
        w = dot3(split(z), split(bv), NN)
        small_ref[0, h] = z
        small_ref[1, h] = bv
        small_ref[2, h] = w
        attended = dot(w.astype(bf16), f, TN)
        conv = dot(windows(vpad_ref, base), toeplitz(conv_ref[h, 0:1]), NT)
        ctx_ref[rows(base, HD), :] = (attended + unstack_blocks(conv)).astype(bf16)
        return 0

    for third in range(3):
        lax.fori_loop(third * 4, third * 4 + 4, head_step, 0, unroll=2)
        at = pl.ds(third * 4 * HD, 4 * HD)
        for src, dst in ((f_ref, f_out), (b_ref, b_out), (ctx_ref, ctx_out)):
            leave(src.at[at, :], dst.at[at, :])
        hook(6 + third)

    def out_step(i, _):
        at = rows(i * 384, 384)
        got = dot(w_ref[:, rows(3 * D + i * 384, 384)], ctx_ref[...], TN)
        xhat_ref[at, :] = got + par_ref[at, p + 2 : p + 3] + x_ref[at, :]
        return 0

    lax.fori_loop(0, 2, out_step, 0)
    norm_forward(xhat_ref, xhat_ref, rstd_ref)
    for copy in leaving:
        copy.wait()
    for k in range(NS_ITERS):
        pltpu.make_async_copy(ns_ref.at[k], ns_out.at[k], ns_sem.at[k]).wait()
    hook(9)
    hook(10)


def attention(x, groups, par, conv, layer, lanes=(None, ())):
    first = layer == 0
    sizes = sizes_of(groups, layer)
    n = sizes[0][0]
    got = call(
        functools.partial(attention_kernel, sizes, 8 * layer), "attention",
        [sd(D, T, t=bf16), sd(3 * D, T, t=bf16), sd(2 * D, LM, t=bf16)] + [sd(D, 128)] * first
        + [
            sd(D, T, t=bf16), sd(D, T, t=bf16), sd(D, T, t=bf16), sd(HEADS, LM, LM),
            sd(NS_ITERS, 4, HEADS, LM, LM), sd(3, HEADS, LM, LM), sd(D, T), sd(8, T),
        ],
        [vm()] * (2 if first else 3) + anywhere(n * len(groups)),
        [ANY, ANY, vm()] + [vm()] * first + [ANY, ANY, ANY, vm(), ANY, vm(), vm(), vm()],
        [
            pltpu.VMEM((D, 4 * D), bf16), pltpu.VMEM((D, T + 2 * LEAD), bf16), pltpu.VMEM((HEADS, LM, LM), f32),
            DMA((len(groups), n)), pltpu.VMEM((D, T), bf16), pltpu.VMEM((3 * D, T), bf16), pltpu.VMEM((D, T), bf16),
            pltpu.VMEM((D, T), bf16), pltpu.VMEM((D, T), bf16), pltpu.VMEM((NS_ITERS, 4, HEADS, LM, LM), f32),
            DMA((16,)), DMA((NS_ITERS,)),
        ] + [pltpu.VMEM((D, 128), bf16), DMA((n,))] * first,
        (x, *([] if first else [par]), conv, *[piece for g in groups for piece in g]), lanes,
        6_800_000_000, 40_000_000, trans=2_000_000)
    return got if first else [*got[:3], par, *got[3:]]


def feed_kernel(n, p, last, xhat_ref, par_ref, inb_ref, *rest, hook):
    pieces1, pieces2, rest = rest[:n], rest[n : 2 * n], rest[2 * n :]
    a_ref, g_ref, xhat2_ref, rstd2_ref, next_ref, w1_ref, w2_ref, hl_ref, sem = rest
    j = pl.program_id(0)

    @pl.when(j == 0)
    def _():
        loads = loader(pieces1, w1_ref, sem.at[0])
        for copy in loads:
            copy.start()
        later = loader(pieces2, w2_ref, sem.at[1])
        for copy in later:
            copy.start()
        hook(0)
        h = xhat_ref[...] * par_ref[:, p + 6 : p + 7] + par_ref[:, p + 3 : p + 4]
        hl_ref[...] = h.astype(bf16)
        xhat2_ref[...] = h + par_ref[:, p + 4 : p + 5]
        for copy in loads + later:
            copy.wait()

    u = dot(w1_ref[:, rows(j * CHUNK, CHUNK)], hl_ref[...], TN)
    u = u + inb_ref[rows(j * CHUNK, CHUNK), 0:1]
    cdf = 0.5 + 0.5 * lax.erf(u * (2.0 ** -0.5))
    pdf = jnp.exp(-0.5 * u * u) * ((2.0 * np.pi) ** -0.5)
    a_ref[...] = (u * cdf).astype(bf16)
    g_ref[...] = (cdf + u * pdf).astype(bf16)
    xhat2_ref[...] += dot(w2_ref[rows(j * CHUNK, CHUNK), :], a_ref[...], TN)

    @pl.when(j == STEPS - 1)
    def _():
        norm_forward(xhat2_ref, xhat2_ref, rstd2_ref)
        y = xhat2_ref[...] * par_ref[:, p + 7 : p + 8] + par_ref[:, p + 5 : p + 6]
        if last:
            next_ref[...] = y.T.astype(bf16)
        else:
            next_ref[...] = y

    for i in range(STEPS):

        @pl.when(j == i)
        def _():
            hook(i + 1)


def feed(xhat, pieces1, pieces2, par, inb, layer, last, lanes=(None, ())):
    n = len(pieces1)
    chunk = pl.BlockSpec((CHUNK, T), lambda j: (j, 0))
    next_shape = (T, D) if last else (D, T)
    return call(
        functools.partial(feed_kernel, n, 8 * layer, last), "feed",
        [sd(FF, T, t=bf16), sd(FF, T, t=bf16), sd(D, T), sd(8, T), sd(*next_shape, t=bf16 if last else f32)],
        [whole(D, T), whole(D, 128), whole(FF, 1)] + anywhere(2 * n),
        [chunk, chunk, whole(D, T), whole(8, T), whole(*next_shape)],
        [pltpu.VMEM((D, FF), bf16), pltpu.VMEM((FF, D), bf16), pltpu.VMEM((D, T), bf16), DMA((2, n))],
        (xhat, par, inb, *pieces1, *pieces2), lanes, 9_800_000_000, 40_000_000, (STEPS,), 6_000_000)


def norm_backward(dy_ref, xhat_ref, rstd_ref, gain, out_ref, grads_ref, gain_col, shift_col, width=128):
    total_gain = jnp.zeros((D, width), f32)
    total_shift = jnp.zeros((D, width), f32)
    for c in range(0, T, width):
        dy = dy_ref[:, c : c + width]
        xhat = xhat_ref[:, c : c + width]
        total_shift = total_shift + dy
        total_gain = total_gain + dy * xhat
        dxhat = dy * gain
        m1 = jnp.mean(dxhat, axis=0, keepdims=True)
        m2 = jnp.mean(dxhat * xhat, axis=0, keepdims=True)
        out_ref[:, c : c + width] = rstd_ref[0:1, c : c + width] * (dxhat - m1 - xhat * m2)
    grads_ref[:, gain_col : gain_col + 1] = jnp.sum(total_gain, axis=1, keepdims=True)
    grads_ref[:, shift_col : shift_col + 1] = jnp.sum(total_shift, axis=1, keepdims=True)


def lane_sum(value):
    return jnp.sum(value.astype(f32), axis=1, keepdims=True)


def permute_rows(dst_ref, src_ref, order, block):
    for i in range(D // block):
        dst_ref[i * block : (i + 1) * block, :] = src_ref[
            rows(order.target(i) * block, block), :]


def hidden_kernel(n, p, first, sums_in, dy_ref, xhat_ref, rstd_ref, par_ref, a_ref, g_ref, *rest, hook):
    order = Order(n)
    pieces, (keep_ref, send_ref, du_ref, dr_ref, cols_ref, w_ref, dz_ref, inb_ref, sem) = rest[:n], rest[n:]
    j = pl.program_id(0)

    @pl.when(j == 0)
    def _():
        loads = loader(pieces, w_ref, sem)
        for copy in loads:
            copy.start()
        hook(0)
        if first:
            dr_ref[...] = dy_ref[...].astype(f32).T
            dy = dr_ref
        else:
            dy = dy_ref
        cols_ref[...] = sums_in[...]
        norm_backward(dy, xhat_ref, rstd_ref, par_ref[:, p + 7 : p + 8], dr_ref, cols_ref, p + 7, p + 5)
        dz_ref[...] = dr_ref[...].astype(bf16)
        cols_ref[:, p + 4 : p + 5] = lane_sum(dz_ref[...])
        for copy in loads:
            copy.wait()

    def du_step(i, _):
        base = i * SUB
        da = dot(w_ref[rows(j * CHUNK + base, SUB), :], dz_ref[...], NN)
        du = (da * g_ref[rows(base, SUB), :].astype(f32)).astype(bf16)
        du_ref[rows(base, SUB), :] = du
        inb_ref[rows(base, SUB), :] = lane_sum(du)
        return 0

    lax.fori_loop(0, CHUNK // SUB, du_step, 0)
    half = CHUNK // 2
    core = order.core

    def own(start):
        return a_ref[rows(start, half), :]

    keep_ref[order.slot(j, 0)] = dot(own(core * half), dz_ref[...], NT).astype(bf16)
    send_ref[order.slot(j, 1)] = dot(own((1 - core) * half), dz_ref[...], NT).astype(bf16)
    for i in range(STEPS):

        @pl.when(j == i)
        def _():
            column = 2 * 8 + p // 2 + i
            cols_ref[:, column : column + 1] = inb_ref[...]
            hook(i + 1)


def hidden(sums, dy, xhat, rstd, par, a, g, pieces, layer, first, lanes=(None, ())):
    n = len(pieces)
    chunk = pl.BlockSpec((CHUNK, T), lambda j: (j, 0))
    half = CHUNK // 2
    return call(
        functools.partial(hidden_kernel, n, 8 * layer, first), "hidden",
        [
            sd(STEPS, half, D, t=bf16), sd(STEPS, half, D, t=bf16), sd(FF, T, t=bf16), sd(D, T), sd(D, 128),
        ],
        [whole(D, 128), whole(*dy.shape), whole(D, T), whole(8, T), whole(D, 128), chunk, chunk] + anywhere(n),
        [
            whole(STEPS, half, D), whole(STEPS, half, D), chunk, whole(D, T), whole(D, 128),
        ],
        [pltpu.VMEM((FF, D), bf16), pltpu.VMEM((D, T), bf16), pltpu.VMEM((CHUNK, 1), f32), pltpu.SemaphoreType.DMA((n,))],
        (sums, dy, xhat, rstd, par, a, g, *pieces), lanes, 9_700_000_000, 40_000_000, (STEPS,))


def inner_kernel(n, p, sums_in, du_ref, dr_ref, xhat_ref, rstd_ref, par_ref, *rest, hook):
    order = Order(n)
    pieces, (keep_ref, send_ref, out_ref, cols_ref, w_ref, hl_ref, acc_ref, sem) = rest[:n], rest[n:]
    j = pl.program_id(0)

    @pl.when(j == 0)
    def _():
        loads = loader(pieces, w_ref, sem)
        for copy in loads:
            copy.start()
        hook(0)
        block = D // 8
        for i in range(8):
            at = rows(order.target(i) * block, block)
            hl_ref[i * block : (i + 1) * block, :] = (
                xhat_ref[at, :] * par_ref[at, p + 6 : p + 7] + par_ref[at, p + 3 : p + 4]).astype(bf16)
        acc_ref[...] = dr_ref[...]
        for copy in loads:
            copy.wait()

    for i, ref in enumerate((keep_ref, send_ref)):
        ref[...] = dot(hl_ref[i * (D // 2) : (i + 1) * (D // 2), :], du_ref[...], NT).astype(bf16)

    def dh_step(i, _):
        acc_ref[rows(i * SUB, SUB), :] += dot(
            w_ref[rows(i * SUB, SUB), rows(j * CHUNK, CHUNK)], du_ref[...], NN)
        return 0

    lax.fori_loop(0, D // SUB, dh_step, 0)

    @pl.when(j == STEPS - 1)
    def _():
        cols_ref[...] = sums_in[...]
        norm_backward(acc_ref, xhat_ref, rstd_ref, par_ref[:, p + 6 : p + 7], out_ref, cols_ref, p + 6, p + 3)
        cols_ref[:, p + 2 : p + 3] = lane_sum(out_ref[...].astype(bf16))
    for i in range(STEPS):

        @pl.when(j == i)
        def _():
            hook(i + 1)


def inner(sums, du, dr, xhat, rstd, par, pieces, layer, lanes=(None, ())):
    n = len(pieces)
    return call(
        functools.partial(inner_kernel, n, 8 * layer), "inner",
        [sd(D // 2, FF, t=bf16), sd(D // 2, FF, t=bf16), sd(D, T), sd(D, 128)],
        [whole(D, 128), pl.BlockSpec((CHUNK, T), lambda j: (j, 0)), whole(D, T), whole(D, T), whole(8, T), whole(D, 128)]
        + anywhere(n),
        [
            pl.BlockSpec((D // 2, CHUNK), lambda j: (0, j)), pl.BlockSpec((D // 2, CHUNK), lambda j: (0, j)),
            whole(D, T), whole(D, 128),
        ],
        [pltpu.VMEM((D, FF), bf16), pltpu.VMEM((D, T), bf16), pltpu.VMEM((D, T), f32), pltpu.SemaphoreType.DMA((n,))],
        (sums, du, dr, xhat, rstd, par, *pieces), lanes, 9_700_000_000, 35_000_000, (STEPS,))


def row_loader(src, dst, order, sem):
    block = D // 8
    return [
        pltpu.make_async_copy(
            src.at[rows(order.target(i) * block, block), :], dst.at[pl.ds(i * block, block), :], sem.at[i])
        for i in range(8)]


def values_kernel(sizes, p, sums_in, dr1_ref, mix_from, ctx_from, f_from, b_from, xl_from, small_ref, conv_ref,
                  *rest, hook):
    order = Order(sizes[0][0])
    groups, rest = grouped(rest, sizes)
    (keep_ref, send_ref, dctx_out, dv_ref, dz_ref, dbv_ref, taps_ref, cols_ref,
     w_ref, dp_ref, perm_ref, vpad_ref, dpad_ref, dctx_ref, f_ref, b_ref, v_ref, xperm_ref,
     sem, perm_sem, late_sem) = rest
    early = column_loader(groups, sizes, w_ref, sem, 3 * D, 4 * D)
    perms = row_loader(ctx_from, perm_ref, order, perm_sem.at[0])
    late = [pltpu.make_async_copy(mix_from.at[pl.ds(2 * D, D), :], v_ref, late_sem.at[0]),
            pltpu.make_async_copy(f_from, f_ref, late_sem.at[1]),
            pltpu.make_async_copy(b_from, b_ref, late_sem.at[2])]
    last = row_loader(xl_from, xperm_ref, order, perm_sem.at[1])
    for copy in early + perms + late + last:
        copy.start()
    for ref in (vpad_ref, dpad_ref):
        ref[:, 0:LEAD] = jnp.zeros((D, LEAD), bf16)
        ref[:, LEAD + T :] = jnp.zeros((D, LEAD), bf16)
    dp_ref[...] = dr1_ref[...].astype(bf16)
    hook(0)
    for copy in early:
        copy.wait()

    def dctx_step(i, _):
        at = rows(i * 384, 384)
        got = dot(w_ref[at, :], dp_ref[...], NN).astype(bf16)
        dctx_ref[at, :] = got
        dpad_ref[at, LEAD : LEAD + T] = got
        return 0

    lax.fori_loop(0, 2, dctx_step, 0)
    leave = pltpu.make_async_copy(dctx_ref, dctx_out, late_sem.at[3])
    leave.start()
    for copy in perms:
        copy.wait()
    for i, ref in enumerate((keep_ref, send_ref)):
        ref[:, 0:D] = dot(perm_ref[i * (D // 2) : (i + 1) * (D // 2), :], dp_ref[...], NT).astype(bf16)
    for copy in late:
        copy.wait()
    vpad_ref[:, LEAD : LEAD + T] = v_ref[...]
    hook(1)
    flip = jnp.where(
        lax.broadcasted_iota(jnp.int32, (CONV_N, CONV_N), 0)
        + lax.broadcasted_iota(jnp.int32, (CONV_N, CONV_N), 1) == CONV_N - 1, 1.0, 0.0).astype(bf16)

    def value_step(h, _):
        base = h * HD
        dctx = dctx_ref[rows(base, HD), :]
        f = f_ref[rows(base, HD), :]
        dw = split(dot(f, dctx, NT))
        dz_ref[h] = dot3(dw, split(small_ref[1, h]), NT)
        dbv = dot3(split(small_ref[0, h]), dw, TN).astype(bf16)
        dbv_ref[h] = dbv
        dv = dot(dbv, b_ref[rows(base, HD), :], TN)
        conv = dot(windows(dpad_ref, base), toeplitz(conv_ref[h, 1:2]), NT)
        dv_ref[rows(base, HD), :] = (dv + unstack_blocks(conv)).astype(bf16)
        flipped = dot(stack_blocks(dctx), flip, NN).astype(bf16)
        g = dot(flipped, windows(vpad_ref, base), TN)
        g = pltpu.roll(g, CONV_K - CONV_N + 1 - (LEAD - RADIUS), 1, stride=1, stride_axis=0)
        taps_ref[pl.ds(h, 1), :] = jnp.sum(g[:, 0:128], axis=0, keepdims=True)
        return 0

    lax.fori_loop(0, HEADS // 2, value_step, 0, unroll=2)
    hook(2)
    lax.fori_loop(HEADS // 2, HEADS, value_step, 0, unroll=2)
    hook(3)
    for copy in last:
        copy.wait()
    for i, ref in enumerate((keep_ref, send_ref)):
        ref[:, D:] = dot(xperm_ref[i * (D // 2) : (i + 1) * (D // 2), :], dv_ref[...], NT).astype(bf16)
    cols_ref[...] = sums_in[...]
    cols_ref[:, p + 1 : p + 2] = lane_sum(dv_ref[...])
    leave.wait()
    hook(4)


def values(sums, dr1, mix, ctx, f, b, xl, small, conv, groups, layer, lanes=(None, ())):
    sizes = sizes_of(groups, layer)
    n = sizes[0][0]
    return call(
        functools.partial(values_kernel, sizes, 8 * layer), "values",
        [
            sd(D // 2, 2 * D, t=bf16), sd(D // 2, 2 * D, t=bf16), sd(D, T, t=bf16), sd(D, T, t=bf16),
            sd(HEADS, LM, LM), sd(HEADS, LM, LM, t=bf16), sd(HEADS, 128), sd(D, 128),
        ],
        [vm(), vm()] + [ANY] * 5 + [vm(), vm()] + anywhere(n * len(groups)),
        [vm(), vm(), ANY] + [vm()] * 5,
        [
            pltpu.VMEM((D, D), bf16), pltpu.VMEM((D, T), bf16), pltpu.VMEM((D, T), bf16),
            pltpu.VMEM((D, T + 2 * LEAD), bf16), pltpu.VMEM((D, T + 2 * LEAD), bf16),
        ] + [pltpu.VMEM((D, T), bf16)] * 5 + [DMA((len(groups), n)), DMA((2, 8)), DMA((4,))],
        (sums, dr1, mix, ctx, f, b, xl, small, conv, *[piece for g in groups for piece in g]), lanes,
        6_200_000_000, 25_000_000)


QK = 2 * D
TURNS = 20


def back_kernel(sizes, p, out, tail, sums_in, ns_from, mix_from, dctx_from, f_from, b_from, dv_from, xl_from, dr1_from,
                lm_ref, a_ref, small_ref, dz0_ref, dbv_ref, *rest, hook):
    order = Order(sizes[0][0])
    groups, rest = grouped(rest, sizes)
    if out:
        keep_ref, send_ref, *rest = rest
    dx_ref, cols_ref, *rest = rest
    if not out:
        keep_ref, send_ref, *rest = rest
    (w_ref, ns_ref, mix_ref, dctx_ref, f_ref, b_ref, dv_ref, perm_ref, dr1_ref, dz_ref, da_ref,
     sem, ns_sem, late_sem, perm_sem) = rest

    def load_ns(i):
        return pltpu.make_async_copy(
            ns_from.at[NS_ITERS - 1 - i], ns_ref.at[lax.rem(i, 2)], ns_sem.at[lax.rem(i, 2)])

    load_ns(0).start()
    late = [
        pltpu.make_async_copy(src, dst, late_sem.at[i]) for i, (src, dst) in enumerate((
            (mix_from, mix_ref), (dctx_from, dctx_ref), (f_from, f_ref), (b_from, b_ref), (dv_from, dv_ref),
            (dr1_from, dr1_ref)))]
    late += row_loader(xl_from, perm_ref, order, perm_sem)
    late += column_loader(groups, sizes, w_ref, sem, 0, 3 * D)
    for lane in tail:
        lane.use(keep_ref, send_ref, cols_ref)
    for copy in late:
        copy.start()
    hook(0)
    for h in range(HEADS):
        da_ref[h] = jnp.zeros((LM, LM), f32)
        dz_ref[h] = dz0_ref[h]

    def ns_step(i, _):
        k = lax.rem(i, 2)
        load_ns(i).wait()

        @pl.when(i + 1 < NS_ITERS)
        def _():
            load_ns(i + 1).start()

        d3, dzs, dps, d2 = [], [], [], []
        for h in range(HEADS):
            dzn = split(0.25 * dz_ref[h])
            d3.append(split(dot3(split(ns_ref[k, 0, h]), dzn, TN)))
            dz_ref[h] = dot3(dzn, split(ns_ref[k, 3, h]), NT)
        for h in range(HEADS):
            p = split(ns_ref[k, 1, h])
            d2.append(split(-dot3(p, d3[h], TN)))
            dps.append(dot3(d3[h], split(ns_ref[k, 2, h]), NT))
        for h in range(HEADS):
            p = ns_ref[k, 1, h]
            d1 = dot3(split(p), d2[h], TN)
            dp = d1 - dps[h] - dot3(d2[h], split(eye(7.0) - p), NT)
            dps[h] = split(dp)
        for h in range(HEADS):
            da_ref[h] += dot3(dps[h], split(ns_ref[k, 0, h]), NT)
            dz_ref[h] += dot3(split(a_ref[h]), dps[h], TN)
        return 0

    lax.fori_loop(0, NS_ITERS // 2, ns_step, 0)
    hook(1)
    lax.fori_loop(NS_ITERS // 2, NS_ITERS, ns_step, 0)
    for copy in late:
        copy.wait()
    hook(2)
    spread = segment_spread()

    def score_step(h, _):
        base = h * HD
        a = a_ref[h]
        dz0 = dz_ref[h].T
        s = 1.0 / jnp.sum(a * a)
        da = da_ref[h] + s * dz0 - (2.0 * s * s * jnp.sum(dz0 * a)) * a
        dsa = (SCALE * a * (da - jnp.sum(a * da, axis=1, keepdims=True))).astype(bf16)
        ql = lm_ref[rows(base, HD), :]
        kl = lm_ref[rows(D + base, HD), :]
        q = mix_ref[rows(base, HD), :]
        k = mix_ref[rows(D + base, HD), :]
        f = f_ref[rows(base, HD), :].astype(f32)
        df = dot(small_ref[2, h].astype(bf16), dctx_ref[rows(base, HD), :], NN)
        dsf = (SCALE * f * (df - jnp.sum(f * df, axis=0, keepdims=True))).astype(bf16)
        b = b_ref[rows(base, HD), :].astype(f32)
        db = dot(dbv_ref[h], mix_ref[rows(2 * D + base, HD), :], NN)
        dsb = (SCALE * b * (db - jnp.sum(b * db, axis=1, keepdims=True))).astype(bf16)
        dkl = dot(q, dsf, NT) + dot(ql, dsa, NN)
        dql = dot(kl, dsa, NT) + dot(k, dsb, NT)
        dq = dot(kl, dsf, NN) + dot((dql * (1.0 / SEG)).astype(bf16), spread, NN)
        dk = dot(ql, dsb, NN) + dot((dkl * (1.0 / SEG)).astype(bf16), spread, NN)
        mix_ref[rows(base, HD), :] = dq.astype(bf16)
        mix_ref[rows(D + base, HD), :] = dk.astype(bf16)
        return 0

    half = D // 2
    for part in range(2):
        for quarter in range(2):
            start = (2 * part + quarter) * (HEADS // 4)
            lax.fori_loop(start, start + HEADS // 4, score_step, 0)
            if quarter == 0:
                hook(3 + 2 * part)
        for side, ref in ((1, send_ref), (0, keep_ref)):
            mine = perm_ref[side * half : (side + 1) * half, :]
            for k in range(2):
                at = part * D + k * half
                d = mix_ref[k * D + part * half : k * D + (part + 1) * half, :]
                ref[:, at : at + half] = dot(mine, d, NT).astype(bf16)
        hook(4 + 2 * part)
    cols_ref[...] = sums_in[...]
    cols_ref[:, p : p + 1] = lane_sum(mix_ref[0:D, :])
    for i in range(3):
        at = slice(i * 256, (i + 1) * 256)
        got = dr1_ref[at, :] + dot(w_ref[at, 0:QK], mix_ref[0:QK, :], NN) + dot(w_ref[at, QK:], dv_ref[...], NN)
        if p:
            dx_ref[at, :] = got
        else:
            dx_ref[:, at] = got.T
        hook(7 + i)
    for i in range(10, TURNS):
        hook(i)


def back(sums, ns, mix, dctx, f, b, dv, xl, dr1, lm, a, small, dz0, dbv, groups, layer, lanes=(None, ()), tail=(), on=False):
    sizes = sizes_of(groups, layer)
    n = sizes[0][0]
    halves = [(D // 2, QK)] * 2
    out = 0 if on and layer == 0 else 1
    got = call(
        functools.partial(back_kernel, sizes, 8 * layer, out, tail), "back",
        [sd(*h, t=bf16) for h in halves] * out + [sd(*((D, T) if layer else (T, D))), sd(D, 128)],
        [vm()] + [ANY] * 8 + [vm()] * 5 + anywhere(n * len(groups)), [vm()] * (2 + 2 * out),
        [pltpu.VMEM(h, bf16) for h in halves] * (1 - out) + [
            pltpu.VMEM((D, 3 * D), bf16), pltpu.VMEM((2, 4, HEADS, LM, LM), f32), pltpu.VMEM((3 * D, T), bf16),
        ] + [pltpu.VMEM((D, T), bf16)] * 5 + [
            pltpu.VMEM((D, T), f32), pltpu.VMEM((HEADS, LM, LM), f32), pltpu.VMEM((HEADS, LM, LM), f32),
            DMA((len(groups), n)), DMA((2,)), DMA((6,)), DMA((8,)),
        ],
        (sums, ns, mix, dctx, f, b, dv, xl, dr1, lm, a, small, dz0, dbv, *[piece for g in groups for piece in g]),
        lanes, 10_000_000_000, 50_000_000)
    return got if out else [None, None, *got]


class Ring:
    def __init__(self, wide, narrow):
        self.wide, self.narrow = wide, narrow
        self.bits = wide.bit_length() - 1
        up = list(range(1, self.bits))
        self.gather_order = (up, up[::-1])
        self.scatter_order = (up[::-1], up)
        self.exact = wide == 8 and narrow == 4

    def pairs(self, flip):
        n = self.narrow
        out = []
        for w in range(self.wide):
            for z in range(n):
                to_w, to_z = flip(w, z)
                out.append((w * n + z, to_w * n + to_z))
        return out

    def narrow_pairs(self, k):
        return self.pairs(lambda w, z: (w, z ^ k))

    def step_pairs(self, order, s):
        return self.pairs(lambda w, z: (w ^ (1 << order[w & 1][s]), z))

    def core_pairs(self):
        return self.pairs(lambda w, z: (w ^ 1, z))

    def gathered(self, w):
        out = []
        for other in (0, 1):
            v = w ^ other
            for code in range(self.wide // 2):
                t = v
                for s in range(self.bits - 1):
                    if code >> s & 1:
                        t ^= 1 << self.gather_order[v & 1][s]
                out.append(t)
        return out

    def slots(self, w):
        out = []
        for other in (0, 1):
            v = w ^ other
            for code in range(self.wide // 2):
                t = v
                for s in range(self.bits - 1):
                    if code >> (self.bits - 2 - s) & 1:
                        t ^= 1 << self.scatter_order[v & 1][s]
                out.append(t)
        return out

    def mine(self, table):
        return lax.dynamic_index_in_dim(jnp.asarray(table), lax.axis_index("wide"), 0, keepdims=False)

    def gather(self, shard):
        z = lax.axis_index("narrow")
        parts = [shard] + [lax.ppermute(shard, AXES, self.narrow_pairs(k)) for k in range(1, self.narrow)]
        yield []
        bit = 1
        while bit < self.narrow:
            swap = (z & bit) != 0
            parts = [jnp.where(swap, parts[k ^ bit], parts[k]) for k in range(self.narrow)]
            bit *= 2
        held = [jnp.concatenate(parts, axis=0)]
        got = held
        for s in range(self.bits - 1):
            pairs = self.step_pairs(self.gather_order, s)
            fresh, got = got, [lax.ppermute(h, AXES, pairs) for h in held]
            held = held + got
            yield fresh
        other = [lax.ppermute(h, AXES, self.core_pairs()) for h in held]
        yield got
        held = held + other
        return held if self.exact else [self.join(held)]

    def join(self, pieces):
        inverse = np.stack([np.argsort(self.gathered(w)) for w in range(self.wide)]).astype(np.int32)
        stacked = jnp.stack(pieces)
        return jnp.take(stacked, self.mine(inverse), axis=0).reshape(-1, stacked.shape[-1])

    def scatter(self, keep, send):
        half = self.wide // 2
        if not self.exact:
            slots = np.stack([self.slots(w) for w in range(self.wide)]).astype(np.int32)
            whole = jnp.concatenate([keep, send], axis=0)
            whole = whole.reshape(self.wide, -1, whole.shape[-1])
            whole = jnp.take(whole, self.mine(slots), axis=0)
            keep, send = whole[:half], whole[half:]
        got = lax.ppermute(send, AXES, self.core_pairs())
        yield [send]
        total = keep.astype(f32) + got.astype(f32)
        for s in range(self.bits - 1):
            half //= 2
            away = total[half:].astype(bf16)
            got = lax.ppermute(away, AXES, self.step_pairs(self.scatter_order, s))
            yield [away]
            total = total[:half] + got.astype(f32)
        total = total[0]
        size = total.shape[0] // self.narrow
        z = lax.axis_index("narrow")
        own = lax.dynamic_slice_in_dim(total, z * size, size, axis=0)
        low = total.astype(bf16)
        parts = [lax.dynamic_slice_in_dim(low, (z ^ k) * size, size, axis=0) for k in range(1, self.narrow)]
        got = [lax.ppermute(parts[k - 1], AXES, self.narrow_pairs(k)) for k in range(1, self.narrow)]
        yield parts
        for part in got:
            own = own + part.astype(f32)
        return own

    def sum(self, keep, send):
        blocks = self.wide // 2
        return finish(self.scatter(
            keep.reshape(blocks, -1, keep.shape[-1]), send.reshape(blocks, -1, send.shape[-1])))

    def total(self, value):
        bit = 1
        while bit < self.narrow:
            value = value + lax.ppermute(value, AXES, self.narrow_pairs(bit))
            bit *= 2
        for s in range(self.bits - 1):
            value = value + lax.ppermute(value, AXES, self.pairs(lambda w, z: (w ^ (2 << s), z)))
        return value + lax.ppermute(value, AXES, self.core_pairs())


def natural_halves(keep, send):
    both = jnp.stack([keep, send], axis=1)
    both = both.reshape(2, -1, both.shape[-1])
    return both[0], both[1]


def conv_rows(conv):
    at = LEAD - RADIUS
    tail = CONV_K - at - KSIZE
    both = jnp.stack([conv, conv[:, ::-1]], axis=1)
    return jnp.pad(both.astype(f32), ((0, 0), (0, 0), (at, tail)))


def finish(steps):
    while True:
        try:
            next(steps)
        except StopIteration as end:
            return end.value


def small_outputs(ring, total, size, hidden_size):
    layers = total.shape[0] // (8 + STEPS)
    here = lax.axis_index("wide") * ring.narrow + lax.axis_index("narrow")
    lines = total[: 8 * layers, :D].reshape(layers, 8, D)
    lines = lax.dynamic_slice_in_dim(lines, here * size, size, axis=2)
    inb = total[8 * layers :, :D].reshape(layers, FF)
    inb = lax.dynamic_slice_in_dim(inb, here * hidden_size, hidden_size, axis=1)
    taps = total[:, D : D + KSIZE].reshape(layers, HEADS, KSIZE)
    return lines[:, :6], lines[:, 6:], inb, taps


def small_shard(in_b, bias_rows, gain_rows):
    layers, size = bias_rows.shape[0], bias_rows.shape[2]
    columns = jnp.concatenate([bias_rows, gain_rows], axis=1).transpose(2, 0, 1).reshape(size, 8 * layers)
    inner_bias = in_b.reshape(layers, size, -1).transpose(1, 0, 2).reshape(size, -1)
    small = jnp.concatenate([columns, inner_bias], axis=1)
    return jnp.pad(small, ((0, 0), (0, 128 - small.shape[1])))


def gather_all(ring, attention_shards, in_w, out2_w):
    layers = in_w.shape[0]
    return (
        [finish(ring.gather(shard)) for shard in attention_shards],
        [finish(ring.gather(in_w[layer])) for layer in range(layers)],
        [finish(ring.gather(out2_w[layer])) for layer in range(layers)],
    )


class Plan:
    def __init__(self):
        self.count = 0

    def lanes(self, *lanes):
        self.count += 1
        return (self.count, list(lanes))


def body(ring, tokens, cotangent, qkv_w, out_w, in_w, in_b, out2_w, bias_rows, gain_rows, conv_w):
    layers = qkv_w.shape[0]
    size = qkv_w.shape[1]
    small = small_shard(in_b, bias_rows, gain_rows)
    plan = Plan()
    none = (None, ())
    on = ring.exact and layers == 2
    x = tokens.T.astype(f32)
    conv = [conv_rows(conv_w[layer]) for layer in range(layers)]
    on_attention, on_feed = [none] * layers, [none] * layers
    qkvo = [jnp.concatenate([qkv_w[layer], out_w[layer]], axis=1) for layer in range(layers)]
    if on:
        s1 = Spread(jnp.concatenate([qkvo[0][:, : 2 * D], small], axis=1), 0, 1)
        s2 = Spread(qkvo[0][:, 2 * D :], 1, 3)
        g1, g2 = Gather(s1), Gather(s2)
        s3 = Spread(in_w[0], 3, 8)
        m1 = g1.go(a=(1, 2), b=(2, 4), core0=(1, 8), core1=(2, 8), core2=(4, 8))
        m2 = g2.go(a=(3, 5), b=(5, 7), core0=(3, 8), core1=(5, 8), core2=(7, 8))
        exchange(plan.lanes(s1, s2, *m1, *m2, s3), 9)
        att = [[g1.pieces(), g2.pieces()], None]
        win, wout = [None] * 2, [None] * 2
        g3 = Gather(s3)
        s4, s5 = Spread(out2_w[0], 0, 4), Spread(qkvo[1], 4, 9)
        g4 = Gather(s4)
        m3 = g3.go(a=(0, 2), b=(2, 6), core0=(0, 3), core1=(2, 5), core2=(6, 9))
        m4 = g4.go(a=(4, 6), b=(6, 9), core0=(4, 7), core1=(6, 9), core2=(9, 10))
        on_attention[0] = plan.lanes(s4, *m3, *m4, s5)
    else:
        shards = [jnp.concatenate([qkvo[0], small], axis=1)] + qkvo[1:]
        att, win, wout = gather_all(ring, shards, in_w, out2_w)
        att = [[pieces] for pieces in att]

    kept = []
    par = None
    for layer in range(layers):
        final = layer == layers - 1
        xl, mix, lm, par, ctx, f, b, a, ns, sm, xhat1, rstd1 = attention(
            x, att[layer], par, conv[layer], layer, on_attention[layer])
        if on and layer == 0:
            win[0], wout[0] = g3.pieces(), g4.pieces()
            s6, s7 = Spread(in_w[1], 0, 2), Spread(out2_w[1], 2, 4)
            g5, g6, g7 = Gather(s5), Gather(s6), Gather(s7)
            m5 = g5.go(a=(0, 1), b=(1, 3), core0=(0, 1), core1=(1, 3), core2=(3, 4))
            m6 = g6.go(a=(3, 4))
            on_feed[0] = plan.lanes(*m5, s6, s7, *m6)
        if on and layer == 1:
            win[1], wout[1] = g6.pieces(), g7.pieces()
        at = 8 * layers + FF // D * layer
        inb = par[:, at : at + FF // D].reshape(FF, 1)
        act, slope, xhat2, rstd2, x = feed(
            xhat1, win[layer], wout[layer], par, inb, layer, final, on_feed[layer])
        if on and layer == 0:
            att[1] = [g5.pieces()]
            m6 = g6.go(b=(0, 4), core0=(0, 3), core1=(0, 3), core2=(4, 9))
            m7 = g7.go(a=(0, 2), b=(4, 8), core0=(0, 3), core1=(2, 5), core2=(8, 10))
            on_attention[1] = plan.lanes(*m6, *m7)
        kept.append((xl, mix, lm, ctx, f, b, a, ns, sm, xhat1, rstd1, act, slope, xhat2, rstd2))
    output = x

    dy = cotangent
    sums = jnp.zeros((D, 128), f32)
    taps = [None] * layers
    grads = [{} for _ in range(layers)]
    firsts, thirds, ends = {}, {}, []

    def sum_first(keep, send, turns, layer, place):
        firsts[layer, place] = ReduceFirst(keep, send, turns)
        return firsts[layer, place]

    def sum_third(layer, place, turns):
        thirds[layer, place] = Third(*firsts[layer, place].value, turns)
        return thirds[layer, place]

    def ending(lane, layer, place):
        ends.append((lane, layer, place))
        return lane

    def sum_final(layer, place, turns):
        return ending(Final(*thirds[layer, place].value, turns), layer, place)

    def sum_last(layer, place, turns):
        return ending(ReduceLast(*firsts[layer, place].value, turns), layer, place)

    halves = None
    for layer in reversed(range(layers)):
        xl, mix, lm, ctx, f, b, a, ns, sm, xhat1, rstd1, act, slope, xhat2, rstd2 = kept[layer]
        above = layer + 1 < layers
        lane = none
        if on and above:
            lane = plan.lanes(sum_first(*halves, (0, 1, 4), layer + 1, "qk"), sum_last(layer + 1, "ov", (0, 1, 4)))
        keep, send, du, dr2, sums = hidden(
            sums, dy, xhat2, rstd2, par, act, slope, wout[layer], layer, not above, lane)
        if on:
            lane = [sum_first(keep.reshape(-1, D), send.reshape(-1, D), (0, 1, 4), layer, "out2")]
            lane += [sum_last(layer + 1, "qk", (0, 1, 4))] if above else []
            lane = plan.lanes(*lane)
        else:
            grads[layer]["out2"] = ring.sum(*natural_halves(keep, send))
        keep, send, dr1, sums = inner(sums, du, dr2, xhat1, rstd1, par, win[layer], layer, lane)
        if on:
            lane = plan.lanes(sum_third(layer, "out2", (0, 1)), sum_first(keep, send, (0, 1, 4), layer, "in"))
        else:
            grads[layer]["in"] = ring.sum(keep, send)
        keep, send, dctx, dv, dz, dbv, taps[layer], sums = values(
            sums, dr1, mix, ctx, f, b, xl, sm, conv[layer], att[layer], layer, lane)
        tail = []
        if on:
            lane = [sum_final(layer, "out2", (0, 2)), sum_last(layer, "in", (0, 1, 6))]
            if layer:
                lane.append(sum_first(keep, send, (0, 1, 3), layer, "ov"))
            else:
                lead = ReduceFirst(keep, send, (0, 1, 3), chained=True)
                lane += [lead, ending(ReduceLast(None, None, (3, 4, 10), inside=lead), 0, "ov")]
                for part, (go, end) in enumerate((((4, 5, 7), (7, 9, 12)), ((6, 7, 9), (9, 11, 13)))):
                    lead = ReduceFirst(None, None, go, chained=True, columns=slice(part * D, (part + 1) * D))
                    tail.append(lead)
                    lane += [lead, ending(ReduceLast(None, None, end, inside=lead), 0, f"qk{part}")]
                total = Total(taps, (7, 8, 9, 10, 11, 12))
                tail.append(total)
                lane.append(total)
            lane = plan.lanes(*lane)
        else:
            grads[layer]["ov"] = ring.sum(keep, send)
        keep, send, dy, sums = back(
            sums, ns, mix, dctx, f, b, dv, xl, dr1, lm, a, sm, dz, dbv, att[layer], layer, lane, tuple(tail), on)
        halves = (keep, send)
        if not on:
            grads[layer]["qk"] = ring.sum(keep, send)
    if on:
        for lane, layer, place in ends:
            grads[layer][place] = lane.value
        grads[0]["qk"] = jnp.concatenate([grads[0]["qk0"], grads[0]["qk1"]], axis=1)
        total = total.value
    else:
        flat = jnp.concatenate([sums.T[:SMALL], jnp.concatenate(taps, axis=0)], axis=1)
        total = ring.total(flat)
    gbias, ggain, ginb, gtaps = small_outputs(ring, total, size, in_b.shape[1])
    half = D // 2
    stacked = [
        jnp.stack([
            jnp.concatenate([
                g["qk"][:, :half], g["qk"][:, D : D + half], g["qk"][:, half:D], g["qk"][:, D + half :],
                g["ov"][:, D:]], axis=1) for g in grads]),
        jnp.stack([g["ov"][:, :D] for g in grads]),
        jnp.stack([g["in"] for g in grads]),
        jnp.stack([g["out2"] for g in grads])]
    return (output, dy, stacked[0], stacked[1], stacked[2], ginb, stacked[3], gbias, ggain, gtaps)


def solution(mesh):
    ring = Ring(mesh.shape["wide"], mesh.shape["narrow"])
    rows3 = P(None, AXES, None)
    columns3 = P(None, None, AXES)
    weights = (rows3, rows3, rows3, P(None, AXES), rows3, columns3, columns3, P())
    return jax.shard_map(
        functools.partial(body, ring),
        mesh=mesh,
        in_specs=(P(AXES, None), P(AXES, None)) + weights,
        out_specs=(P(AXES, None), P(AXES, None)) + weights,
        check_vma=False,
    )
```

```python
import functools
import jax
import jax.numpy as jnp
import numpy as np
from jax import lax
from jax.experimental import pallas as pl
from jax.experimental.pallas import tpu as pltpu
from jax.sharding import PartitionSpec as P

D = 768
HEADS = 12
HD = 64
FF = 3072
LM = 64
KSIZE = 33
RADIUS = KSIZE // 2
NS_ITERS = 6
T = 1024
SEG = T // LM
SCALE = HD ** -0.5
EPS = 1e-05
CONV_N = 256
CONV_K = 512
CONV_BLOCKS = T // CONV_N
LEAD = 128
f32 = jnp.float32
bf16 = jnp.bfloat16
AXES = ("wide", "narrow")
NN = (((1,), (0,)), ((), ()))
NT = (((1,), (1,)), ((), ()))
TN = (((0,), (0,)), ((), ()))
VMEM_LIMIT = 60 * 1024 * 1024


def dot(a, b, dims):
    return lax.dot_general(a, b, dims, preferred_element_type=f32)


def split(a):
    high = a.astype(bf16)
    return high, (a - high.astype(f32)).astype(bf16)


def dot3(a, b, dims):
    return dot(a[0], b[0], dims) + (dot(a[0], b[1], dims) + dot(a[1], b[0], dims))


def rows(start, size):
    if isinstance(start, int):
        return pl.ds(start, size)
    return pl.ds(pl.multiple_of(start, size), size)


def segment_mean():
    token = lax.broadcasted_iota(jnp.int32, (T, LM), 0)
    seg = lax.broadcasted_iota(jnp.int32, (T, LM), 1)
    return jnp.where(token // SEG == seg, 1.0 / SEG, 0.0).astype(bf16)


def segment_spread():
    token = lax.broadcasted_iota(jnp.int32, (LM, T), 1)
    seg = lax.broadcasted_iota(jnp.int32, (LM, T), 0)
    return jnp.where(token // SEG == seg, 1.0, 0.0).astype(bf16)


def eye(value):
    i = lax.broadcasted_iota(jnp.int32, (LM, LM), 0)
    j = lax.broadcasted_iota(jnp.int32, (LM, LM), 1)
    return jnp.where(i == j, value, 0.0).astype(f32)


def toeplitz(row):
    full = jnp.broadcast_to(row, (CONV_N, CONV_K))
    return pltpu.roll(full, 0, 1, stride=1, stride_axis=0).astype(bf16)


def windows(ref, base):
    return jnp.concatenate(
        [ref[rows(base, HD), CONV_N * b : CONV_N * b + CONV_K] for b in range(CONV_BLOCKS)], axis=0
    )


def stack_blocks(value):
    return jnp.concatenate(
        [value[:, CONV_N * b : CONV_N * (b + 1)] for b in range(CONV_BLOCKS)], axis=0
    )


def unstack_blocks(value):
    return jnp.concatenate(
        [value[HD * b : HD * (b + 1), :] for b in range(CONV_BLOCKS)], axis=1
    )


def norm_forward(r_ref, xhat_ref, rstd_ref, width=128):
    for c in range(0, T, width):
        r = r_ref[:, c : c + width]
        center = r - jnp.mean(r, axis=0, keepdims=True)
        rstd = lax.rsqrt(jnp.mean(center * center, axis=0, keepdims=True) + EPS)
        xhat_ref[:, c : c + width] = center * rstd
        rstd_ref[:, c : c + width] = jnp.broadcast_to(rstd, (8, width))


def vm():
    return pl.BlockSpec(memory_space=pltpu.VMEM)


def anywhere(n):
    return [pl.BlockSpec(memory_space=pl.ANY)] * n


def whole(*s):
    return pl.BlockSpec(s, lambda *_: (0,) * len(s))


def sd(*s, t=f32):
    return jax.ShapeDtypeStruct(s, t)


def loader(pieces, dst, sem, columns=None):
    r = pieces[0].shape[0]
    order = Order(len(pieces))
    out = []
    for i, piece in enumerate(pieces):
        src = piece if columns is None else piece.at[:, pl.ds(*columns)]
        at = rows(order.target(i) * r, r)
        out.append(pltpu.make_async_copy(src, dst.at[at, :], sem.at[i]))
    return out


def sizes_of(groups, layer):
    return [(len(g), g[0].shape[1] - (128 if layer == 0 and i == 0 else 0)) for i, g in enumerate(groups)]


def grouped(refs, sizes):
    groups = []
    for n, _ in sizes:
        groups.append(refs[:n])
        refs = refs[n:]
    return groups, refs


def column_loader(groups, sizes, dst, sem, low, high):
    out = []
    at = 0
    for g, (n, width) in enumerate(sizes):
        a, b = max(low, at), min(high, at + width)
        if b > a:
            out += loader(groups[g], dst.at[:, pl.ds(a - low, b - a)], sem.at[g], (a - at, b - a))
        at += width
    return out


def call(kernel, name, out_shape, in_specs, out_specs, scratch, args, lanes, flops, size, grid=None, trans=0):
    identity, lanes = lanes
    ins, outs = len(args), len(out_shape)
    lane_args = [a for lane in lanes for a in lane.args]
    lane_outs = [o for lane in lanes for o in lane.outs]
    lane_scratch = [o for lane in lanes for o in lane.scratch]

    def run(*refs):
        refs = list(refs)

        def take(n):
            got = refs[:n]
            del refs[:n]
            return got

        own = take(ins)
        lane_in = [take(len(lane.args)) for lane in lanes]
        own += take(outs)
        lane_out = [take(len(lane.outs)) for lane in lanes]
        own += take(len(scratch))
        for lane, a, o in zip(lanes, lane_in, lane_out):
            lane.bind(a, o, take(len(lane.scratch)))

        def hook(i):
            if lanes and i == 0:
                near = Near()
                names = sorted({p for lane in lanes for p in lane.partners})
                barrier = pltpu.get_barrier_semaphore()
                for p in names:
                    pl.semaphore_signal(barrier, inc=1, device_id=near.at(p), device_id_type=pl.DeviceIdType.MESH)
                pl.semaphore_wait(barrier, len(names))
            for lane in lanes:
                lane.turn(i)

        kernel(*own, hook=hook)

    params = {"collective_id": identity, "has_side_effects": True} if lanes else {}
    got = pl.pallas_call(
        run,
        out_shape=list(out_shape) + [o for o, _ in lane_outs],
        in_specs=list(in_specs) + [spec for lane in lanes for spec in lane.specs],
        out_specs=list(out_specs) + [spec for _, spec in lane_outs],
        scratch_shapes=list(scratch) + lane_scratch,
        **({} if grid is None else {"grid": grid}),
        compiler_params=pltpu.CompilerParams(vmem_limit_bytes=VMEM_LIMIT, **params),
        cost_estimate=pl.CostEstimate(flops=flops, bytes_accessed=size, transcendentals=trans),
        name=name,
    )(*args, *lane_args)
    own, rest = list(got[:outs]), list(got[outs:])
    for lane in lanes:
        n = len(lane.outs)
        lane.done(rest[:n])
        rest = rest[n:]
    return own


class Near:
    def __init__(self):
        self.w, self.z = lax.axis_index("wide"), lax.axis_index("narrow")

    def over(self, k):
        z = self.z
        if k == 1:
            return z + 1 - 2 * (z % 2)
        if k == 2:
            return z + 2 - 4 * (z // 2)
        return 3 - z

    def at(self, name):
        w, core = self.w, self.w % 2
        if name[0] == "z":
            return (w, self.over(int(name[1])))
        if name == "core":
            return (w + 1 - 2 * core, self.z)
        step = {"a": 2 + 2 * core, "b": 4 - 2 * core, "x": 2, "y": 4}[name]
        return (w + step - 2 * step * ((w // step) % 2), self.z)


def remote(src, dst, send, recv, name):
    return pltpu.make_async_remote_copy(
        src_ref=src, dst_ref=dst, send_sem=send, recv_sem=recv, device_id=Near().at(name),
        device_id_type=pl.DeviceIdType.MESH)


DMA = pltpu.SemaphoreType.DMA
ANY = pl.BlockSpec(memory_space=pl.ANY)


class Move:
    def __init__(self, source, name, start, wait):
        self.chained = not hasattr(source, "dtype")
        self.source, self.name, self.start, self.wait = source, name, start, wait
        self.shape = source.shape
        self.args = [] if self.chained else [source]
        self.specs = [ANY] * len(self.args)
        self.outs = [(sd(*self.shape, t=bf16), ANY)]
        self.scratch = [DMA((2,))]
        self.partners = [name]

    def bind(self, args, outs, scratch):
        self.src = self.source.dst if self.chained else args[0]
        self.dst, self.sem = outs[0], scratch[0]

    def copy(self):
        return remote(self.src, self.dst, self.sem.at[0], self.sem.at[1], self.name)

    def turn(self, i):
        if i == self.wait:
            self.copy().wait()
        if i == self.start:
            self.copy().start()

    def done(self, got):
        self.value = got[0].reshape(-1, self.shape[-1])


class Spread:
    def __init__(self, shard, start, wait):
        self.start, self.wait = start, wait
        self.shape = (4, *shard.shape)
        self.args, self.specs = [shard], [ANY]
        self.outs = [(sd(*self.shape, t=bf16), ANY)]
        self.scratch = [DMA((7,))]
        self.partners = ["z1", "z2", "z3"]

    def bind(self, args, outs, scratch):
        self.src, self.dst, self.sem = args[0], outs[0], scratch[0]

    def copies(self):
        z = lax.axis_index("narrow")
        out = [pltpu.make_async_copy(self.src, self.dst.at[z], self.sem.at[6])]
        for k in (1, 2, 3):
            out.append(remote(self.src, self.dst.at[z], self.sem.at[2 * k - 2], self.sem.at[2 * k - 1], f"z{k}"))
        return out

    def turn(self, i):
        if i == self.wait:
            for copy in self.copies():
                copy.wait()
        if i == self.start:
            for copy in self.copies():
                copy.start()

    def done(self, got):
        self.value = got[0].reshape(-1, self.shape[-1])


class Gather:
    def __init__(self, block):
        self.block, self.moves = block, {}

    def at(self, name):
        if name == "own":
            return self.block
        return self.moves[name]

    def go(self, apart=0, **turns):
        out = []
        fresh = {}
        value = lambda k: fresh[k] if k in fresh else (
            self.moves[k].value if k in self.moves else
            self.block.value if hasattr(self.block, "value") else self.block)
        for key, turn in turns.items():
            if key == "a":
                todo = [("a", "own", "a")]
            elif key == "b":
                todo = [("b0", "own", "b"), ("b1", "a", "b")]
            else:
                todo = {"core0": [("c0", "own", "core")], "core1": [("c1", "a", "core")],
                        "core2": [("c2", "b0", "core"), ("c3", "b1", "core")]}[key]
            for name, source, partner in todo:
                start, wait = turn
                if name == "b1":
                    wait += apart
                if name == "c3":
                    start += apart
                fresh[name] = Move(value(source), partner, start, wait)
                out.append(fresh[name])
        self.moves.update(fresh)
        return sorted(out, key=lambda m: m.start)

    def pieces(self):
        block = self.block.value if hasattr(self.block, "value") else self.block
        return [block] + [self.moves[k].value for k in ("a", "b0", "b1", "c0", "c1", "c2", "c3")]


def strips(columns):
    width = 384 if columns % 384 == 0 else 512 if columns % 512 == 0 else columns
    return [slice(c, c + width) for c in range(0, columns, width)]


class ReduceFirst:
    def __init__(self, keep, send, turns, chained=False, columns=None):
        self.turns, self.chained, self.at = turns, chained, columns
        rows4 = D // 2 if columns is not None else send.shape[0]
        self.columns = columns.stop - columns.start if columns is not None else send.shape[1]
        self.r = r = rows4 // 4
        self.partners = ["core", "b"]
        shape = (r, self.columns)
        self.args = [] if columns is not None else [keep, send]
        self.specs = [ANY] * len(self.args)
        self.outs = [] if chained else [(sd(*shape, t=bf16), whole(*shape)), (sd(*shape), whole(*shape))]
        self.scratch = [pltpu.VMEM((2 * r, self.columns), bf16), pltpu.VMEM((2 * r, self.columns), bf16),
                        pltpu.VMEM((4 * r, self.columns), bf16), DMA((7,))]
        if chained:
            self.scratch += [pltpu.VMEM(shape, bf16), pltpu.VMEM(shape, f32)]
        if columns is None:
            self.scratch += [pltpu.VMEM((4 * r, self.columns), bf16)]

    def bind(self, args, outs, scratch):
        self.away1, self.got1, self.got0, self.sem = scratch[:4]
        rest = scratch[4:]
        if self.chained:
            self.away2, self.own2 = rest[:2]
            rest = rest[2:]
        else:
            self.away2, self.own2 = outs
        if self.at is None:
            self.keep_from, self.send = args
            self.keep = rest[0]

    def use(self, keep, send, sums):
        self.keep, self.send = keep.at[:, self.at], send.at[:, self.at]

    def load(self):
        return pltpu.make_async_copy(self.keep_from, self.keep, self.sem.at[4])

    def first(self, half):
        at = pl.ds(2 * self.r * half, 2 * self.r)
        k = 5 if half == 0 else 0
        return remote(self.send.at[at, :], self.got0.at[at, :], self.sem.at[k], self.sem.at[k + 1], "core")

    def second(self):
        return remote(self.away1, self.got1, self.sem.at[2], self.sem.at[3], "b")

    def turn(self, i):
        r = self.r
        if i == self.turns[0]:
            self.first(1).start()
            if self.at is None:
                self.load().start()
            self.first(0).start()
        if i == self.turns[1]:
            if self.at is None:
                self.load().wait()
            self.first(1).wait()
            for at in strips(self.columns):
                self.away1[:, at] = self.keep[2 * r :, at] + self.got0[2 * r :, at]
            self.second().start()
        if i == self.turns[2]:
            self.first(0).wait()
            self.second().wait()
            for at in strips(self.columns):
                for k, out in ((0, self.own2), (1, self.away2)):
                    block = slice(k * r, (k + 1) * r)
                    value = self.keep[block, at].astype(f32) + self.got0[block, at].astype(f32)
                    out[:, at] = (value + self.got1[block, at].astype(f32)).astype(out.dtype)

    def done(self, got):
        self.value = got


class ReduceLast:
    def __init__(self, away, own, turns, inside=None):
        self.turns, self.inside = turns, inside
        r, columns = (inside.r, inside.columns) if inside else away.shape
        size = r // 4
        self.r, self.columns, self.size = r, columns, size
        self.partners = ["a", "z1", "z2", "z3"]
        self.args = [] if inside else [away, own]
        self.specs = [] if inside else [ANY, whole(r, columns)]
        self.outs = [(sd(size, columns), whole(size, columns))]
        self.scratch = [pltpu.VMEM((r, columns), bf16), pltpu.VMEM((4, size, columns), bf16),
                        pltpu.VMEM((4, size, columns), bf16), pltpu.VMEM((4, size, columns), f32), DMA((8,))]

    def bind(self, args, outs, scratch):
        self.got2, self.parts, self.got3, self.sums, self.sem = scratch
        self.out = outs[0]
        self.away, self.own = (self.inside.away2, self.inside.own2) if self.inside else args

    def third(self):
        return remote(self.away, self.got2, self.sem.at[0], self.sem.at[1], "a")

    def last(self):
        near = Near()
        return [
            remote(self.parts.at[near.over(k)], self.got3.at[near.z], self.sem.at[2 * k], self.sem.at[2 * k + 1], f"z{k}")
            for k in (1, 2, 3)]

    def turn(self, i):
        if i == self.turns[0]:
            self.third().start()
        if i == self.turns[1]:
            self.third().wait()
            for at in strips(self.columns):
                value = self.own[:, at] + self.got2[:, at].astype(f32)
                for k in range(4):
                    block = value[k * self.size : (k + 1) * self.size]
                    self.sums[k, :, at] = block
                    self.parts[k, :, at] = block.astype(bf16)
            for copy in self.last():
                copy.start()
        if i == self.turns[2]:
            for copy in self.last():
                copy.wait()
            near = Near()
            for at in strips(self.columns):
                value = self.sums[near.z, :, at]
                for k in (1, 2, 3):
                    value = value + self.got3[near.over(k), :, at].astype(f32)
                self.out[:, at] = value

    def done(self, got):
        self.value = got[0]


class Core:
    def __init__(self, keep, send, turns):
        self.turns = turns
        r, columns = send.shape[0] // 2, send.shape[1]
        self.r, self.columns = r, columns
        self.partners = ["core"]
        self.args, self.specs = [keep, send], [ANY, ANY]
        self.outs = [(sd(r, columns, t=bf16), whole(r, columns))] * 2
        self.scratch = [pltpu.VMEM((2 * r, columns), bf16), pltpu.VMEM((2 * r, columns), bf16), DMA((3,))]

    def bind(self, args, outs, scratch):
        self.keep_from, self.send = args
        self.away, self.own = outs
        self.keep, self.got, self.sem = scratch

    def copies(self):
        return [pltpu.make_async_copy(self.keep_from, self.keep, self.sem.at[2]),
                remote(self.send, self.got, self.sem.at[0], self.sem.at[1], "core")]

    def turn(self, i):
        if i == self.turns[0]:
            for copy in self.copies():
                copy.start()
        if i == self.turns[1]:
            for copy in self.copies():
                copy.wait()
            for at in strips(self.columns):
                self.away[:, at] = self.keep[self.r :, at] + self.got[self.r :, at]
                self.own[:, at] = self.keep[: self.r, at] + self.got[: self.r, at]

    def done(self, got):
        self.value = got


class Plane:
    def __init__(self, away, own, turns, chained=False):
        self.turns, self.chained = turns, chained
        rows2, self.columns = away.shape
        self.r = rows2 // 2
        shape = (self.r, self.columns)
        self.partners = ["b"]
        self.args, self.specs = [away, own], [ANY, whole(rows2, self.columns)]
        self.outs = [] if chained else [(sd(*shape, t=bf16), whole(*shape)), (sd(*shape), whole(*shape))]
        self.scratch = [pltpu.VMEM((rows2, self.columns), bf16), DMA((2,))]
        if chained:
            self.scratch += [pltpu.VMEM(shape, bf16), pltpu.VMEM(shape, f32)]

    def bind(self, args, outs, scratch):
        self.away1, self.own1 = args
        self.got, self.sem = scratch[:2]
        self.away2, self.own2 = scratch[2:] if self.chained else outs

    def copy(self):
        return remote(self.away1, self.got, self.sem.at[0], self.sem.at[1], "b")

    def turn(self, i):
        r = self.r
        if i == self.turns[0]:
            self.copy().start()
        if i == self.turns[1]:
            self.copy().wait()
            for at in strips(self.columns):
                for block, out in ((slice(0, r), self.own2), (slice(r, 2 * r), self.away2)):
                    value = self.own1[block, at].astype(f32) + self.got[block, at].astype(f32)
                    out[:, at] = value.astype(out.dtype)

    def done(self, got):
        self.value = got


class Third:
    def __init__(self, away, own, turns, inside=None):
        self.turns, self.inside = turns, inside
        r, columns = (inside.r, inside.columns) if inside else away.shape
        self.columns, self.size = columns, r // 4
        self.partners = ["a"]
        self.args = [] if inside else [away, own]
        self.specs = [] if inside else [ANY, whole(r, columns)]
        shape = (4, self.size, columns)
        self.outs = [(sd(*shape, t=bf16), whole(*shape)), (sd(*shape), whole(*shape))]
        self.scratch = [pltpu.VMEM((r, columns), bf16), DMA((2,))]

    def bind(self, args, outs, scratch):
        self.away, self.own = (self.inside.away2, self.inside.own2) if self.inside else args
        self.parts, self.sums = outs
        self.got, self.sem = scratch

    def copy(self):
        return remote(self.away, self.got, self.sem.at[0], self.sem.at[1], "a")

    def turn(self, i):
        if i == self.turns[0]:
            self.copy().start()
        if i == self.turns[1]:
            self.copy().wait()
            for at in strips(self.columns):
                value = self.own[:, at] + self.got[:, at].astype(f32)
                for k in range(4):
                    block = value[k * self.size : (k + 1) * self.size]
                    self.sums[k, :, at] = block
                    self.parts[k, :, at] = block.astype(bf16)

    def done(self, got):
        self.value = got


class Final:
    def __init__(self, parts, sums, turns):
        self.turns = turns
        _, self.size, self.columns = shape = parts.shape
        self.partners = ["z1", "z2", "z3"]
        self.args, self.specs = [parts, sums], [ANY, whole(*shape)]
        self.outs = [(sd(*shape[1:]), whole(*shape[1:]))]
        self.scratch = [pltpu.VMEM(shape, bf16), DMA((8,))]

    def bind(self, args, outs, scratch):
        self.parts, self.sums = args
        self.out = outs[0]
        self.got, self.sem = scratch

    def copies(self):
        near = Near()
        return [
            remote(self.parts.at[near.over(k)], self.got.at[near.z], self.sem.at[2 * k], self.sem.at[2 * k + 1], f"z{k}")
            for k in (1, 2, 3)]

    def turn(self, i):
        if i == self.turns[0]:
            for copy in self.copies():
                copy.start()
        if i == self.turns[1]:
            for copy in self.copies():
                copy.wait()
            near = Near()
            for at in strips(self.columns):
                value = self.sums[near.z, :, at]
                for k in (1, 2, 3):
                    value = value + self.got[near.over(k), :, at].astype(f32)
                self.out[:, at] = value

    def done(self, got):
        self.value = got[0]


SMALL = 24


class Total:
    def __init__(self, packed, turns):
        self.turns = turns
        self.args, self.specs = [packed], [whole(*packed.shape)]
        shape = packed.shape
        self.outs = [(sd(*shape), whole(*shape))]
        self.scratch = [pltpu.VMEM((5, *shape), f32), pltpu.VMEM((5, *shape), f32), DMA((10,))]
        self.partners = ["core", "x", "y", "z1", "z2"]

    def bind(self, args, outs, scratch):
        self.packed, self.out = args[0], outs[0]
        self.held, self.got, self.sem = scratch

    def use(self, keep, send, sums):
        self.sums = sums

    def copy(self, s):
        return remote(self.held.at[s], self.got.at[s], self.sem.at[2 * s], self.sem.at[2 * s + 1], self.partners[s])

    def turn(self, i):
        for s in range(6):
            if i == self.turns[s]:
                if s:
                    self.copy(s - 1).wait()
                    value = self.held[s - 1] + self.got[s - 1]
                    if s < 5:
                        self.held[s] = value
                    else:
                        self.out[...] = value
                else:
                    self.held[0, :, 0:D] = self.sums[...].T[0:SMALL, :]
                    self.held[0, :, D:] = self.packed[:, D:]
                if s < 5:
                    self.copy(s).start()

    def done(self, got):
        self.value = got[0]


CHUNK = 768
STEPS = FF // CHUNK
SUB = 768


def flip(t, stride):
    return t + stride - 2 * stride * ((t // stride) % 2)


class Order:
    def __init__(self, n):
        self.exact = n == 8
        self.core = 0
        if self.exact:
            self.w = lax.axis_index("wide")
            self.core = self.w % 2

    def target(self, i):
        if not self.exact:
            return i
        other, code = i // 4, i % 4
        t = self.w + other * (1 - 2 * self.core)
        core = t % 2
        if code % 2:
            t = flip(t, 2 + 2 * core)
        if code // 2:
            t = flip(t, 4 - 2 * core)
        return t

    def slot(self, j, other):
        if not self.exact:
            return j
        plane = self.w // 2
        core = self.core if other == 0 else 1 - self.core
        dx, dy = (j + plane) % 2, (j // 2 + plane // 2) % 2
        return dx * (1 + core) + dy * (2 - core)


def exchange(lanes, turns):
    def kernel(hook):
        for i in range(turns):
            hook(i)

    call(kernel, "exchange", [], [], [], [], (), lanes, 0, 10_000_000)


def attention_kernel(sizes, p, x_ref, *rest, hook):
    if p:
        par_ref, *rest = rest
    conv_ref, *rest = rest
    groups, rest = grouped(rest, sizes)
    xl_out, mix_out, lm_ref, *rest = rest
    if not p:
        par_ref, *rest = rest
    (ctx_out, f_out, b_out, a_ref, ns_out, small_ref, xhat_ref, rstd_ref,
     w_ref, vpad_ref, z_ref, sem, xl_ref, mix_ref, ctx_ref, f_ref, b_ref, ns_ref, out_sem, ns_sem, *rest) = rest
    leaving = []

    def leave(src, dst):
        copy = pltpu.make_async_copy(src, dst, out_sem.at[len(leaving)])
        copy.start()
        leaving.append(copy)

    loads = column_loader(groups, sizes, w_ref, sem, 0, 4 * D)
    if not p:
        low_ref, low_sem = rest
        loads += loader(groups[0], low_ref, low_sem, (sizes[0][1], 128))
    for copy in loads:
        copy.start()
    xl_ref[...] = x_ref[...].astype(bf16)
    leave(xl_ref, xl_out)
    vpad_ref[:, 0:LEAD] = jnp.zeros((D, LEAD), bf16)
    vpad_ref[:, LEAD + T :] = jnp.zeros((D, LEAD), bf16)
    hook(0)
    for copy in loads:
        copy.wait()
    if not p:
        par_ref[...] = low_ref[...].astype(f32)
    for part, column in ((0, p), (1, None), (2, p + 1)):

        def mix_step(i, _):
            at = rows(part * D + i * 384, 384)
            got = dot(w_ref[:, at], xl_ref[...], TN)
            if column is not None:
                got = got + par_ref[rows(i * 384, 384), column : column + 1]
            mix_ref[at, :] = got.astype(bf16)
            return 0

        lax.fori_loop(0, 2, mix_step, 0)
        leave(mix_ref.at[pl.ds(part * D, D), :], mix_out.at[pl.ds(part * D, D), :])
        hook(part + 1)
    vpad_ref[:, LEAD : LEAD + T] = mix_ref[2 * D :, :]
    lm_ref[...] = dot(mix_ref[0 : 2 * D, :], segment_mean(), NN).astype(bf16)

    for h in range(HEADS):
        ql = lm_ref[h * HD : (h + 1) * HD, :]
        kl = lm_ref[D + h * HD : D + (h + 1) * HD, :]
        s = dot(ql, kl, TN) * SCALE
        e = jnp.exp(s - jnp.max(s, axis=1, keepdims=True))
        a = e / jnp.sum(e, axis=1, keepdims=True)
        a_ref[h] = a
        z_ref[h] = a.T / jnp.sum(a * a)

    def ns_step(k, _):
        ps, rs = [], []
        for h in range(HEADS):
            z = z_ref[h]
            ns_ref[k, 0, h] = z
            p = dot3(split(a_ref[h]), split(z), NN)
            ns_ref[k, 1, h] = p
            ps.append(split(p))
            rs.append(split(eye(7.0) - p))
        for h in range(HEADS):
            r2 = eye(15.0) - dot3(ps[h], rs[h], NN)
            ns_ref[k, 2, h] = r2
            rs[h] = split(r2)
        for h in range(HEADS):
            r3 = eye(13.0) - dot3(ps[h], rs[h], NN)
            ns_ref[k, 3, h] = r3
            rs[h] = split(r3)
        for h in range(HEADS):
            z_ref[h] = 0.25 * dot3(split(z_ref[h]), rs[h], NN)
        pltpu.make_async_copy(ns_ref.at[k], ns_out.at[k], ns_sem.at[k]).start()
        return 0

    lax.fori_loop(0, NS_ITERS // 2, ns_step, 0)
    hook(4)
    lax.fori_loop(NS_ITERS // 2, NS_ITERS, ns_step, 0)
    hook(5)

    def head_step(h, _):
        base = h * HD
        q = mix_ref[rows(base, HD), :]
        k = mix_ref[rows(D + base, HD), :]
        v = mix_ref[rows(2 * D + base, HD), :]
        ql = lm_ref[rows(base, HD), :]
        kl = lm_ref[rows(D + base, HD), :]
        s = dot(kl, q, TN) * SCALE
        e = jnp.exp(s - jnp.max(s, axis=0, keepdims=True))
        f = (e / jnp.sum(e, axis=0, keepdims=True)).astype(bf16)
        f_ref[rows(base, HD), :] = f
        s = dot(ql, k, TN) * SCALE
        e = jnp.exp(s - jnp.max(s, axis=1, keepdims=True))
        b = (e / jnp.sum(e, axis=1, keepdims=True)).astype(bf16)
        b_ref[rows(base, HD), :] = b
        bv = dot(b, v, NT)
        z = z_ref[h]
        w = dot3(split(z), split(bv), NN)
        small_ref[0, h] = z
        small_ref[1, h] = bv
        small_ref[2, h] = w
        attended = dot(w.astype(bf16), f, TN)
        conv = dot(windows(vpad_ref, base), toeplitz(conv_ref[h, 0:1]), NT)
        ctx_ref[rows(base, HD), :] = (attended + unstack_blocks(conv)).astype(bf16)
        return 0

    for third in range(3):
        lax.fori_loop(third * 4, third * 4 + 4, head_step, 0, unroll=4)
        at = pl.ds(third * 4 * HD, 4 * HD)
        for src, dst in ((f_ref, f_out), (b_ref, b_out), (ctx_ref, ctx_out)):
            leave(src.at[at, :], dst.at[at, :])
        hook(6 + third)

    def out_step(i, _):
        at = rows(i * 384, 384)
        got = dot(w_ref[:, rows(3 * D + i * 384, 384)], ctx_ref[...], TN)
        xhat_ref[at, :] = got + par_ref[at, p + 2 : p + 3] + x_ref[at, :]
        return 0

    lax.fori_loop(0, 2, out_step, 0)
    norm_forward(xhat_ref, xhat_ref, rstd_ref)
    for copy in leaving:
        copy.wait()
    for k in range(NS_ITERS):
        pltpu.make_async_copy(ns_ref.at[k], ns_out.at[k], ns_sem.at[k]).wait()
    for i in range(9, 13):
        hook(i)


def attention(x, groups, par, conv, layer, lanes=(None, ())):
    first = layer == 0
    sizes = sizes_of(groups, layer)
    n = sizes[0][0]
    got = call(
        functools.partial(attention_kernel, sizes, 8 * layer), "attention",
        [sd(D, T, t=bf16), sd(3 * D, T, t=bf16), sd(2 * D, LM, t=bf16)] + [sd(D, 128)] * first
        + [
            sd(D, T, t=bf16), sd(D, T, t=bf16), sd(D, T, t=bf16), sd(HEADS, LM, LM),
            sd(NS_ITERS, 4, HEADS, LM, LM), sd(3, HEADS, LM, LM), sd(D, T), sd(8, T),
        ],
        [vm()] * (2 if first else 3) + anywhere(n * len(groups)),
        [ANY, ANY, vm()] + [vm()] * first + [ANY, ANY, ANY, vm(), ANY, vm(), vm(), vm()],
        [
            pltpu.VMEM((D, 4 * D), bf16), pltpu.VMEM((D, T + 2 * LEAD), bf16), pltpu.VMEM((HEADS, LM, LM), f32),
            DMA((len(groups), n)), pltpu.VMEM((D, T), bf16), pltpu.VMEM((3 * D, T), bf16), pltpu.VMEM((D, T), bf16),
            pltpu.VMEM((D, T), bf16), pltpu.VMEM((D, T), bf16), pltpu.VMEM((NS_ITERS, 4, HEADS, LM, LM), f32),
            DMA((16,)), DMA((NS_ITERS,)),
        ] + [pltpu.VMEM((D, 128), bf16), DMA((n,))] * first,
        (x, *([] if first else [par]), conv, *[piece for g in groups for piece in g]), lanes,
        6_800_000_000, 40_000_000, trans=2_000_000)
    return got if first else [*got[:3], par, *got[3:]]


def feed_kernel(n, p, last, xhat_ref, par_ref, inb_ref, *rest, hook):
    pieces1, pieces2, rest = rest[:n], rest[n : 2 * n], rest[2 * n :]
    a_ref, g_ref, xhat2_ref, rstd2_ref, next_ref, w1_ref, w2_ref, hl_ref, sem = rest
    j = pl.program_id(0)

    @pl.when(j == 0)
    def _():
        loads = loader(pieces1, w1_ref, sem.at[0])
        for copy in loads:
            copy.start()
        later = loader(pieces2, w2_ref, sem.at[1])
        for copy in later:
            copy.start()
        hook(0)
        h = xhat_ref[...] * par_ref[:, p + 6 : p + 7] + par_ref[:, p + 3 : p + 4]
        hl_ref[...] = h.astype(bf16)
        xhat2_ref[...] = h + par_ref[:, p + 4 : p + 5]
        for copy in loads + later:
            copy.wait()

    u = dot(w1_ref[:, rows(j * CHUNK, CHUNK)], hl_ref[...], TN)
    u = u + inb_ref[rows(j * CHUNK, CHUNK), 0:1]
    cdf = 0.5 + 0.5 * lax.erf(u * (2.0 ** -0.5))
    pdf = jnp.exp(-0.5 * u * u) * ((2.0 * np.pi) ** -0.5)
    a_ref[...] = (u * cdf).astype(bf16)
    g_ref[...] = (cdf + u * pdf).astype(bf16)
    xhat2_ref[...] += dot(w2_ref[rows(j * CHUNK, CHUNK), :], a_ref[...], TN)

    @pl.when(j == STEPS - 1)
    def _():
        norm_forward(xhat2_ref, xhat2_ref, rstd2_ref)
        y = xhat2_ref[...] * par_ref[:, p + 7 : p + 8] + par_ref[:, p + 5 : p + 6]
        if last:
            next_ref[...] = y.T.astype(bf16)
        else:
            next_ref[...] = y

    for i in range(STEPS):

        @pl.when(j == i)
        def _():
            hook(i + 1)

    @pl.when(j == STEPS - 1)
    def _():
        hook(STEPS + 1)


def feed(xhat, pieces1, pieces2, par, inb, layer, last, lanes=(None, ())):
    n = len(pieces1)
    chunk = pl.BlockSpec((CHUNK, T), lambda j: (j, 0))
    next_shape = (T, D) if last else (D, T)
    return call(
        functools.partial(feed_kernel, n, 8 * layer, last), "feed",
        [sd(FF, T, t=bf16), sd(FF, T, t=bf16), sd(D, T), sd(8, T), sd(*next_shape, t=bf16 if last else f32)],
        [whole(D, T), whole(D, 128), whole(FF, 1)] + anywhere(2 * n),
        [chunk, chunk, whole(D, T), whole(8, T), whole(*next_shape)],
        [pltpu.VMEM((D, FF), bf16), pltpu.VMEM((FF, D), bf16), pltpu.VMEM((D, T), bf16), DMA((2, n))],
        (xhat, par, inb, *pieces1, *pieces2), lanes, 9_800_000_000, 40_000_000, (STEPS,), 6_000_000)


def norm_backward(dy_ref, xhat_ref, rstd_ref, gain, out_ref, grads_ref, gain_col, shift_col, width=128):
    total_gain = jnp.zeros((D, width), f32)
    total_shift = jnp.zeros((D, width), f32)
    for c in range(0, T, width):
        dy = dy_ref[:, c : c + width]
        xhat = xhat_ref[:, c : c + width]
        total_shift = total_shift + dy
        total_gain = total_gain + dy * xhat
        dxhat = dy * gain
        m1 = jnp.mean(dxhat, axis=0, keepdims=True)
        m2 = jnp.mean(dxhat * xhat, axis=0, keepdims=True)
        out_ref[:, c : c + width] = rstd_ref[0:1, c : c + width] * (dxhat - m1 - xhat * m2)
    grads_ref[:, gain_col : gain_col + 1] = jnp.sum(total_gain, axis=1, keepdims=True)
    grads_ref[:, shift_col : shift_col + 1] = jnp.sum(total_shift, axis=1, keepdims=True)


def lane_sum(value):
    return jnp.sum(value.astype(f32), axis=1, keepdims=True)


def permute_rows(dst_ref, src_ref, order, block):
    for i in range(D // block):
        dst_ref[i * block : (i + 1) * block, :] = src_ref[
            rows(order.target(i) * block, block), :]


def hidden_kernel(n, p, first, sums_in, dy_ref, xhat_ref, rstd_ref, par_ref, a_ref, g_ref, *rest, hook):
    order = Order(n)
    pieces, (keep_ref, send_ref, du_ref, dr_ref, cols_ref, w_ref, dz_ref, inb_ref, sem) = rest[:n], rest[n:]
    j = pl.program_id(0)

    @pl.when(j == 0)
    def _():
        loads = loader(pieces, w_ref, sem)
        for copy in loads:
            copy.start()
        hook(0)
        if first:
            dr_ref[...] = dy_ref[...].astype(f32).T
            dy = dr_ref
        else:
            dy = dy_ref
        cols_ref[...] = sums_in[...]
        norm_backward(dy, xhat_ref, rstd_ref, par_ref[:, p + 7 : p + 8], dr_ref, cols_ref, p + 7, p + 5)
        dz_ref[...] = dr_ref[...].astype(bf16)
        cols_ref[:, p + 4 : p + 5] = lane_sum(dz_ref[...])
        hook(1)
        for copy in loads:
            copy.wait()

    def du_step(i, _):
        base = i * SUB
        da = dot(w_ref[rows(j * CHUNK + base, SUB), :], dz_ref[...], NN)
        du = (da * g_ref[rows(base, SUB), :].astype(f32)).astype(bf16)
        du_ref[rows(base, SUB), :] = du
        inb_ref[rows(base, SUB), :] = lane_sum(du)
        return 0

    lax.fori_loop(0, CHUNK // SUB, du_step, 0)
    half = CHUNK // 2
    core = order.core

    def own(start):
        return a_ref[rows(start, half), :]

    keep_ref[order.slot(j, 0)] = dot(own(core * half), dz_ref[...], NT).astype(bf16)
    send_ref[order.slot(j, 1)] = dot(own((1 - core) * half), dz_ref[...], NT).astype(bf16)
    for i in range(STEPS):

        @pl.when(j == i)
        def _():
            column = 2 * 8 + p // 2 + i
            cols_ref[:, column : column + 1] = inb_ref[...]
            hook(i + 2)


def hidden(sums, dy, xhat, rstd, par, a, g, pieces, layer, first, lanes=(None, ())):
    n = len(pieces)
    chunk = pl.BlockSpec((CHUNK, T), lambda j: (j, 0))
    half = CHUNK // 2
    return call(
        functools.partial(hidden_kernel, n, 8 * layer, first), "hidden",
        [
            sd(STEPS, half, D, t=bf16), sd(STEPS, half, D, t=bf16), sd(FF, T, t=bf16), sd(D, T), sd(D, 128),
        ],
        [whole(D, 128), whole(*dy.shape), whole(D, T), whole(8, T), whole(D, 128), chunk, chunk] + anywhere(n),
        [
            whole(STEPS, half, D), whole(STEPS, half, D), chunk, whole(D, T), whole(D, 128),
        ],
        [pltpu.VMEM((FF, D), bf16), pltpu.VMEM((D, T), bf16), pltpu.VMEM((CHUNK, 1), f32), pltpu.SemaphoreType.DMA((n,))],
        (sums, dy, xhat, rstd, par, a, g, *pieces), lanes, 9_700_000_000, 40_000_000, (STEPS,))


def inner_kernel(n, p, sums_in, du_ref, dr_ref, xhat_ref, rstd_ref, par_ref, *rest, hook):
    order = Order(n)
    pieces, (keep_ref, send_ref, out_ref, cols_ref, w_ref, hl_ref, acc_ref, sem) = rest[:n], rest[n:]
    j = pl.program_id(0)

    @pl.when(j == 0)
    def _():
        loads = loader(pieces, w_ref, sem)
        for copy in loads:
            copy.start()
        hook(0)
        block = D // 8
        for i in range(8):
            at = rows(order.target(i) * block, block)
            hl_ref[i * block : (i + 1) * block, :] = (
                xhat_ref[at, :] * par_ref[at, p + 6 : p + 7] + par_ref[at, p + 3 : p + 4]).astype(bf16)
        acc_ref[...] = dr_ref[...]
        for copy in loads:
            copy.wait()

    for i, ref in enumerate((keep_ref, send_ref)):
        ref[...] = dot(hl_ref[i * (D // 2) : (i + 1) * (D // 2), :], du_ref[...], NT).astype(bf16)

    def dh_step(i, _):
        acc_ref[rows(i * SUB, SUB), :] += dot(
            w_ref[rows(i * SUB, SUB), rows(j * CHUNK, CHUNK)], du_ref[...], NN)
        return 0

    lax.fori_loop(0, D // SUB, dh_step, 0)

    @pl.when(j == STEPS - 1)
    def _():
        cols_ref[...] = sums_in[...]
        norm_backward(acc_ref, xhat_ref, rstd_ref, par_ref[:, p + 6 : p + 7], out_ref, cols_ref, p + 6, p + 3)
        cols_ref[:, p + 2 : p + 3] = lane_sum(out_ref[...].astype(bf16))
    for i in range(STEPS):

        @pl.when(j == i)
        def _():
            hook(i + 1)


def inner(sums, du, dr, xhat, rstd, par, pieces, layer, lanes=(None, ())):
    n = len(pieces)
    return call(
        functools.partial(inner_kernel, n, 8 * layer), "inner",
        [sd(D // 2, FF, t=bf16), sd(D // 2, FF, t=bf16), sd(D, T), sd(D, 128)],
        [whole(D, 128), pl.BlockSpec((CHUNK, T), lambda j: (j, 0)), whole(D, T), whole(D, T), whole(8, T), whole(D, 128)]
        + anywhere(n),
        [
            pl.BlockSpec((D // 2, CHUNK), lambda j: (0, j)), pl.BlockSpec((D // 2, CHUNK), lambda j: (0, j)),
            whole(D, T), whole(D, 128),
        ],
        [pltpu.VMEM((D, FF), bf16), pltpu.VMEM((D, T), bf16), pltpu.VMEM((D, T), f32), pltpu.SemaphoreType.DMA((n,))],
        (sums, du, dr, xhat, rstd, par, *pieces), lanes, 9_700_000_000, 35_000_000, (STEPS,))


def row_loader(src, dst, order, sem):
    block = D // 8
    return [
        pltpu.make_async_copy(
            src.at[rows(order.target(i) * block, block), :], dst.at[pl.ds(i * block, block), :], sem.at[i])
        for i in range(8)]


def values_kernel(sizes, p, small_in, sums_in, dr1_ref, mix_from, ctx_from, f_from, b_from, xl_from, small_ref, conv_ref,
                  *rest, hook):
    order = Order(sizes[0][0])
    groups, rest = grouped(rest, sizes)
    (keep_ref, send_ref, dctx_out, dv_ref, dz_ref, dbv_ref, small_out, cols_ref,
     w_ref, dp_ref, perm_ref, vpad_ref, dpad_ref, dctx_ref, f_ref, b_ref, v_ref, xperm_ref, taps_ref,
     sem, perm_sem, late_sem) = rest
    early = column_loader(groups, sizes, w_ref, sem, 3 * D, 4 * D)
    perms = row_loader(ctx_from, perm_ref, order, perm_sem.at[0])
    late = [pltpu.make_async_copy(mix_from.at[pl.ds(2 * D, D), :], v_ref, late_sem.at[0]),
            pltpu.make_async_copy(f_from, f_ref, late_sem.at[1]),
            pltpu.make_async_copy(b_from, b_ref, late_sem.at[2])]
    last = row_loader(xl_from, xperm_ref, order, perm_sem.at[1])
    for copy in early + perms + late + last:
        copy.start()
    for ref in (vpad_ref, dpad_ref):
        ref[:, 0:LEAD] = jnp.zeros((D, LEAD), bf16)
        ref[:, LEAD + T :] = jnp.zeros((D, LEAD), bf16)
    dp_ref[...] = dr1_ref[...].astype(bf16)
    hook(0)
    for copy in early:
        copy.wait()

    def dctx_step(i, _):
        at = rows(i * 384, 384)
        got = dot(w_ref[at, :], dp_ref[...], NN).astype(bf16)
        dctx_ref[at, :] = got
        dpad_ref[at, LEAD : LEAD + T] = got
        return 0

    lax.fori_loop(0, 2, dctx_step, 0)
    hook(1)
    leave = pltpu.make_async_copy(dctx_ref, dctx_out, late_sem.at[3])
    leave.start()
    for copy in perms:
        copy.wait()
    for i, ref in enumerate((keep_ref, send_ref)):
        ref[:, 0:D] = dot(perm_ref[i * (D // 2) : (i + 1) * (D // 2), :], dp_ref[...], NT).astype(bf16)
    for copy in late:
        copy.wait()
    vpad_ref[:, LEAD : LEAD + T] = v_ref[...]
    hook(2)
    flip = jnp.where(
        lax.broadcasted_iota(jnp.int32, (CONV_N, CONV_N), 0)
        + lax.broadcasted_iota(jnp.int32, (CONV_N, CONV_N), 1) == CONV_N - 1, 1.0, 0.0).astype(bf16)

    def value_step(h, _):
        base = h * HD
        dctx = dctx_ref[rows(base, HD), :]
        f = f_ref[rows(base, HD), :]
        dw = split(dot(f, dctx, NT))
        dz_ref[h] = dot3(dw, split(small_ref[1, h]), NT)
        dbv = dot3(split(small_ref[0, h]), dw, TN).astype(bf16)
        dbv_ref[h] = dbv
        dv = dot(dbv, b_ref[rows(base, HD), :], TN)
        conv = dot(windows(dpad_ref, base), toeplitz(conv_ref[h, 1:2]), NT)
        dv_ref[rows(base, HD), :] = (dv + unstack_blocks(conv)).astype(bf16)
        flipped = dot(stack_blocks(dctx), flip, NN).astype(bf16)
        g = dot(flipped, windows(vpad_ref, base), TN)
        g = pltpu.roll(g, CONV_K - CONV_N + 1 - (LEAD - RADIUS), 1, stride=1, stride_axis=0)
        taps_ref[pl.ds(h, 1), :] = jnp.sum(g[:, 0:128], axis=0, keepdims=True)
        return 0

    lax.fori_loop(0, HEADS // 2, value_step, 0, unroll=2)
    hook(3)
    lax.fori_loop(HEADS // 2, HEADS, value_step, 0, unroll=2)
    hook(4)
    for copy in last:
        copy.wait()
    for i, ref in enumerate((keep_ref, send_ref)):
        ref[:, D:] = dot(xperm_ref[i * (D // 2) : (i + 1) * (D // 2), :], dv_ref[...], NT).astype(bf16)
    cols_ref[...] = sums_in[...]
    cols_ref[:, p + 1 : p + 2] = lane_sum(dv_ref[...])
    first = p // 8 * HEADS
    small_out[...] = small_in[...]
    small_out[:, 0:D] = cols_ref[...].T[0:SMALL, :]
    small_out[first : first + HEADS, D:] = taps_ref[...]
    leave.wait()
    hook(5)


def values(total, sums, dr1, mix, ctx, f, b, xl, small, conv, groups, layer, lanes=(None, ())):
    sizes = sizes_of(groups, layer)
    n = sizes[0][0]
    return call(
        functools.partial(values_kernel, sizes, 8 * layer), "values",
        [
            sd(D // 2, 2 * D, t=bf16), sd(D // 2, 2 * D, t=bf16), sd(D, T, t=bf16), sd(D, T, t=bf16),
            sd(HEADS, LM, LM), sd(HEADS, LM, LM, t=bf16), sd(SMALL, D + 128), sd(D, 128),
        ],
        [vm(), vm(), vm()] + [ANY] * 5 + [vm(), vm()] + anywhere(n * len(groups)),
        [vm(), vm(), ANY] + [vm()] * 5,
        [
            pltpu.VMEM((D, D), bf16), pltpu.VMEM((D, T), bf16), pltpu.VMEM((D, T), bf16),
            pltpu.VMEM((D, T + 2 * LEAD), bf16), pltpu.VMEM((D, T + 2 * LEAD), bf16),
        ] + [pltpu.VMEM((D, T), bf16)] * 5 + [pltpu.VMEM((HEADS, 128), f32), DMA((len(groups), n)), DMA((2, 8)), DMA((4,))],
        (total, sums, dr1, mix, ctx, f, b, xl, small, conv, *[piece for g in groups for piece in g]), lanes,
        6_200_000_000, 25_000_000)


QK = 2 * D
QK_HEADS = ((0, 8), (8, 4))
TURNS = 20


def back_kernel(sizes, p, out, tail, sums_in, ns_from, mix_from, dctx_from, f_from, b_from, dv_from, xl_from, dr1_from,
                lm_ref, a_ref, small_ref, dz0_ref, dbv_ref, *rest, hook):
    order = Order(sizes[0][0])
    groups, rest = grouped(rest, sizes)
    if out:
        keep_ref, send_ref, *rest = rest
    dx_ref, cols_ref, *rest = rest
    if not out:
        keep_ref, send_ref, *rest = rest
    (w_ref, ns_ref, mix_ref, dctx_ref, f_ref, b_ref, dv_ref, perm_ref, dr1_ref, dz_ref, da_ref,
     sem, ns_sem, late_sem, perm_sem) = rest

    def load_ns(i):
        return pltpu.make_async_copy(
            ns_from.at[NS_ITERS - 1 - i], ns_ref.at[lax.rem(i, 2)], ns_sem.at[lax.rem(i, 2)])

    load_ns(0).start()
    late = [
        pltpu.make_async_copy(src, dst, late_sem.at[i]) for i, (src, dst) in enumerate((
            (mix_from, mix_ref), (dctx_from, dctx_ref), (f_from, f_ref), (b_from, b_ref), (dv_from, dv_ref),
            (dr1_from, dr1_ref)))]
    late += row_loader(xl_from, perm_ref, order, perm_sem)
    late += column_loader(groups, sizes, w_ref, sem, 0, 3 * D)
    for lane in tail:
        lane.use(keep_ref, send_ref, cols_ref)
    for copy in late:
        copy.start()
    hook(0)
    for h in range(HEADS):
        da_ref[h] = jnp.zeros((LM, LM), f32)
        dz_ref[h] = dz0_ref[h]

    def ns_step(i, _):
        k = lax.rem(i, 2)
        load_ns(i).wait()

        @pl.when(i + 1 < NS_ITERS)
        def _():
            load_ns(i + 1).start()

        d3, dzs, dps, d2 = [], [], [], []
        for h in range(HEADS):
            dzn = split(0.25 * dz_ref[h])
            d3.append(split(dot3(split(ns_ref[k, 0, h]), dzn, TN)))
            dz_ref[h] = dot3(dzn, split(ns_ref[k, 3, h]), NT)
        for h in range(HEADS):
            p = split(ns_ref[k, 1, h])
            d2.append(split(-dot3(p, d3[h], TN)))
            dps.append(dot3(d3[h], split(ns_ref[k, 2, h]), NT))
        for h in range(HEADS):
            p = ns_ref[k, 1, h]
            d1 = dot3(split(p), d2[h], TN)
            dp = d1 - dps[h] - dot3(d2[h], split(eye(7.0) - p), NT)
            dps[h] = split(dp)
        for h in range(HEADS):
            da_ref[h] += dot3(dps[h], split(ns_ref[k, 0, h]), NT)
            dz_ref[h] += dot3(split(a_ref[h]), dps[h], TN)
        return 0

    lax.fori_loop(0, NS_ITERS // 2, ns_step, 0)
    hook(1)
    lax.fori_loop(NS_ITERS // 2, NS_ITERS, ns_step, 0)
    for copy in late:
        copy.wait()
    hook(2)
    spread = segment_spread()

    def score_step(h, _):
        base = h * HD
        a = a_ref[h]
        dz0 = dz_ref[h].T
        s = 1.0 / jnp.sum(a * a)
        da = da_ref[h] + s * dz0 - (2.0 * s * s * jnp.sum(dz0 * a)) * a
        dsa = (SCALE * a * (da - jnp.sum(a * da, axis=1, keepdims=True))).astype(bf16)
        ql = lm_ref[rows(base, HD), :]
        kl = lm_ref[rows(D + base, HD), :]
        q = mix_ref[rows(base, HD), :]
        k = mix_ref[rows(D + base, HD), :]
        f = f_ref[rows(base, HD), :].astype(f32)
        df = dot(small_ref[2, h].astype(bf16), dctx_ref[rows(base, HD), :], NN)
        dsf = (SCALE * f * (df - jnp.sum(f * df, axis=0, keepdims=True))).astype(bf16)
        b = b_ref[rows(base, HD), :].astype(f32)
        db = dot(dbv_ref[h], mix_ref[rows(2 * D + base, HD), :], NN)
        dsb = (SCALE * b * (db - jnp.sum(b * db, axis=1, keepdims=True))).astype(bf16)
        dkl = dot(q, dsf, NT) + dot(ql, dsa, NN)
        dql = dot(kl, dsa, NT) + dot(k, dsb, NT)
        dq = dot(kl, dsf, NN) + dot((dql * (1.0 / SEG)).astype(bf16), spread, NN)
        dk = dot(ql, dsb, NN) + dot((dkl * (1.0 / SEG)).astype(bf16), spread, NN)
        mix_ref[rows(base, HD), :] = dq.astype(bf16)
        mix_ref[rows(D + base, HD), :] = dk.astype(bf16)
        return 0

    half = D // 2
    at = 0
    for part, (head, heads) in enumerate(QK_HEADS):
        middle = head + heads // 2
        lax.fori_loop(head, middle, score_step, 0, unroll=heads // 2)
        hook(3 + 2 * part)
        lax.fori_loop(middle, head + heads, score_step, 0, unroll=heads // 2)
        if head + heads == HEADS:
            cols_ref[...] = sums_in[...]
            cols_ref[:, p : p + 1] = lane_sum(mix_ref[0:D, :])
        width = heads * HD
        for k in range(2):
            d = mix_ref[k * D + head * HD : k * D + head * HD + width, :]
            for side, ref in ((1, send_ref), (0, keep_ref)):
                mine = perm_ref[side * half : (side + 1) * half, :]
                ref[:, at : at + width] = dot(mine, d, NT).astype(bf16)
            at += width
        hook(4 + 2 * part)
    for i in range(3):
        at = slice(i * 256, (i + 1) * 256)
        got = dr1_ref[at, :] + dot(w_ref[at, 0:QK], mix_ref[0:QK, :], NN) + dot(w_ref[at, QK:], dv_ref[...], NN)
        if p:
            dx_ref[at, :] = got
        else:
            dx_ref[:, at] = got.T
        hook(7 + i)
    for i in range(10, TURNS):
        hook(i)


def back(sums, ns, mix, dctx, f, b, dv, xl, dr1, lm, a, small, dz0, dbv, groups, layer, lanes=(None, ()), tail=(), on=False):
    sizes = sizes_of(groups, layer)
    n = sizes[0][0]
    halves = [(D // 2, QK)] * 2
    out = 0 if on and layer == 0 else 1
    got = call(
        functools.partial(back_kernel, sizes, 8 * layer, out, tail), "back",
        [sd(*h, t=bf16) for h in halves] * out + [sd(*((D, T) if layer else (T, D))), sd(D, 128)],
        [vm()] + [ANY] * 8 + [vm()] * 5 + anywhere(n * len(groups)), [vm()] * (2 + 2 * out),
        [pltpu.VMEM(h, bf16) for h in halves] * (1 - out) + [
            pltpu.VMEM((D, 3 * D), bf16), pltpu.VMEM((2, 4, HEADS, LM, LM), f32), pltpu.VMEM((3 * D, T), bf16),
        ] + [pltpu.VMEM((D, T), bf16)] * 5 + [
            pltpu.VMEM((D, T), f32), pltpu.VMEM((HEADS, LM, LM), f32), pltpu.VMEM((HEADS, LM, LM), f32),
            DMA((len(groups), n)), DMA((2,)), DMA((6,)), DMA((8,)),
        ],
        (sums, ns, mix, dctx, f, b, dv, xl, dr1, lm, a, small, dz0, dbv, *[piece for g in groups for piece in g]),
        lanes, 10_000_000_000, 50_000_000)
    return got if out else [None, None, *got]


class Ring:
    def __init__(self, wide, narrow):
        self.wide, self.narrow = wide, narrow
        self.bits = wide.bit_length() - 1
        up = list(range(1, self.bits))
        self.gather_order = (up, up[::-1])
        self.scatter_order = (up[::-1], up)
        self.exact = wide == 8 and narrow == 4

    def pairs(self, flip):
        n = self.narrow
        out = []
        for w in range(self.wide):
            for z in range(n):
                to_w, to_z = flip(w, z)
                out.append((w * n + z, to_w * n + to_z))
        return out

    def narrow_pairs(self, k):
        return self.pairs(lambda w, z: (w, z ^ k))

    def step_pairs(self, order, s):
        return self.pairs(lambda w, z: (w ^ (1 << order[w & 1][s]), z))

    def core_pairs(self):
        return self.pairs(lambda w, z: (w ^ 1, z))

    def gathered(self, w):
        out = []
        for other in (0, 1):
            v = w ^ other
            for code in range(self.wide // 2):
                t = v
                for s in range(self.bits - 1):
                    if code >> s & 1:
                        t ^= 1 << self.gather_order[v & 1][s]
                out.append(t)
        return out

    def slots(self, w):
        out = []
        for other in (0, 1):
            v = w ^ other
            for code in range(self.wide // 2):
                t = v
                for s in range(self.bits - 1):
                    if code >> (self.bits - 2 - s) & 1:
                        t ^= 1 << self.scatter_order[v & 1][s]
                out.append(t)
        return out

    def mine(self, table):
        return lax.dynamic_index_in_dim(jnp.asarray(table), lax.axis_index("wide"), 0, keepdims=False)

    def gather(self, shard):
        z = lax.axis_index("narrow")
        parts = [shard] + [lax.ppermute(shard, AXES, self.narrow_pairs(k)) for k in range(1, self.narrow)]
        yield []
        bit = 1
        while bit < self.narrow:
            swap = (z & bit) != 0
            parts = [jnp.where(swap, parts[k ^ bit], parts[k]) for k in range(self.narrow)]
            bit *= 2
        held = [jnp.concatenate(parts, axis=0)]
        got = held
        for s in range(self.bits - 1):
            pairs = self.step_pairs(self.gather_order, s)
            fresh, got = got, [lax.ppermute(h, AXES, pairs) for h in held]
            held = held + got
            yield fresh
        other = [lax.ppermute(h, AXES, self.core_pairs()) for h in held]
        yield got
        held = held + other
        return held if self.exact else [self.join(held)]

    def join(self, pieces):
        inverse = np.stack([np.argsort(self.gathered(w)) for w in range(self.wide)]).astype(np.int32)
        stacked = jnp.stack(pieces)
        return jnp.take(stacked, self.mine(inverse), axis=0).reshape(-1, stacked.shape[-1])

    def scatter(self, keep, send):
        half = self.wide // 2
        if not self.exact:
            slots = np.stack([self.slots(w) for w in range(self.wide)]).astype(np.int32)
            whole = jnp.concatenate([keep, send], axis=0)
            whole = whole.reshape(self.wide, -1, whole.shape[-1])
            whole = jnp.take(whole, self.mine(slots), axis=0)
            keep, send = whole[:half], whole[half:]
        got = lax.ppermute(send, AXES, self.core_pairs())
        yield [send]
        total = keep.astype(f32) + got.astype(f32)
        for s in range(self.bits - 1):
            half //= 2
            away = total[half:].astype(bf16)
            got = lax.ppermute(away, AXES, self.step_pairs(self.scatter_order, s))
            yield [away]
            total = total[:half] + got.astype(f32)
        total = total[0]
        size = total.shape[0] // self.narrow
        z = lax.axis_index("narrow")
        own = lax.dynamic_slice_in_dim(total, z * size, size, axis=0)
        low = total.astype(bf16)
        parts = [lax.dynamic_slice_in_dim(low, (z ^ k) * size, size, axis=0) for k in range(1, self.narrow)]
        got = [lax.ppermute(parts[k - 1], AXES, self.narrow_pairs(k)) for k in range(1, self.narrow)]
        yield parts
        for part in got:
            own = own + part.astype(f32)
        return own

    def sum(self, keep, send):
        blocks = self.wide // 2
        return finish(self.scatter(
            keep.reshape(blocks, -1, keep.shape[-1]), send.reshape(blocks, -1, send.shape[-1])))

    def total(self, value):
        bit = 1
        while bit < self.narrow:
            value = value + lax.ppermute(value, AXES, self.narrow_pairs(bit))
            bit *= 2
        for s in range(self.bits - 1):
            value = value + lax.ppermute(value, AXES, self.pairs(lambda w, z: (w ^ (2 << s), z)))
        return value + lax.ppermute(value, AXES, self.core_pairs())


def natural_halves(keep, send):
    both = jnp.stack([keep, send], axis=1)
    both = both.reshape(2, -1, both.shape[-1])
    return both[0], both[1]


def conv_rows(conv):
    at = LEAD - RADIUS
    tail = CONV_K - at - KSIZE
    both = jnp.stack([conv, conv[:, ::-1]], axis=1)
    return jnp.pad(both.astype(f32), ((0, 0), (0, 0), (at, tail)))


def finish(steps):
    while True:
        try:
            next(steps)
        except StopIteration as end:
            return end.value


def small_outputs(ring, total, size, hidden_size):
    layers = total.shape[0] // (8 + STEPS)
    here = lax.axis_index("wide") * ring.narrow + lax.axis_index("narrow")
    lines = total[: 8 * layers, :D].reshape(layers, 8, D)
    lines = lax.dynamic_slice_in_dim(lines, here * size, size, axis=2)
    inb = total[8 * layers :, :D].reshape(layers, FF)
    inb = lax.dynamic_slice_in_dim(inb, here * hidden_size, hidden_size, axis=1)
    taps = total[:, D : D + KSIZE].reshape(layers, HEADS, KSIZE)
    return lines[:, :6], lines[:, 6:], inb, taps


def small_shard(in_b, bias_rows, gain_rows):
    layers, size = bias_rows.shape[0], bias_rows.shape[2]
    columns = jnp.concatenate([bias_rows, gain_rows], axis=1).transpose(2, 0, 1).reshape(size, 8 * layers)
    inner_bias = in_b.reshape(layers, size, -1).transpose(1, 0, 2).reshape(size, -1)
    small = jnp.concatenate([columns, inner_bias], axis=1)
    return jnp.pad(small, ((0, 0), (0, 128 - small.shape[1])))


def gather_all(ring, attention_shards, in_w, out2_w):
    layers = in_w.shape[0]
    return (
        [finish(ring.gather(shard)) for shard in attention_shards],
        [finish(ring.gather(in_w[layer])) for layer in range(layers)],
        [finish(ring.gather(out2_w[layer])) for layer in range(layers)],
    )


class Plan:
    def __init__(self):
        self.count = 0

    def lanes(self, *lanes):
        self.count += 1
        return (self.count, list(lanes))


def body(ring, tokens, cotangent, qkv_w, out_w, in_w, in_b, out2_w, bias_rows, gain_rows, conv_w):
    layers = qkv_w.shape[0]
    size = qkv_w.shape[1]
    small = small_shard(in_b, bias_rows, gain_rows)
    plan = Plan()
    none = (None, ())
    on = ring.exact and layers == 2
    x = tokens.T.astype(f32)
    conv = [conv_rows(conv_w[layer]) for layer in range(layers)]
    on_attention, on_feed = [none] * layers, [none] * layers
    qkvo = [jnp.concatenate([qkv_w[layer], out_w[layer]], axis=1) for layer in range(layers)]
    if on:
        s1 = Spread(jnp.concatenate([qkvo[0][:, : 2 * D], small], axis=1), 0, 1)
        s2 = Spread(qkvo[0][:, 2 * D :], 1, 3)
        g1, g2 = Gather(s1), Gather(s2)
        s3 = Spread(in_w[0], 3, 8)
        g3 = Gather(s3)
        m1 = g1.go(a=(1, 2), b=(2, 4), core0=(1, 8), core1=(2, 8), core2=(4, 8))
        m2 = g2.go(apart=1, a=(3, 5), b=(5, 7), core0=(3, 9), core1=(5, 9), core2=(7, 9))
        exchange(plan.lanes(s1, s2, *m1, *m2, s3), 10)
        att = [[g1.pieces(), g2.pieces()], None]
        win, wout = [None] * 2, [None] * 2
        s4, s5 = Spread(out2_w[0], 0, 6), Spread(qkvo[1], 6, 10)
        g4 = Gather(s4)
        m3 = g3.go(a=(0, 4), b=(4, 9), core0=(0, 4), core1=(4, 9), core2=(9, 11))
        m4 = g4.go(apart=1, a=(6, 8), b=(8, 10), core0=(6, 9), core1=(8, 10), core2=(10, 12))
        g5 = Gather(s5)
        m5 = g5.go(a=(10, 12))
        on_attention[0] = plan.lanes(s4, *m3, *m4, s5, *m5)
    else:
        shards = [jnp.concatenate([qkvo[0], small], axis=1)] + qkvo[1:]
        att, win, wout = gather_all(ring, shards, in_w, out2_w)
        att = [[pieces] for pieces in att]

    kept = []
    par = None
    for layer in range(layers):
        final = layer == layers - 1
        xl, mix, lm, par, ctx, f, b, a, ns, sm, xhat1, rstd1 = attention(
            x, att[layer], par, conv[layer], layer, on_attention[layer])
        if on and layer == 0:
            win[0], wout[0] = g3.pieces(), g4.pieces()
            s6, s7 = Spread(in_w[1], 0, 3), Spread(out2_w[1], 3, 5)
            g6, g7 = Gather(s6), Gather(s7)
            m5 = g5.go(b=(0, 3), core0=(0, 3), core1=(0, 3), core2=(3, 5))
            m6 = g6.go(a=(3, 5))
            on_feed[0] = plan.lanes(*m5, s6, s7, *m6)
        if on and layer == 1:
            win[1], wout[1] = g6.pieces(), g7.pieces()
        at = 8 * layers + FF // D * layer
        inb = par[:, at : at + FF // D].reshape(FF, 1)
        act, slope, xhat2, rstd2, x = feed(
            xhat1, win[layer], wout[layer], par, inb, layer, final, on_feed[layer])
        if on and layer == 0:
            att[1] = [g5.pieces()]
            m6 = g6.go(b=(0, 6), core0=(0, 6), core1=(0, 6), core2=(6, 11))
            m7 = g7.go(apart=1, a=(0, 6), b=(6, 10), core0=(0, 6), core1=(6, 10), core2=(10, 12))
            on_attention[1] = plan.lanes(*m6, *m7)
        kept.append((xl, mix, lm, ctx, f, b, a, ns, sm, xhat1, rstd1, act, slope, xhat2, rstd2))
    output = x

    dy = cotangent
    sums = jnp.zeros((D, 128), f32)
    total = jnp.zeros((SMALL, D + 128), f32)
    grads = [{} for _ in range(layers)]
    firsts, thirds, ends = {}, {}, []

    def sum_first(keep, send, turns, layer, place):
        firsts[layer, place] = ReduceFirst(keep, send, turns)
        return firsts[layer, place]

    def sum_third(layer, place, turns):
        thirds[layer, place] = Third(*firsts[layer, place].value, turns)
        return thirds[layer, place]

    def ending(lane, layer, place):
        ends.append((lane, layer, place))
        return lane

    def sum_final(layer, place, turns):
        return ending(Final(*thirds[layer, place].value, turns), layer, place)

    def sum_last(layer, place, turns):
        return ending(ReduceLast(*firsts[layer, place].value, turns), layer, place)

    halves = None
    for layer in reversed(range(layers)):
        xl, mix, lm, ctx, f, b, a, ns, sm, xhat1, rstd1, act, slope, xhat2, rstd2 = kept[layer]
        above = layer + 1 < layers
        lane = none
        if on and above:
            firsts[layer + 1, "ov"] = Plane(*core_ov.value, (0, 5))
            lane = plan.lanes(
                sum_first(*halves, (0, 1, 5), layer + 1, "qk"), firsts[layer + 1, "ov"],
                sum_final(layer + 1, "in", (0, 5)))
        keep, send, du, dr2, sums = hidden(
            sums, dy, xhat2, rstd2, par, act, slope, wout[layer], layer, not above, lane)
        if on:
            out2 = (keep.reshape(-1, D), send.reshape(-1, D))
            if above:
                lane = [
                    sum_first(*out2, (0, 1, 4), layer, "out2"),
                    sum_third(layer + 1, "qk", (0, 3)), sum_third(layer + 1, "ov", (0, 3))]
            else:
                core2 = Core(*out2, (0, 2))
                lane = [core2]
            lane = plan.lanes(*lane)
        else:
            grads[layer]["out2"] = ring.sum(*natural_halves(keep, send))
        keep, send, dr1, sums = inner(sums, du, dr2, xhat1, rstd1, par, win[layer], layer, lane)
        if on:
            core1 = Core(keep, send, (0, 3))
            if above:
                lane = [
                    sum_third(layer, "out2", (0, 5)), sum_first(keep, send, (0, 1, 5), layer, "in"),
                    sum_final(layer + 1, "qk", (0, 5)), sum_final(layer + 1, "ov", (0, 5))]
            else:
                core1 = Core(keep, send, (0, 3))
                firsts[layer, "out2"] = Plane(*core2.value, (0, 5))
                lane = [firsts[layer, "out2"], core1]
            lane = plan.lanes(*lane)
        else:
            grads[layer]["in"] = ring.sum(keep, send)
        keep, send, dctx, dv, dz, dbv, total, sums = values(
            total, sums, dr1, mix, ctx, f, b, xl, sm, conv[layer], att[layer], layer, lane)
        tail = []
        if on:
            if layer:
                core_ov = Core(keep, send, (0, 2))
                lead = Plane(*core1.value, (0, 4), chained=True)
                thirds[layer, "in"] = Third(None, None, (4, 10), inside=lead)
                lane = [sum_last(layer, "out2", (0, 3, 10)), lead, thirds[layer, "in"], core_ov]
            else:
                late = Total(total, (6, 8, 10, 11, 13, 15))
                lane, tail = [late], [late]
                starts = (0, 2 * QK_HEADS[0][1] * HD, QK)
                for part, (go, end) in enumerate((((4, 5, 8), (8, 11, 14)), ((6, 9, 11), (11, 13, 15)))):
                    lead = ReduceFirst(None, None, go, chained=True, columns=slice(starts[part], starts[part + 1]))
                    tail.append(lead)
                    lane = [lead, ending(ReduceLast(None, None, end, inside=lead), 0, f"qk{part}")] + lane
                lead = ReduceFirst(keep, send, (0, 1, 3), chained=True)
                lane += [
                    sum_final(0, "out2", (0, 4)), sum_last(0, "in", (0, 2, 6)), lead,
                    ending(ReduceLast(None, None, (3, 4, 10), inside=lead), 0, "ov")]
            lane = plan.lanes(*lane)
        else:
            grads[layer]["ov"] = ring.sum(keep, send)
        keep, send, dy, sums = back(
            sums, ns, mix, dctx, f, b, dv, xl, dr1, lm, a, sm, dz, dbv, att[layer], layer, lane, tuple(tail), on)
        halves = (keep, send)
        if not on:
            grads[layer]["qk"] = ring.sum(keep, send)
    if on:
        for lane, layer, place in ends:
            grads[layer][place] = lane.value
        grads[0]["qk"] = jnp.concatenate([grads[0]["qk0"], grads[0]["qk1"]], axis=1)
        total = late.value
    else:
        total = ring.total(jnp.concatenate([sums.T[:SMALL], total[:, D:]], axis=1))
    gbias, ggain, ginb, gtaps = small_outputs(ring, total, size, in_b.shape[1])
    first = 2 * QK_HEADS[0][1] * HD
    cut, rest = first // 2, (QK - first) // 2
    stacked = [
        jnp.stack([
            jnp.concatenate([
                g["qk"][:, :cut], g["qk"][:, first : first + rest], g["qk"][:, cut:first], g["qk"][:, first + rest :],
                g["ov"][:, D:]], axis=1) for g in grads]),
        jnp.stack([g["ov"][:, :D] for g in grads]),
        jnp.stack([g["in"] for g in grads]),
        jnp.stack([g["out2"] for g in grads])]
    return (output, dy, stacked[0], stacked[1], stacked[2], ginb, stacked[3], gbias, ggain, gtaps)


def solution(mesh):
    ring = Ring(mesh.shape["wide"], mesh.shape["narrow"])
    rows3 = P(None, AXES, None)
    columns3 = P(None, None, AXES)
    weights = (rows3, rows3, rows3, P(None, AXES), rows3, columns3, columns3, P())
    return jax.shard_map(
        functools.partial(body, ring),
        mesh=mesh,
        in_specs=(P(AXES, None), P(AXES, None)) + weights,
        out_specs=(P(AXES, None), P(AXES, None)) + weights,
        check_vma=False,
    )
```

```python
import functools
import jax
import jax.numpy as jnp
import numpy as np
from jax import lax
from jax.experimental import pallas as pl
from jax.experimental.pallas import tpu as pltpu
from jax.sharding import PartitionSpec as P

D = 768
HEADS = 12
HD = 64
FF = 3072
LM = 64
KSIZE = 33
RADIUS = KSIZE // 2
NS_ITERS = 6
T = 1024
SEG = T // LM
SCALE = HD ** -0.5
EPS = 1e-05
CONV_N = 256
CONV_K = 512
CONV_BLOCKS = T // CONV_N
LEAD = 128
f32 = jnp.float32
bf16 = jnp.bfloat16
AXES = ("wide", "narrow")
NN = (((1,), (0,)), ((), ()))
NT = (((1,), (1,)), ((), ()))
TN = (((0,), (0,)), ((), ()))
VMEM_LIMIT = 60 * 1024 * 1024


def dot(a, b, dims):
    return lax.dot_general(a, b, dims, preferred_element_type=f32)


def split(a):
    high = a.astype(bf16)
    return high, (a - high.astype(f32)).astype(bf16)


def dot3(a, b, dims):
    if dims is NN:
        return dot(a[0], b[0], dims) + (dot(a[0], b[1], dims) + dot(a[1], b[0], dims))
    (i,), (j,) = dims[0]
    return dot(jnp.concatenate([a[0], a[0], a[1]], axis=i), jnp.concatenate([b[0], b[1], b[0]], axis=j), dims)


def rows(start, size):
    if isinstance(start, int):
        return pl.ds(start, size)
    return pl.ds(pl.multiple_of(start, size), size)


def segment_mean():
    token = lax.broadcasted_iota(jnp.int32, (T, LM), 0)
    seg = lax.broadcasted_iota(jnp.int32, (T, LM), 1)
    return jnp.where(token // SEG == seg, 1.0 / SEG, 0.0).astype(bf16)


def segment_spread():
    token = lax.broadcasted_iota(jnp.int32, (LM, T), 1)
    seg = lax.broadcasted_iota(jnp.int32, (LM, T), 0)
    return jnp.where(token // SEG == seg, 1.0, 0.0).astype(bf16)


def eye(value):
    i = lax.broadcasted_iota(jnp.int32, (LM, LM), 0)
    j = lax.broadcasted_iota(jnp.int32, (LM, LM), 1)
    return jnp.where(i == j, value, 0.0).astype(f32)


def toeplitz(row):
    full = jnp.broadcast_to(row, (CONV_N, CONV_K))
    return pltpu.roll(full, 0, 1, stride=1, stride_axis=0).astype(bf16)


def windows(ref, base):
    return jnp.concatenate(
        [ref[rows(base, HD), CONV_N * b : CONV_N * b + CONV_K] for b in range(CONV_BLOCKS)], axis=0
    )


def stack_blocks(value):
    return jnp.concatenate(
        [value[:, CONV_N * b : CONV_N * (b + 1)] for b in range(CONV_BLOCKS)], axis=0
    )


def unstack_blocks(value):
    return jnp.concatenate(
        [value[HD * b : HD * (b + 1), :] for b in range(CONV_BLOCKS)], axis=1
    )


def norm_forward(r_ref, xhat_ref, rstd_ref, width=128):
    for c in range(0, T, width):
        r = r_ref[:, c : c + width]
        center = r - jnp.mean(r, axis=0, keepdims=True)
        rstd = lax.rsqrt(jnp.mean(center * center, axis=0, keepdims=True) + EPS)
        xhat_ref[:, c : c + width] = center * rstd
        rstd_ref[:, c : c + width] = jnp.broadcast_to(rstd, (8, width))


def vm():
    return pl.BlockSpec(memory_space=pltpu.VMEM)


def anywhere(n):
    return [pl.BlockSpec(memory_space=pl.ANY)] * n


def whole(*s):
    return pl.BlockSpec(s, lambda *_: (0,) * len(s))


def sd(*s, t=f32):
    return jax.ShapeDtypeStruct(s, t)


def loader(pieces, dst, sem, columns=None):
    r = pieces[0].shape[0]
    order = Order(len(pieces))
    out = []
    for i, piece in enumerate(pieces):
        src = piece if columns is None else piece.at[:, pl.ds(*columns)]
        at = rows(order.target(i) * r, r)
        out.append(pltpu.make_async_copy(src, dst.at[at, :], sem.at[i]))
    return out


def sizes_of(groups, layer):
    return [(len(g), g[0].shape[1] - (128 if layer == 0 and i == 0 else 0)) for i, g in enumerate(groups)]


def grouped(refs, sizes):
    groups = []
    for n, _ in sizes:
        groups.append(refs[:n])
        refs = refs[n:]
    return groups, refs


def column_loader(groups, sizes, dst, sem, low, high):
    out = []
    at = 0
    for g, (n, width) in enumerate(sizes):
        a, b = max(low, at), min(high, at + width)
        if b > a:
            out += loader(groups[g], dst.at[:, pl.ds(a - low, b - a)], sem.at[g], (a - at, b - a))
        at += width
    return out


def call(kernel, name, out_shape, in_specs, out_specs, scratch, args, lanes, flops, size, grid=None, trans=0):
    identity, lanes = lanes
    ins, outs = len(args), len(out_shape)
    lane_args = [a for lane in lanes for a in lane.args]
    lane_outs = [o for lane in lanes for o in lane.outs]
    lane_scratch = [o for lane in lanes for o in lane.scratch]

    def run(*refs):
        refs = list(refs)

        def take(n):
            got = refs[:n]
            del refs[:n]
            return got

        own = take(ins)
        lane_in = [take(len(lane.args)) for lane in lanes]
        own += take(outs)
        lane_out = [take(len(lane.outs)) for lane in lanes]
        own += take(len(scratch))
        for lane, a, o in zip(lanes, lane_in, lane_out):
            lane.bind(a, o, take(len(lane.scratch)))

        def hook(i):
            if lanes and i == 0:
                near = Near()
                names = sorted({p for lane in lanes for p in lane.partners})
                barrier = pltpu.get_barrier_semaphore()
                for p in names:
                    pl.semaphore_signal(barrier, inc=1, device_id=near.at(p), device_id_type=pl.DeviceIdType.MESH)
                pl.semaphore_wait(barrier, len(names))
            for lane in lanes:
                lane.turn(i)

        kernel(*own, hook=hook)

    params = {"collective_id": identity, "has_side_effects": True} if lanes else {}
    got = pl.pallas_call(
        run,
        out_shape=list(out_shape) + [o for o, _ in lane_outs],
        in_specs=list(in_specs) + [spec for lane in lanes for spec in lane.specs],
        out_specs=list(out_specs) + [spec for _, spec in lane_outs],
        scratch_shapes=list(scratch) + lane_scratch,
        **({} if grid is None else {"grid": grid}),
        compiler_params=pltpu.CompilerParams(vmem_limit_bytes=VMEM_LIMIT, **params),
        cost_estimate=pl.CostEstimate(flops=flops, bytes_accessed=size, transcendentals=trans),
        name=name,
    )(*args, *lane_args)
    own, rest = list(got[:outs]), list(got[outs:])
    for lane in lanes:
        n = len(lane.outs)
        lane.done(rest[:n])
        rest = rest[n:]
    return own


class Near:
    def __init__(self):
        self.w, self.z = lax.axis_index("wide"), lax.axis_index("narrow")

    def over(self, k):
        z = self.z
        if k == 1:
            return z + 1 - 2 * (z % 2)
        if k == 2:
            return z + 2 - 4 * (z // 2)
        return 3 - z

    def at(self, name):
        w, core = self.w, self.w % 2
        if name[0] == "z":
            return (w, self.over(int(name[1])))
        if name == "core":
            return (w + 1 - 2 * core, self.z)
        step = {"a": 2 + 2 * core, "b": 4 - 2 * core, "x": 2, "y": 4}[name]
        return (w + step - 2 * step * ((w // step) % 2), self.z)


def remote(src, dst, send, recv, name):
    return pltpu.make_async_remote_copy(
        src_ref=src, dst_ref=dst, send_sem=send, recv_sem=recv, device_id=Near().at(name),
        device_id_type=pl.DeviceIdType.MESH)


DMA = pltpu.SemaphoreType.DMA
ANY = pl.BlockSpec(memory_space=pl.ANY)


class Move:
    def __init__(self, source, name, start, wait):
        self.chained = not hasattr(source, "dtype")
        self.source, self.name, self.start, self.wait = source, name, start, wait
        self.shape = source.shape
        self.args = [] if self.chained else [source]
        self.specs = [ANY] * len(self.args)
        self.outs = [(sd(*self.shape, t=bf16), ANY)]
        self.scratch = [DMA((2,))]
        self.partners = [name]

    def bind(self, args, outs, scratch):
        self.src = self.source.dst if self.chained else args[0]
        self.dst, self.sem = outs[0], scratch[0]

    def copy(self):
        return remote(self.src, self.dst, self.sem.at[0], self.sem.at[1], self.name)

    def turn(self, i):
        if i == self.wait:
            self.copy().wait()
        if i == self.start:
            self.copy().start()

    def done(self, got):
        self.value = got[0].reshape(-1, self.shape[-1])


class Spread:
    def __init__(self, shard, start, wait):
        self.start, self.wait = start, wait
        self.shape = (4, *shard.shape)
        self.args, self.specs = [shard], [ANY]
        self.outs = [(sd(*self.shape, t=bf16), ANY)]
        self.scratch = [DMA((7,))]
        self.partners = ["z1", "z2", "z3"]

    def bind(self, args, outs, scratch):
        self.src, self.dst, self.sem = args[0], outs[0], scratch[0]

    def copies(self):
        z = lax.axis_index("narrow")
        out = [pltpu.make_async_copy(self.src, self.dst.at[z], self.sem.at[6])]
        for k in (1, 2, 3):
            out.append(remote(self.src, self.dst.at[z], self.sem.at[2 * k - 2], self.sem.at[2 * k - 1], f"z{k}"))
        return out

    def turn(self, i):
        if i == self.wait:
            for copy in self.copies():
                copy.wait()
        if i == self.start:
            for copy in self.copies():
                copy.start()

    def done(self, got):
        self.value = got[0].reshape(-1, self.shape[-1])


class Gather:
    def __init__(self, block):
        self.block, self.moves = block, {}

    def at(self, name):
        if name == "own":
            return self.block
        return self.moves[name]

    def go(self, apart=0, **turns):
        out = []
        fresh = {}
        value = lambda k: fresh[k] if k in fresh else (
            self.moves[k].value if k in self.moves else
            self.block.value if hasattr(self.block, "value") else self.block)
        for key, turn in turns.items():
            if key == "a":
                todo = [("a", "own", "a")]
            elif key == "b":
                todo = [("b0", "own", "b"), ("b1", "a", "b")]
            else:
                todo = {"core0": [("c0", "own", "core")], "core1": [("c1", "a", "core")],
                        "core2": [("c2", "b0", "core"), ("c3", "b1", "core")]}[key]
            for name, source, partner in todo:
                start, wait = turn
                if name == "b1":
                    wait += apart
                if name == "c3":
                    start += apart
                fresh[name] = Move(value(source), partner, start, wait)
                out.append(fresh[name])
        self.moves.update(fresh)
        return sorted(out, key=lambda m: m.start)

    def pieces(self):
        block = self.block.value if hasattr(self.block, "value") else self.block
        return [block] + [self.moves[k].value for k in ("a", "b0", "b1", "c0", "c1", "c2", "c3")]


def strips(columns):
    width = 384 if columns % 384 == 0 else 512 if columns % 512 == 0 else columns
    return [slice(c, c + width) for c in range(0, columns, width)]


class ReduceFirst:
    def __init__(self, keep, send, turns, chained=False, columns=None):
        self.turns, self.chained, self.at = turns, chained, columns
        rows4 = D // 2 if columns is not None else send.shape[0]
        self.columns = columns.stop - columns.start if columns is not None else send.shape[1]
        self.r = r = rows4 // 4
        self.partners = ["core", "b"]
        shape = (r, self.columns)
        self.args = [] if columns is not None else [keep, send]
        self.specs = [ANY] * len(self.args)
        self.outs = [] if chained else [(sd(*shape, t=bf16), whole(*shape)), (sd(*shape), whole(*shape))]
        self.scratch = [pltpu.VMEM((2 * r, self.columns), bf16), pltpu.VMEM((2 * r, self.columns), bf16),
                        pltpu.VMEM((4 * r, self.columns), bf16), DMA((7,))]
        if chained:
            self.scratch += [pltpu.VMEM(shape, bf16), pltpu.VMEM(shape, f32)]
        if columns is None:
            self.scratch += [pltpu.VMEM((4 * r, self.columns), bf16)]

    def bind(self, args, outs, scratch):
        self.away1, self.got1, self.got0, self.sem = scratch[:4]
        rest = scratch[4:]
        if self.chained:
            self.away2, self.own2 = rest[:2]
            rest = rest[2:]
        else:
            self.away2, self.own2 = outs
        if self.at is None:
            self.keep_from, self.send = args
            self.keep = rest[0]

    def use(self, keep, send, sums):
        self.keep, self.send = keep.at[:, self.at], send.at[:, self.at]

    def load(self):
        return pltpu.make_async_copy(self.keep_from, self.keep, self.sem.at[4])

    def first(self, half):
        at = pl.ds(2 * self.r * half, 2 * self.r)
        k = 5 if half == 0 else 0
        return remote(self.send.at[at, :], self.got0.at[at, :], self.sem.at[k], self.sem.at[k + 1], "core")

    def second(self):
        return remote(self.away1, self.got1, self.sem.at[2], self.sem.at[3], "b")

    def turn(self, i):
        r = self.r
        if i == self.turns[0]:
            self.first(1).start()
            if self.at is None:
                self.load().start()
            self.first(0).start()
        if i == self.turns[1]:
            if self.at is None:
                self.load().wait()
            self.first(1).wait()
            for at in strips(self.columns):
                self.away1[:, at] = self.keep[2 * r :, at] + self.got0[2 * r :, at]
            self.second().start()
        if i == self.turns[2]:
            self.first(0).wait()
            self.second().wait()
            for at in strips(self.columns):
                for k, out in ((0, self.own2), (1, self.away2)):
                    block = slice(k * r, (k + 1) * r)
                    value = self.keep[block, at].astype(f32) + self.got0[block, at].astype(f32)
                    out[:, at] = (value + self.got1[block, at].astype(f32)).astype(out.dtype)

    def done(self, got):
        self.value = got


class ReduceLast:
    def __init__(self, away, own, turns, inside=None):
        self.turns, self.inside = turns, inside
        r, columns = (inside.r, inside.columns) if inside else away.shape
        size = r // 4
        self.r, self.columns, self.size = r, columns, size
        self.partners = ["a", "z1", "z2", "z3"]
        self.args = [] if inside else [away, own]
        self.specs = [] if inside else [ANY, whole(r, columns)]
        self.outs = [(sd(size, columns), whole(size, columns))]
        self.scratch = [pltpu.VMEM((r, columns), bf16), pltpu.VMEM((4, size, columns), bf16),
                        pltpu.VMEM((4, size, columns), bf16), pltpu.VMEM((4, size, columns), f32), DMA((8,))]

    def bind(self, args, outs, scratch):
        self.got2, self.parts, self.got3, self.sums, self.sem = scratch
        self.out = outs[0]
        self.away, self.own = (self.inside.away2, self.inside.own2) if self.inside else args

    def third(self):
        return remote(self.away, self.got2, self.sem.at[0], self.sem.at[1], "a")

    def last(self):
        near = Near()
        return [
            remote(self.parts.at[near.over(k)], self.got3.at[near.z], self.sem.at[2 * k], self.sem.at[2 * k + 1], f"z{k}")
            for k in (1, 2, 3)]

    def turn(self, i):
        if i == self.turns[0]:
            self.third().start()
        if i == self.turns[1]:
            self.third().wait()
            for at in strips(self.columns):
                value = self.own[:, at] + self.got2[:, at].astype(f32)
                for k in range(4):
                    block = value[k * self.size : (k + 1) * self.size]
                    self.sums[k, :, at] = block
                    self.parts[k, :, at] = block.astype(bf16)
            for copy in self.last():
                copy.start()
        if i == self.turns[2]:
            for copy in self.last():
                copy.wait()
            near = Near()
            for at in strips(self.columns):
                value = self.sums[near.z, :, at]
                for k in (1, 2, 3):
                    value = value + self.got3[near.over(k), :, at].astype(f32)
                self.out[:, at] = value

    def done(self, got):
        self.value = got[0]


class Core:
    def __init__(self, keep, send, turns):
        self.turns = turns
        r, columns = send.shape[0] // 2, send.shape[1]
        self.r, self.columns = r, columns
        self.partners = ["core"]
        self.args, self.specs = [keep, send], [ANY, ANY]
        self.outs = [(sd(r, columns, t=bf16), whole(r, columns))] * 2
        self.scratch = [pltpu.VMEM((2 * r, columns), bf16), pltpu.VMEM((2 * r, columns), bf16), DMA((3,))]

    def bind(self, args, outs, scratch):
        self.keep_from, self.send = args
        self.away, self.own = outs
        self.keep, self.got, self.sem = scratch

    def copies(self):
        return [pltpu.make_async_copy(self.keep_from, self.keep, self.sem.at[2]),
                remote(self.send, self.got, self.sem.at[0], self.sem.at[1], "core")]

    def turn(self, i):
        if i == self.turns[0]:
            for copy in self.copies():
                copy.start()
        if i == self.turns[1]:
            for copy in self.copies():
                copy.wait()
            for at in strips(self.columns):
                self.away[:, at] = self.keep[self.r :, at] + self.got[self.r :, at]
                self.own[:, at] = self.keep[: self.r, at] + self.got[: self.r, at]

    def done(self, got):
        self.value = got


class Plane:
    def __init__(self, away, own, turns, chained=False):
        self.turns, self.chained = turns, chained
        rows2, self.columns = away.shape
        self.r = rows2 // 2
        shape = (self.r, self.columns)
        self.partners = ["b"]
        self.args, self.specs = [away, own], [ANY, whole(rows2, self.columns)]
        self.outs = [] if chained else [(sd(*shape, t=bf16), whole(*shape)), (sd(*shape), whole(*shape))]
        self.scratch = [pltpu.VMEM((rows2, self.columns), bf16), DMA((2,))]
        if chained:
            self.scratch += [pltpu.VMEM(shape, bf16), pltpu.VMEM(shape, f32)]

    def bind(self, args, outs, scratch):
        self.away1, self.own1 = args
        self.got, self.sem = scratch[:2]
        self.away2, self.own2 = scratch[2:] if self.chained else outs

    def copy(self):
        return remote(self.away1, self.got, self.sem.at[0], self.sem.at[1], "b")

    def turn(self, i):
        r = self.r
        if i == self.turns[0]:
            self.copy().start()
        if i == self.turns[1]:
            self.copy().wait()
            for at in strips(self.columns):
                for block, out in ((slice(0, r), self.own2), (slice(r, 2 * r), self.away2)):
                    value = self.own1[block, at].astype(f32) + self.got[block, at].astype(f32)
                    out[:, at] = value.astype(out.dtype)

    def done(self, got):
        self.value = got


class Third:
    def __init__(self, away, own, turns, inside=None):
        self.turns, self.inside = turns, inside
        r, columns = (inside.r, inside.columns) if inside else away.shape
        self.columns, self.size = columns, r // 4
        self.partners = ["a"]
        self.args = [] if inside else [away, own]
        self.specs = [] if inside else [ANY, whole(r, columns)]
        shape = (4, self.size, columns)
        self.outs = [(sd(*shape, t=bf16), whole(*shape)), (sd(*shape), whole(*shape))]
        self.scratch = [pltpu.VMEM((r, columns), bf16), DMA((2,))]

    def bind(self, args, outs, scratch):
        self.away, self.own = (self.inside.away2, self.inside.own2) if self.inside else args
        self.parts, self.sums = outs
        self.got, self.sem = scratch

    def copy(self):
        return remote(self.away, self.got, self.sem.at[0], self.sem.at[1], "a")

    def turn(self, i):
        if i == self.turns[0]:
            self.copy().start()
        if i == self.turns[1]:
            self.copy().wait()
            for at in strips(self.columns):
                value = self.own[:, at] + self.got[:, at].astype(f32)
                for k in range(4):
                    block = value[k * self.size : (k + 1) * self.size]
                    self.sums[k, :, at] = block
                    self.parts[k, :, at] = block.astype(bf16)

    def done(self, got):
        self.value = got


class Final:
    def __init__(self, parts, sums, turns):
        self.turns = turns
        _, self.size, self.columns = shape = parts.shape
        self.partners = ["z1", "z2", "z3"]
        self.args, self.specs = [parts, sums], [ANY, whole(*shape)]
        self.outs = [(sd(*shape[1:]), whole(*shape[1:]))]
        self.scratch = [pltpu.VMEM(shape, bf16), DMA((8,))]

    def bind(self, args, outs, scratch):
        self.parts, self.sums = args
        self.out = outs[0]
        self.got, self.sem = scratch

    def copies(self):
        near = Near()
        return [
            remote(self.parts.at[near.over(k)], self.got.at[near.z], self.sem.at[2 * k], self.sem.at[2 * k + 1], f"z{k}")
            for k in (1, 2, 3)]

    def turn(self, i):
        if i == self.turns[0]:
            for copy in self.copies():
                copy.start()
        if i == self.turns[1]:
            for copy in self.copies():
                copy.wait()
            near = Near()
            for at in strips(self.columns):
                value = self.sums[near.z, :, at]
                for k in (1, 2, 3):
                    value = value + self.got[near.over(k), :, at].astype(f32)
                self.out[:, at] = value

    def done(self, got):
        self.value = got[0]


SMALL = 24


class Total:
    def __init__(self, packed, turns):
        self.turns = turns
        self.args, self.specs = [packed], [whole(*packed.shape)]
        shape = packed.shape
        self.outs = [(sd(*shape), whole(*shape))]
        self.scratch = [pltpu.VMEM((5, *shape), f32), pltpu.VMEM((5, *shape), f32), DMA((10,))]
        self.partners = ["core", "x", "y", "z1", "z2"]

    def bind(self, args, outs, scratch):
        self.packed, self.out = args[0], outs[0]
        self.held, self.got, self.sem = scratch

    def use(self, keep, send, sums):
        self.sums = sums

    def copy(self, s):
        return remote(self.held.at[s], self.got.at[s], self.sem.at[2 * s], self.sem.at[2 * s + 1], self.partners[s])

    def turn(self, i):
        for s in range(6):
            if i == self.turns[s]:
                if s:
                    self.copy(s - 1).wait()
                    value = self.held[s - 1] + self.got[s - 1]
                    if s < 5:
                        self.held[s] = value
                    else:
                        self.out[...] = value
                else:
                    self.held[0, :, 0:D] = self.sums[...].T[0:SMALL, :]
                    self.held[0, :, D:] = self.packed[:, D:]
                if s < 5:
                    self.copy(s).start()

    def done(self, got):
        self.value = got[0]


CHUNK = 768
STEPS = FF // CHUNK
SUB = 768


def flip(t, stride):
    return t + stride - 2 * stride * ((t // stride) % 2)


class Order:
    def __init__(self, n):
        self.exact = n == 8
        self.core = 0
        if self.exact:
            self.w = lax.axis_index("wide")
            self.core = self.w % 2

    def target(self, i):
        if not self.exact:
            return i
        other, code = i // 4, i % 4
        t = self.w + other * (1 - 2 * self.core)
        core = t % 2
        if code % 2:
            t = flip(t, 2 + 2 * core)
        if code // 2:
            t = flip(t, 4 - 2 * core)
        return t

    def slot(self, j, other):
        if not self.exact:
            return j
        plane = self.w // 2
        core = self.core if other == 0 else 1 - self.core
        dx, dy = (j + plane) % 2, (j // 2 + plane // 2) % 2
        return dx * (1 + core) + dy * (2 - core)


def exchange(lanes, turns):
    def kernel(hook):
        for i in range(turns):
            hook(i)

    call(kernel, "exchange", [], [], [], [], (), lanes, 0, 10_000_000)


def attention_kernel(sizes, p, x_ref, *rest, hook):
    if p:
        par_ref, *rest = rest
    conv_ref, *rest = rest
    groups, rest = grouped(rest, sizes)
    xl_out, mix_out, lm_ref, *rest = rest
    if not p:
        par_ref, *rest = rest
    (ctx_out, f_out, b_out, a_ref, ns_out, small_ref, xhat_ref, rstd_ref,
     w_ref, vpad_ref, z_ref, sem, xl_ref, mix_ref, ctx_ref, f_ref, b_ref, ns_ref, out_sem, ns_sem, *rest) = rest
    leaving = []

    def leave(src, dst):
        copy = pltpu.make_async_copy(src, dst, out_sem.at[len(leaving)])
        copy.start()
        leaving.append(copy)

    loads = column_loader(groups, sizes, w_ref, sem, 0, 4 * D)
    if not p:
        low_ref, low_sem = rest
        loads += loader(groups[0], low_ref, low_sem, (sizes[0][1], 128))
    for copy in loads:
        copy.start()
    xl_ref[...] = x_ref[...].astype(bf16)
    leave(xl_ref, xl_out)
    vpad_ref[:, 0:LEAD] = jnp.zeros((D, LEAD), bf16)
    vpad_ref[:, LEAD + T :] = jnp.zeros((D, LEAD), bf16)
    hook(0)
    for copy in loads:
        copy.wait()
    if not p:
        par_ref[...] = low_ref[...].astype(f32)
    for part, column in ((0, p), (1, None), (2, p + 1)):

        def mix_step(i, _):
            at = rows(part * D + i * 384, 384)
            got = dot(w_ref[:, at], xl_ref[...], TN)
            if column is not None:
                got = got + par_ref[rows(i * 384, 384), column : column + 1]
            mix_ref[at, :] = got.astype(bf16)
            return 0

        lax.fori_loop(0, 2, mix_step, 0)
        leave(mix_ref.at[pl.ds(part * D, D), :], mix_out.at[pl.ds(part * D, D), :])
        hook(part + 1)
    vpad_ref[:, LEAD : LEAD + T] = mix_ref[2 * D :, :]
    lm_ref[...] = dot(mix_ref[0 : 2 * D, :], segment_mean(), NN).astype(bf16)

    for h in range(HEADS):
        ql = lm_ref[h * HD : (h + 1) * HD, :]
        kl = lm_ref[D + h * HD : D + (h + 1) * HD, :]
        s = dot(ql, kl, TN) * SCALE
        e = jnp.exp(s - jnp.max(s, axis=1, keepdims=True))
        a = e / jnp.sum(e, axis=1, keepdims=True)
        a_ref[h] = a
        z_ref[h] = a.T / jnp.sum(a * a)

    def ns_step(k, _):
        ps, rs = [], []
        for h in range(HEADS):
            z = z_ref[h]
            ns_ref[k, 0, h] = z
            p = dot3(split(a_ref[h]), split(z), NN)
            ns_ref[k, 1, h] = p
            ps.append(split(p))
            rs.append(split(eye(7.0) - p))
        for h in range(HEADS):
            r2 = eye(15.0) - dot3(ps[h], rs[h], NN)
            ns_ref[k, 2, h] = r2
            rs[h] = split(r2)
        for h in range(HEADS):
            r3 = eye(13.0) - dot3(ps[h], rs[h], NN)
            ns_ref[k, 3, h] = r3
            rs[h] = split(r3)
        for h in range(HEADS):
            z_ref[h] = 0.25 * dot3(split(z_ref[h]), rs[h], NN)
        pltpu.make_async_copy(ns_ref.at[k], ns_out.at[k], ns_sem.at[k]).start()
        return 0

    lax.fori_loop(0, NS_ITERS // 2, ns_step, 0)
    hook(4)
    lax.fori_loop(NS_ITERS // 2, NS_ITERS, ns_step, 0)
    hook(5)

    def head_step(h, _):
        base = h * HD
        q = mix_ref[rows(base, HD), :]
        k = mix_ref[rows(D + base, HD), :]
        v = mix_ref[rows(2 * D + base, HD), :]
        ql = lm_ref[rows(base, HD), :]
        kl = lm_ref[rows(D + base, HD), :]
        s = dot(kl, q, TN) * SCALE
        e = jnp.exp(s - jnp.max(s, axis=0, keepdims=True))
        f = (e / jnp.sum(e, axis=0, keepdims=True)).astype(bf16)
        f_ref[rows(base, HD), :] = f
        s = dot(ql, k, TN) * SCALE
        e = jnp.exp(s - jnp.max(s, axis=1, keepdims=True))
        b = (e / jnp.sum(e, axis=1, keepdims=True)).astype(bf16)
        b_ref[rows(base, HD), :] = b
        bv = dot(b, v, NT)
        z = z_ref[h]
        w = dot3(split(z), split(bv), NN)
        small_ref[0, h] = z
        small_ref[1, h] = bv
        small_ref[2, h] = w
        attended = dot(w.astype(bf16), f, TN)
        conv = dot(windows(vpad_ref, base), toeplitz(conv_ref[h, 0:1]), NT)
        ctx_ref[rows(base, HD), :] = (attended + unstack_blocks(conv)).astype(bf16)
        return 0

    for third in range(3):
        lax.fori_loop(third * 4, third * 4 + 4, head_step, 0, unroll=4)
        at = pl.ds(third * 4 * HD, 4 * HD)
        for src, dst in ((f_ref, f_out), (b_ref, b_out), (ctx_ref, ctx_out)):
            leave(src.at[at, :], dst.at[at, :])
        hook(6 + third)

    def out_step(i, _):
        at = rows(i * 384, 384)
        got = dot(w_ref[:, rows(3 * D + i * 384, 384)], ctx_ref[...], TN)
        xhat_ref[at, :] = got + par_ref[at, p + 2 : p + 3] + x_ref[at, :]
        return 0

    lax.fori_loop(0, 2, out_step, 0)
    norm_forward(xhat_ref, xhat_ref, rstd_ref)
    for copy in leaving:
        copy.wait()
    for k in range(NS_ITERS):
        pltpu.make_async_copy(ns_ref.at[k], ns_out.at[k], ns_sem.at[k]).wait()
    for i in range(9, 13):
        hook(i)


def attention(x, groups, par, conv, layer, lanes=(None, ())):
    first = layer == 0
    sizes = sizes_of(groups, layer)
    n = sizes[0][0]
    got = call(
        functools.partial(attention_kernel, sizes, 8 * layer), "attention",
        [sd(D, T, t=bf16), sd(3 * D, T, t=bf16), sd(2 * D, LM, t=bf16)] + [sd(D, 128)] * first
        + [
            sd(D, T, t=bf16), sd(D, T, t=bf16), sd(D, T, t=bf16), sd(HEADS, LM, LM),
            sd(NS_ITERS, 4, HEADS, LM, LM), sd(3, HEADS, LM, LM), sd(D, T), sd(8, T),
        ],
        [vm()] * (2 if first else 3) + anywhere(n * len(groups)),
        [ANY, ANY, vm()] + [vm()] * first + [ANY, ANY, ANY, vm(), ANY, vm(), vm(), vm()],
        [
            pltpu.VMEM((D, 4 * D), bf16), pltpu.VMEM((D, T + 2 * LEAD), bf16), pltpu.VMEM((HEADS, LM, LM), f32),
            DMA((len(groups), n)), pltpu.VMEM((D, T), bf16), pltpu.VMEM((3 * D, T), bf16), pltpu.VMEM((D, T), bf16),
            pltpu.VMEM((D, T), bf16), pltpu.VMEM((D, T), bf16), pltpu.VMEM((NS_ITERS, 4, HEADS, LM, LM), f32),
            DMA((16,)), DMA((NS_ITERS,)),
        ] + [pltpu.VMEM((D, 128), bf16), DMA((n,))] * first,
        (x, *([] if first else [par]), conv, *[piece for g in groups for piece in g]), lanes,
        6_800_000_000, 40_000_000, trans=2_000_000)
    return got if first else [*got[:3], par, *got[3:]]


def feed_kernel(n, p, last, xhat_ref, par_ref, inb_ref, *rest, hook):
    pieces1, pieces2, rest = rest[:n], rest[n : 2 * n], rest[2 * n :]
    a_ref, g_ref, xhat2_ref, rstd2_ref, next_ref, w1_ref, w2_ref, hl_ref, sem = rest
    j = pl.program_id(0)

    @pl.when(j == 0)
    def _():
        loads = loader(pieces1, w1_ref, sem.at[0])
        for copy in loads:
            copy.start()
        later = loader(pieces2, w2_ref, sem.at[1])
        for copy in later:
            copy.start()
        hook(0)
        h = xhat_ref[...] * par_ref[:, p + 6 : p + 7] + par_ref[:, p + 3 : p + 4]
        hl_ref[...] = h.astype(bf16)
        xhat2_ref[...] = h + par_ref[:, p + 4 : p + 5]
        for copy in loads + later:
            copy.wait()

    u = dot(w1_ref[:, rows(j * CHUNK, CHUNK)], hl_ref[...], TN)
    u = u + inb_ref[rows(j * CHUNK, CHUNK), 0:1]
    cdf = 0.5 + 0.5 * lax.erf(u * (2.0 ** -0.5))
    pdf = jnp.exp(-0.5 * u * u) * ((2.0 * np.pi) ** -0.5)
    a_ref[...] = (u * cdf).astype(bf16)
    g_ref[...] = (cdf + u * pdf).astype(bf16)
    xhat2_ref[...] += dot(w2_ref[rows(j * CHUNK, CHUNK), :], a_ref[...], TN)

    @pl.when(j == STEPS - 1)
    def _():
        norm_forward(xhat2_ref, xhat2_ref, rstd2_ref)
        y = xhat2_ref[...] * par_ref[:, p + 7 : p + 8] + par_ref[:, p + 5 : p + 6]
        if last:
            next_ref[...] = y.T.astype(bf16)
        else:
            next_ref[...] = y

    for i in range(STEPS):

        @pl.when(j == i)
        def _():
            hook(i + 1)

    @pl.when(j == STEPS - 1)
    def _():
        hook(STEPS + 1)


def feed(xhat, pieces1, pieces2, par, inb, layer, last, lanes=(None, ())):
    n = len(pieces1)
    chunk = pl.BlockSpec((CHUNK, T), lambda j: (j, 0))
    next_shape = (T, D) if last else (D, T)
    return call(
        functools.partial(feed_kernel, n, 8 * layer, last), "feed",
        [sd(FF, T, t=bf16), sd(FF, T, t=bf16), sd(D, T), sd(8, T), sd(*next_shape, t=bf16 if last else f32)],
        [whole(D, T), whole(D, 128), whole(FF, 1)] + anywhere(2 * n),
        [chunk, chunk, whole(D, T), whole(8, T), whole(*next_shape)],
        [pltpu.VMEM((D, FF), bf16), pltpu.VMEM((FF, D), bf16), pltpu.VMEM((D, T), bf16), DMA((2, n))],
        (xhat, par, inb, *pieces1, *pieces2), lanes, 9_800_000_000, 40_000_000, (STEPS,), 6_000_000)


def norm_backward(dy_ref, xhat_ref, rstd_ref, gain, out_ref, grads_ref, gain_col, shift_col, width=128):
    total_gain = jnp.zeros((D, width), f32)
    total_shift = jnp.zeros((D, width), f32)
    for c in range(0, T, width):
        dy = dy_ref[:, c : c + width]
        xhat = xhat_ref[:, c : c + width]
        total_shift = total_shift + dy
        total_gain = total_gain + dy * xhat
        dxhat = dy * gain
        m1 = jnp.mean(dxhat, axis=0, keepdims=True)
        m2 = jnp.mean(dxhat * xhat, axis=0, keepdims=True)
        out_ref[:, c : c + width] = rstd_ref[0:1, c : c + width] * (dxhat - m1 - xhat * m2)
    grads_ref[:, gain_col : gain_col + 1] = jnp.sum(total_gain, axis=1, keepdims=True)
    grads_ref[:, shift_col : shift_col + 1] = jnp.sum(total_shift, axis=1, keepdims=True)


def lane_sum(value):
    return jnp.sum(value.astype(f32), axis=1, keepdims=True)


def permute_rows(dst_ref, src_ref, order, block):
    for i in range(D // block):
        dst_ref[i * block : (i + 1) * block, :] = src_ref[
            rows(order.target(i) * block, block), :]


def hidden_kernel(n, p, first, sums_in, dy_ref, xhat_ref, rstd_ref, par_ref, a_ref, g_ref, *rest, hook):
    order = Order(n)
    pieces, (keep_ref, send_ref, du_ref, dr_ref, cols_ref, w_ref, dz_ref, inb_ref, sem) = rest[:n], rest[n:]
    j = pl.program_id(0)

    @pl.when(j == 0)
    def _():
        loads = loader(pieces, w_ref, sem)
        for copy in loads:
            copy.start()
        hook(0)
        if first:
            dr_ref[...] = dy_ref[...].astype(f32).T
            dy = dr_ref
        else:
            dy = dy_ref
        cols_ref[...] = sums_in[...]
        norm_backward(dy, xhat_ref, rstd_ref, par_ref[:, p + 7 : p + 8], dr_ref, cols_ref, p + 7, p + 5)
        dz_ref[...] = dr_ref[...].astype(bf16)
        cols_ref[:, p + 4 : p + 5] = lane_sum(dz_ref[...])
        hook(1)
        for copy in loads:
            copy.wait()

    def du_step(i, _):
        base = i * SUB
        da = dot(w_ref[rows(j * CHUNK + base, SUB), :], dz_ref[...], NN)
        du = (da * g_ref[rows(base, SUB), :].astype(f32)).astype(bf16)
        du_ref[rows(base, SUB), :] = du
        inb_ref[rows(base, SUB), :] = lane_sum(du)
        return 0

    lax.fori_loop(0, CHUNK // SUB, du_step, 0)
    half = CHUNK // 2
    core = order.core

    def own(start):
        return a_ref[rows(start, half), :]

    keep_ref[order.slot(j, 0)] = dot(own(core * half), dz_ref[...], NT).astype(bf16)
    send_ref[order.slot(j, 1)] = dot(own((1 - core) * half), dz_ref[...], NT).astype(bf16)
    for i in range(STEPS):

        @pl.when(j == i)
        def _():
            column = 2 * 8 + p // 2 + i
            cols_ref[:, column : column + 1] = inb_ref[...]
            hook(i + 2)


def hidden(sums, dy, xhat, rstd, par, a, g, pieces, layer, first, lanes=(None, ())):
    n = len(pieces)
    chunk = pl.BlockSpec((CHUNK, T), lambda j: (j, 0))
    half = CHUNK // 2
    return call(
        functools.partial(hidden_kernel, n, 8 * layer, first), "hidden",
        [
            sd(STEPS, half, D, t=bf16), sd(STEPS, half, D, t=bf16), sd(FF, T, t=bf16), sd(D, T), sd(D, 128),
        ],
        [whole(D, 128), whole(*dy.shape), whole(D, T), whole(8, T), whole(D, 128), chunk, chunk] + anywhere(n),
        [
            whole(STEPS, half, D), whole(STEPS, half, D), chunk, whole(D, T), whole(D, 128),
        ],
        [pltpu.VMEM((FF, D), bf16), pltpu.VMEM((D, T), bf16), pltpu.VMEM((CHUNK, 1), f32), pltpu.SemaphoreType.DMA((n,))],
        (sums, dy, xhat, rstd, par, a, g, *pieces), lanes, 9_700_000_000, 40_000_000, (STEPS,))


def inner_kernel(n, p, sums_in, du_ref, dr_ref, xhat_ref, rstd_ref, par_ref, *rest, hook):
    order = Order(n)
    pieces, (keep_ref, send_ref, out_ref, cols_ref, w_ref, hl_ref, acc_ref, sem) = rest[:n], rest[n:]
    j = pl.program_id(0)

    @pl.when(j == 0)
    def _():
        loads = loader(pieces, w_ref, sem)
        for copy in loads:
            copy.start()
        hook(0)
        block = D // 8
        for i in range(8):
            at = rows(order.target(i) * block, block)
            hl_ref[i * block : (i + 1) * block, :] = (
                xhat_ref[at, :] * par_ref[at, p + 6 : p + 7] + par_ref[at, p + 3 : p + 4]).astype(bf16)
        acc_ref[...] = dr_ref[...]
        for copy in loads:
            copy.wait()

    for i, ref in enumerate((keep_ref, send_ref)):
        ref[...] = dot(hl_ref[i * (D // 2) : (i + 1) * (D // 2), :], du_ref[...], NT).astype(bf16)

    def dh_step(i, _):
        acc_ref[rows(i * SUB, SUB), :] += dot(
            w_ref[rows(i * SUB, SUB), rows(j * CHUNK, CHUNK)], du_ref[...], NN)
        return 0

    lax.fori_loop(0, D // SUB, dh_step, 0)

    @pl.when(j == STEPS - 1)
    def _():
        cols_ref[...] = sums_in[...]
        norm_backward(acc_ref, xhat_ref, rstd_ref, par_ref[:, p + 6 : p + 7], out_ref, cols_ref, p + 6, p + 3)
        cols_ref[:, p + 2 : p + 3] = lane_sum(out_ref[...].astype(bf16))
    for i in range(STEPS):

        @pl.when(j == i)
        def _():
            hook(i + 1)


def inner(sums, du, dr, xhat, rstd, par, pieces, layer, lanes=(None, ())):
    n = len(pieces)
    return call(
        functools.partial(inner_kernel, n, 8 * layer), "inner",
        [sd(D // 2, FF, t=bf16), sd(D // 2, FF, t=bf16), sd(D, T), sd(D, 128)],
        [whole(D, 128), pl.BlockSpec((CHUNK, T), lambda j: (j, 0)), whole(D, T), whole(D, T), whole(8, T), whole(D, 128)]
        + anywhere(n),
        [
            pl.BlockSpec((D // 2, CHUNK), lambda j: (0, j)), pl.BlockSpec((D // 2, CHUNK), lambda j: (0, j)),
            whole(D, T), whole(D, 128),
        ],
        [pltpu.VMEM((D, FF), bf16), pltpu.VMEM((D, T), bf16), pltpu.VMEM((D, T), f32), pltpu.SemaphoreType.DMA((n,))],
        (sums, du, dr, xhat, rstd, par, *pieces), lanes, 9_700_000_000, 35_000_000, (STEPS,))


def row_loader(src, dst, order, sem):
    block = D // 8
    return [
        pltpu.make_async_copy(
            src.at[rows(order.target(i) * block, block), :], dst.at[pl.ds(i * block, block), :], sem.at[i])
        for i in range(8)]


def values_kernel(sizes, p, small_in, sums_in, dr1_ref, mix_from, ctx_from, f_from, b_from, xl_from, small_ref, conv_ref,
                  *rest, hook):
    order = Order(sizes[0][0])
    groups, rest = grouped(rest, sizes)
    (keep_ref, send_ref, dctx_out, dv_ref, dz_ref, dbv_ref, small_out, cols_ref,
     w_ref, dp_ref, perm_ref, vpad_ref, dpad_ref, dctx_ref, f_ref, b_ref, v_ref, xperm_ref, taps_ref,
     sem, perm_sem, late_sem) = rest
    early = column_loader(groups, sizes, w_ref, sem, 3 * D, 4 * D)
    perms = row_loader(ctx_from, perm_ref, order, perm_sem.at[0])
    late = [pltpu.make_async_copy(mix_from.at[pl.ds(2 * D, D), :], v_ref, late_sem.at[0]),
            pltpu.make_async_copy(f_from, f_ref, late_sem.at[1]),
            pltpu.make_async_copy(b_from, b_ref, late_sem.at[2])]
    last = row_loader(xl_from, xperm_ref, order, perm_sem.at[1])
    for copy in early + perms + late + last:
        copy.start()
    for ref in (vpad_ref, dpad_ref):
        ref[:, 0:LEAD] = jnp.zeros((D, LEAD), bf16)
        ref[:, LEAD + T :] = jnp.zeros((D, LEAD), bf16)
    dp_ref[...] = dr1_ref[...].astype(bf16)
    hook(0)
    for copy in early:
        copy.wait()

    def dctx_step(i, _):
        at = rows(i * 384, 384)
        got = dot(w_ref[at, :], dp_ref[...], NN).astype(bf16)
        dctx_ref[at, :] = got
        dpad_ref[at, LEAD : LEAD + T] = got
        return 0

    lax.fori_loop(0, 2, dctx_step, 0)
    hook(1)
    leave = pltpu.make_async_copy(dctx_ref, dctx_out, late_sem.at[3])
    leave.start()
    for copy in perms:
        copy.wait()
    for i, ref in enumerate((keep_ref, send_ref)):
        ref[:, 0:D] = dot(perm_ref[i * (D // 2) : (i + 1) * (D // 2), :], dp_ref[...], NT).astype(bf16)
    for copy in late:
        copy.wait()
    vpad_ref[:, LEAD : LEAD + T] = v_ref[...]
    hook(2)
    flip = jnp.where(
        lax.broadcasted_iota(jnp.int32, (CONV_N, CONV_N), 0)
        + lax.broadcasted_iota(jnp.int32, (CONV_N, CONV_N), 1) == CONV_N - 1, 1.0, 0.0).astype(bf16)

    def value_step(h, _):
        base = h * HD
        dctx = dctx_ref[rows(base, HD), :]
        f = f_ref[rows(base, HD), :]
        dw = split(dot(f, dctx, NT))
        dz_ref[h] = dot3(dw, split(small_ref[1, h]), NT)
        dbv = dot3(split(small_ref[0, h]), dw, TN).astype(bf16)
        dbv_ref[h] = dbv
        dv = dot(dbv, b_ref[rows(base, HD), :], TN)
        conv = dot(windows(dpad_ref, base), toeplitz(conv_ref[h, 1:2]), NT)
        dv_ref[rows(base, HD), :] = (dv + unstack_blocks(conv)).astype(bf16)
        flipped = dot(stack_blocks(dctx), flip, NN).astype(bf16)
        g = dot(flipped, windows(vpad_ref, base), TN)
        g = pltpu.roll(g, CONV_K - CONV_N + 1 - (LEAD - RADIUS), 1, stride=1, stride_axis=0)
        taps_ref[pl.ds(h, 1), :] = jnp.sum(g[:, 0:128], axis=0, keepdims=True)
        return 0

    lax.fori_loop(0, HEADS // 2, value_step, 0, unroll=2)
    hook(3)
    lax.fori_loop(HEADS // 2, HEADS, value_step, 0, unroll=2)
    hook(4)
    for copy in last:
        copy.wait()
    for i, ref in enumerate((keep_ref, send_ref)):
        ref[:, D:] = dot(xperm_ref[i * (D // 2) : (i + 1) * (D // 2), :], dv_ref[...], NT).astype(bf16)
    cols_ref[...] = sums_in[...]
    cols_ref[:, p + 1 : p + 2] = lane_sum(dv_ref[...])
    first = p // 8 * HEADS
    small_out[...] = small_in[...]
    small_out[:, 0:D] = cols_ref[...].T[0:SMALL, :]
    small_out[first : first + HEADS, D:] = taps_ref[...]
    leave.wait()
    hook(5)


def values(total, sums, dr1, mix, ctx, f, b, xl, small, conv, groups, layer, lanes=(None, ())):
    sizes = sizes_of(groups, layer)
    n = sizes[0][0]
    return call(
        functools.partial(values_kernel, sizes, 8 * layer), "values",
        [
            sd(D // 2, 2 * D, t=bf16), sd(D // 2, 2 * D, t=bf16), sd(D, T, t=bf16), sd(D, T, t=bf16),
            sd(HEADS, LM, LM), sd(HEADS, LM, LM, t=bf16), sd(SMALL, D + 128), sd(D, 128),
        ],
        [vm(), vm(), vm()] + [ANY] * 5 + [vm(), vm()] + anywhere(n * len(groups)),
        [vm(), vm(), ANY] + [vm()] * 5,
        [
            pltpu.VMEM((D, D), bf16), pltpu.VMEM((D, T), bf16), pltpu.VMEM((D, T), bf16),
            pltpu.VMEM((D, T + 2 * LEAD), bf16), pltpu.VMEM((D, T + 2 * LEAD), bf16),
        ] + [pltpu.VMEM((D, T), bf16)] * 5 + [pltpu.VMEM((HEADS, 128), f32), DMA((len(groups), n)), DMA((2, 8)), DMA((4,))],
        (total, sums, dr1, mix, ctx, f, b, xl, small, conv, *[piece for g in groups for piece in g]), lanes,
        6_200_000_000, 25_000_000)


QK = 2 * D
QK_HEADS = ((0, 8), (8, 4))
TURNS = 20


def back_kernel(sizes, p, out, tail, sums_in, ns_from, mix_from, dctx_from, f_from, b_from, dv_from, xl_from, dr1_from,
                lm_ref, a_ref, small_ref, dz0_ref, dbv_ref, *rest, hook):
    order = Order(sizes[0][0])
    groups, rest = grouped(rest, sizes)
    if out:
        keep_ref, send_ref, *rest = rest
    dx_ref, cols_ref, *rest = rest
    if not out:
        keep_ref, send_ref, *rest = rest
    (w_ref, ns_ref, mix_ref, dctx_ref, f_ref, b_ref, dv_ref, perm_ref, dr1_ref, dz_ref, da_ref,
     sem, ns_sem, late_sem, perm_sem) = rest

    def load_ns(i):
        return pltpu.make_async_copy(
            ns_from.at[NS_ITERS - 1 - i], ns_ref.at[lax.rem(i, 2)], ns_sem.at[lax.rem(i, 2)])

    load_ns(0).start()
    late = [
        pltpu.make_async_copy(src, dst, late_sem.at[i]) for i, (src, dst) in enumerate((
            (mix_from, mix_ref), (dctx_from, dctx_ref), (f_from, f_ref), (b_from, b_ref), (dv_from, dv_ref),
            (dr1_from, dr1_ref)))]
    late += row_loader(xl_from, perm_ref, order, perm_sem)
    late += column_loader(groups, sizes, w_ref, sem, 0, 3 * D)
    for lane in tail:
        lane.use(keep_ref, send_ref, cols_ref)
    for copy in late:
        copy.start()
    hook(0)
    for h in range(HEADS):
        da_ref[h] = jnp.zeros((LM, LM), f32)
        dz_ref[h] = dz0_ref[h]

    def ns_step(i, _):
        k = lax.rem(i, 2)
        load_ns(i).wait()

        @pl.when(i + 1 < NS_ITERS)
        def _():
            load_ns(i + 1).start()

        d3, dzs, dps, d2 = [], [], [], []
        for h in range(HEADS):
            dzn = split(0.25 * dz_ref[h])
            d3.append(split(dot3(split(ns_ref[k, 0, h]), dzn, TN)))
            dz_ref[h] = dot3(dzn, split(ns_ref[k, 3, h]), NT)
        for h in range(HEADS):
            p = split(ns_ref[k, 1, h])
            d2.append(split(-dot3(p, d3[h], TN)))
            dps.append(dot3(d3[h], split(ns_ref[k, 2, h]), NT))
        for h in range(HEADS):
            p = ns_ref[k, 1, h]
            d1 = dot3(split(p), d2[h], TN)
            dp = d1 - dps[h] - dot3(d2[h], split(eye(7.0) - p), NT)
            dps[h] = split(dp)
        for h in range(HEADS):
            da_ref[h] += dot3(dps[h], split(ns_ref[k, 0, h]), NT)
            dz_ref[h] += dot3(split(a_ref[h]), dps[h], TN)
        return 0

    lax.fori_loop(0, NS_ITERS // 2, ns_step, 0)
    hook(1)
    lax.fori_loop(NS_ITERS // 2, NS_ITERS, ns_step, 0)
    for copy in late:
        copy.wait()
    hook(2)
    spread = segment_spread()

    def score_step(h, _):
        base = h * HD
        a = a_ref[h]
        dz0 = dz_ref[h].T
        s = 1.0 / jnp.sum(a * a)
        da = da_ref[h] + s * dz0 - (2.0 * s * s * jnp.sum(dz0 * a)) * a
        dsa = (SCALE * a * (da - jnp.sum(a * da, axis=1, keepdims=True))).astype(bf16)
        ql = lm_ref[rows(base, HD), :]
        kl = lm_ref[rows(D + base, HD), :]
        q = mix_ref[rows(base, HD), :]
        k = mix_ref[rows(D + base, HD), :]
        f = f_ref[rows(base, HD), :].astype(f32)
        df = dot(small_ref[2, h].astype(bf16), dctx_ref[rows(base, HD), :], NN)
        dsf = (SCALE * f * (df - jnp.sum(f * df, axis=0, keepdims=True))).astype(bf16)
        b = b_ref[rows(base, HD), :].astype(f32)
        db = dot(dbv_ref[h], mix_ref[rows(2 * D + base, HD), :], NN)
        dsb = (SCALE * b * (db - jnp.sum(b * db, axis=1, keepdims=True))).astype(bf16)
        dkl = dot(q, dsf, NT) + dot(ql, dsa, NN)
        dql = dot(kl, dsa, NT) + dot(k, dsb, NT)
        dq = dot(kl, dsf, NN) + dot((dql * (1.0 / SEG)).astype(bf16), spread, NN)
        dk = dot(ql, dsb, NN) + dot((dkl * (1.0 / SEG)).astype(bf16), spread, NN)
        mix_ref[rows(base, HD), :] = dq.astype(bf16)
        mix_ref[rows(D + base, HD), :] = dk.astype(bf16)
        return 0

    half = D // 2
    at = 0
    for part, (head, heads) in enumerate(QK_HEADS):
        middle = head + heads // 2
        lax.fori_loop(head, middle, score_step, 0, unroll=heads // 2)
        hook(3 + 2 * part)
        lax.fori_loop(middle, head + heads, score_step, 0, unroll=heads // 2)
        if head + heads == HEADS:
            cols_ref[...] = sums_in[...]
            cols_ref[:, p : p + 1] = lane_sum(mix_ref[0:D, :])
        width = heads * HD
        for k in range(2):
            d = mix_ref[k * D + head * HD : k * D + head * HD + width, :]
            for side, ref in ((1, send_ref), (0, keep_ref)):
                mine = perm_ref[side * half : (side + 1) * half, :]
                ref[:, at : at + width] = dot(mine, d, NT).astype(bf16)
            at += width
        hook(4 + 2 * part)
    for i in range(3):
        at = slice(i * 256, (i + 1) * 256)
        got = dr1_ref[at, :] + dot(w_ref[at, 0:QK], mix_ref[0:QK, :], NN) + dot(w_ref[at, QK:], dv_ref[...], NN)
        if p:
            dx_ref[at, :] = got
        else:
            dx_ref[:, at] = got.T
        hook(7 + i)
    for i in range(10, TURNS):
        hook(i)


def back(sums, ns, mix, dctx, f, b, dv, xl, dr1, lm, a, small, dz0, dbv, groups, layer, lanes=(None, ()), tail=(), on=False):
    sizes = sizes_of(groups, layer)
    n = sizes[0][0]
    halves = [(D // 2, QK)] * 2
    out = 0 if on and layer == 0 else 1
    got = call(
        functools.partial(back_kernel, sizes, 8 * layer, out, tail), "back",
        [sd(*h, t=bf16) for h in halves] * out + [sd(*((D, T) if layer else (T, D))), sd(D, 128)],
        [vm()] + [ANY] * 8 + [vm()] * 5 + anywhere(n * len(groups)), [vm()] * (2 + 2 * out),
        [pltpu.VMEM(h, bf16) for h in halves] * (1 - out) + [
            pltpu.VMEM((D, 3 * D), bf16), pltpu.VMEM((2, 4, HEADS, LM, LM), f32), pltpu.VMEM((3 * D, T), bf16),
        ] + [pltpu.VMEM((D, T), bf16)] * 5 + [
            pltpu.VMEM((D, T), f32), pltpu.VMEM((HEADS, LM, LM), f32), pltpu.VMEM((HEADS, LM, LM), f32),
            DMA((len(groups), n)), DMA((2,)), DMA((6,)), DMA((8,)),
        ],
        (sums, ns, mix, dctx, f, b, dv, xl, dr1, lm, a, small, dz0, dbv, *[piece for g in groups for piece in g]),
        lanes, 10_000_000_000, 50_000_000)
    return got if out else [None, None, *got]


class Ring:
    def __init__(self, wide, narrow):
        self.wide, self.narrow = wide, narrow
        self.bits = wide.bit_length() - 1
        up = list(range(1, self.bits))
        self.gather_order = (up, up[::-1])
        self.scatter_order = (up[::-1], up)
        self.exact = wide == 8 and narrow == 4

    def pairs(self, flip):
        n = self.narrow
        out = []
        for w in range(self.wide):
            for z in range(n):
                to_w, to_z = flip(w, z)
                out.append((w * n + z, to_w * n + to_z))
        return out

    def narrow_pairs(self, k):
        return self.pairs(lambda w, z: (w, z ^ k))

    def step_pairs(self, order, s):
        return self.pairs(lambda w, z: (w ^ (1 << order[w & 1][s]), z))

    def core_pairs(self):
        return self.pairs(lambda w, z: (w ^ 1, z))

    def gathered(self, w):
        out = []
        for other in (0, 1):
            v = w ^ other
            for code in range(self.wide // 2):
                t = v
                for s in range(self.bits - 1):
                    if code >> s & 1:
                        t ^= 1 << self.gather_order[v & 1][s]
                out.append(t)
        return out

    def slots(self, w):
        out = []
        for other in (0, 1):
            v = w ^ other
            for code in range(self.wide // 2):
                t = v
                for s in range(self.bits - 1):
                    if code >> (self.bits - 2 - s) & 1:
                        t ^= 1 << self.scatter_order[v & 1][s]
                out.append(t)
        return out

    def mine(self, table):
        return lax.dynamic_index_in_dim(jnp.asarray(table), lax.axis_index("wide"), 0, keepdims=False)

    def gather(self, shard):
        z = lax.axis_index("narrow")
        parts = [shard] + [lax.ppermute(shard, AXES, self.narrow_pairs(k)) for k in range(1, self.narrow)]
        yield []
        bit = 1
        while bit < self.narrow:
            swap = (z & bit) != 0
            parts = [jnp.where(swap, parts[k ^ bit], parts[k]) for k in range(self.narrow)]
            bit *= 2
        held = [jnp.concatenate(parts, axis=0)]
        got = held
        for s in range(self.bits - 1):
            pairs = self.step_pairs(self.gather_order, s)
            fresh, got = got, [lax.ppermute(h, AXES, pairs) for h in held]
            held = held + got
            yield fresh
        other = [lax.ppermute(h, AXES, self.core_pairs()) for h in held]
        yield got
        held = held + other
        return held if self.exact else [self.join(held)]

    def join(self, pieces):
        inverse = np.stack([np.argsort(self.gathered(w)) for w in range(self.wide)]).astype(np.int32)
        stacked = jnp.stack(pieces)
        return jnp.take(stacked, self.mine(inverse), axis=0).reshape(-1, stacked.shape[-1])

    def scatter(self, keep, send):
        half = self.wide // 2
        if not self.exact:
            slots = np.stack([self.slots(w) for w in range(self.wide)]).astype(np.int32)
            whole = jnp.concatenate([keep, send], axis=0)
            whole = whole.reshape(self.wide, -1, whole.shape[-1])
            whole = jnp.take(whole, self.mine(slots), axis=0)
            keep, send = whole[:half], whole[half:]
        got = lax.ppermute(send, AXES, self.core_pairs())
        yield [send]
        total = keep.astype(f32) + got.astype(f32)
        for s in range(self.bits - 1):
            half //= 2
            away = total[half:].astype(bf16)
            got = lax.ppermute(away, AXES, self.step_pairs(self.scatter_order, s))
            yield [away]
            total = total[:half] + got.astype(f32)
        total = total[0]
        size = total.shape[0] // self.narrow
        z = lax.axis_index("narrow")
        own = lax.dynamic_slice_in_dim(total, z * size, size, axis=0)
        low = total.astype(bf16)
        parts = [lax.dynamic_slice_in_dim(low, (z ^ k) * size, size, axis=0) for k in range(1, self.narrow)]
        got = [lax.ppermute(parts[k - 1], AXES, self.narrow_pairs(k)) for k in range(1, self.narrow)]
        yield parts
        for part in got:
            own = own + part.astype(f32)
        return own

    def sum(self, keep, send):
        blocks = self.wide // 2
        return finish(self.scatter(
            keep.reshape(blocks, -1, keep.shape[-1]), send.reshape(blocks, -1, send.shape[-1])))

    def total(self, value):
        bit = 1
        while bit < self.narrow:
            value = value + lax.ppermute(value, AXES, self.narrow_pairs(bit))
            bit *= 2
        for s in range(self.bits - 1):
            value = value + lax.ppermute(value, AXES, self.pairs(lambda w, z: (w ^ (2 << s), z)))
        return value + lax.ppermute(value, AXES, self.core_pairs())


def natural_halves(keep, send):
    both = jnp.stack([keep, send], axis=1)
    both = both.reshape(2, -1, both.shape[-1])
    return both[0], both[1]


def conv_rows(conv):
    at = LEAD - RADIUS
    tail = CONV_K - at - KSIZE
    both = jnp.stack([conv, conv[:, ::-1]], axis=1)
    return jnp.pad(both.astype(f32), ((0, 0), (0, 0), (at, tail)))


def finish(steps):
    while True:
        try:
            next(steps)
        except StopIteration as end:
            return end.value


def small_outputs(ring, total, size, hidden_size):
    layers = total.shape[0] // (8 + STEPS)
    here = lax.axis_index("wide") * ring.narrow + lax.axis_index("narrow")
    lines = total[: 8 * layers, :D].reshape(layers, 8, D)
    lines = lax.dynamic_slice_in_dim(lines, here * size, size, axis=2)
    inb = total[8 * layers :, :D].reshape(layers, FF)
    inb = lax.dynamic_slice_in_dim(inb, here * hidden_size, hidden_size, axis=1)
    taps = total[:, D : D + KSIZE].reshape(layers, HEADS, KSIZE)
    return lines[:, :6], lines[:, 6:], inb, taps


def small_shard(in_b, bias_rows, gain_rows):
    layers, size = bias_rows.shape[0], bias_rows.shape[2]
    columns = jnp.concatenate([bias_rows, gain_rows], axis=1).transpose(2, 0, 1).reshape(size, 8 * layers)
    inner_bias = in_b.reshape(layers, size, -1).transpose(1, 0, 2).reshape(size, -1)
    small = jnp.concatenate([columns, inner_bias], axis=1)
    return jnp.pad(small, ((0, 0), (0, 128 - small.shape[1])))


def gather_all(ring, attention_shards, in_w, out2_w):
    layers = in_w.shape[0]
    return (
        [finish(ring.gather(shard)) for shard in attention_shards],
        [finish(ring.gather(in_w[layer])) for layer in range(layers)],
        [finish(ring.gather(out2_w[layer])) for layer in range(layers)],
    )


class Plan:
    def __init__(self):
        self.count = 0

    def lanes(self, *lanes):
        self.count += 1
        return (self.count, list(lanes))


def body(ring, tokens, cotangent, qkv_w, out_w, in_w, in_b, out2_w, bias_rows, gain_rows, conv_w):
    layers = qkv_w.shape[0]
    size = qkv_w.shape[1]
    small = small_shard(in_b, bias_rows, gain_rows)
    plan = Plan()
    none = (None, ())
    on = ring.exact and layers == 2
    x = tokens.T.astype(f32)
    conv = [conv_rows(conv_w[layer]) for layer in range(layers)]
    on_attention, on_feed = [none] * layers, [none] * layers
    qkvo = [jnp.concatenate([qkv_w[layer], out_w[layer]], axis=1) for layer in range(layers)]
    if on:
        s1 = Spread(jnp.concatenate([qkvo[0][:, : 2 * D], small], axis=1), 0, 1)
        s2 = Spread(qkvo[0][:, 2 * D :], 1, 3)
        g1, g2 = Gather(s1), Gather(s2)
        s3 = Spread(in_w[0], 3, 8)
        g3 = Gather(s3)
        m1 = g1.go(a=(1, 2), b=(2, 4), core0=(1, 8), core1=(2, 8), core2=(4, 8))
        m2 = g2.go(apart=1, a=(3, 5), b=(5, 7), core0=(3, 9), core1=(5, 9), core2=(7, 9))
        exchange(plan.lanes(s1, s2, *m1, *m2, s3), 10)
        att = [[g1.pieces(), g2.pieces()], None]
        win, wout = [None] * 2, [None] * 2
        s4, s5 = Spread(out2_w[0], 0, 6), Spread(qkvo[1], 6, 10)
        g4 = Gather(s4)
        m3 = g3.go(a=(0, 4), b=(4, 9), core0=(0, 4), core1=(4, 9), core2=(9, 11))
        m4 = g4.go(apart=1, a=(6, 8), b=(8, 10), core0=(6, 9), core1=(8, 10), core2=(10, 12))
        g5 = Gather(s5)
        m5 = g5.go(a=(10, 12))
        on_attention[0] = plan.lanes(s4, *m3, *m4, s5, *m5)
    else:
        shards = [jnp.concatenate([qkvo[0], small], axis=1)] + qkvo[1:]
        att, win, wout = gather_all(ring, shards, in_w, out2_w)
        att = [[pieces] for pieces in att]

    kept = []
    par = None
    for layer in range(layers):
        final = layer == layers - 1
        xl, mix, lm, par, ctx, f, b, a, ns, sm, xhat1, rstd1 = attention(
            x, att[layer], par, conv[layer], layer, on_attention[layer])
        if on and layer == 0:
            win[0], wout[0] = g3.pieces(), g4.pieces()
            s6, s7 = Spread(in_w[1], 0, 3), Spread(out2_w[1], 3, 5)
            g6, g7 = Gather(s6), Gather(s7)
            m5 = g5.go(b=(0, 3), core0=(0, 3), core1=(0, 3), core2=(3, 5))
            m6 = g6.go(a=(3, 5))
            on_feed[0] = plan.lanes(*m5, s6, s7, *m6)
        if on and layer == 1:
            win[1], wout[1] = g6.pieces(), g7.pieces()
        at = 8 * layers + FF // D * layer
        inb = par[:, at : at + FF // D].reshape(FF, 1)
        act, slope, xhat2, rstd2, x = feed(
            xhat1, win[layer], wout[layer], par, inb, layer, final, on_feed[layer])
        if on and layer == 0:
            att[1] = [g5.pieces()]
            m6 = g6.go(b=(0, 6), core0=(0, 6), core1=(0, 6), core2=(6, 11))
            m7 = g7.go(apart=1, a=(0, 6), b=(6, 10), core0=(0, 6), core1=(6, 10), core2=(10, 12))
            on_attention[1] = plan.lanes(*m6, *m7)
        kept.append((xl, mix, lm, ctx, f, b, a, ns, sm, xhat1, rstd1, act, slope, xhat2, rstd2))
    output = x

    dy = cotangent
    sums = jnp.zeros((D, 128), f32)
    total = jnp.zeros((SMALL, D + 128), f32)
    grads = [{} for _ in range(layers)]
    firsts, thirds, ends = {}, {}, []

    def sum_first(keep, send, turns, layer, place):
        firsts[layer, place] = ReduceFirst(keep, send, turns)
        return firsts[layer, place]

    def sum_third(layer, place, turns):
        thirds[layer, place] = Third(*firsts[layer, place].value, turns)
        return thirds[layer, place]

    def ending(lane, layer, place):
        ends.append((lane, layer, place))
        return lane

    def sum_final(layer, place, turns):
        return ending(Final(*thirds[layer, place].value, turns), layer, place)

    def sum_last(layer, place, turns):
        return ending(ReduceLast(*firsts[layer, place].value, turns), layer, place)

    halves = None
    for layer in reversed(range(layers)):
        xl, mix, lm, ctx, f, b, a, ns, sm, xhat1, rstd1, act, slope, xhat2, rstd2 = kept[layer]
        above = layer + 1 < layers
        lane = none
        if on and above:
            firsts[layer + 1, "ov"] = Plane(*core_ov.value, (0, 5))
            lane = plan.lanes(
                sum_first(*halves, (0, 1, 5), layer + 1, "qk"), firsts[layer + 1, "ov"],
                sum_final(layer + 1, "in", (0, 5)))
        keep, send, du, dr2, sums = hidden(
            sums, dy, xhat2, rstd2, par, act, slope, wout[layer], layer, not above, lane)
        if on:
            out2 = (keep.reshape(-1, D), send.reshape(-1, D))
            if above:
                lane = [
                    sum_first(*out2, (0, 1, 4), layer, "out2"),
                    sum_third(layer + 1, "qk", (0, 3)), sum_third(layer + 1, "ov", (0, 3))]
            else:
                core2 = Core(*out2, (0, 2))
                lane = [core2]
            lane = plan.lanes(*lane)
        else:
            grads[layer]["out2"] = ring.sum(*natural_halves(keep, send))
        keep, send, dr1, sums = inner(sums, du, dr2, xhat1, rstd1, par, win[layer], layer, lane)
        if on:
            core1 = Core(keep, send, (0, 3))
            if above:
                lane = [
                    sum_third(layer, "out2", (0, 5)), sum_first(keep, send, (0, 1, 5), layer, "in"),
                    sum_final(layer + 1, "qk", (0, 5)), sum_final(layer + 1, "ov", (0, 5))]
            else:
                core1 = Core(keep, send, (0, 3))
                firsts[layer, "out2"] = Plane(*core2.value, (0, 5))
                lane = [firsts[layer, "out2"], core1]
            lane = plan.lanes(*lane)
        else:
            grads[layer]["in"] = ring.sum(keep, send)
        keep, send, dctx, dv, dz, dbv, total, sums = values(
            total, sums, dr1, mix, ctx, f, b, xl, sm, conv[layer], att[layer], layer, lane)
        tail = []
        if on:
            if layer:
                core_ov = Core(keep, send, (0, 2))
                lead = Plane(*core1.value, (0, 4), chained=True)
                thirds[layer, "in"] = Third(None, None, (4, 10), inside=lead)
                lane = [sum_last(layer, "out2", (0, 3, 10)), lead, thirds[layer, "in"], core_ov]
            else:
                late = Total(total, (6, 8, 10, 11, 13, 15))
                lane, tail = [late], [late]
                starts = (0, 2 * QK_HEADS[0][1] * HD, QK)
                for part, (go, end) in enumerate((((4, 5, 8), (8, 11, 14)), ((6, 9, 11), (11, 13, 15)))):
                    lead = ReduceFirst(None, None, go, chained=True, columns=slice(starts[part], starts[part + 1]))
                    tail.append(lead)
                    lane = [lead, ending(ReduceLast(None, None, end, inside=lead), 0, f"qk{part}")] + lane
                lead = ReduceFirst(keep, send, (0, 1, 3), chained=True)
                lane += [
                    sum_final(0, "out2", (0, 4)), sum_last(0, "in", (0, 2, 6)), lead,
                    ending(ReduceLast(None, None, (3, 4, 10), inside=lead), 0, "ov")]
            lane = plan.lanes(*lane)
        else:
            grads[layer]["ov"] = ring.sum(keep, send)
        keep, send, dy, sums = back(
            sums, ns, mix, dctx, f, b, dv, xl, dr1, lm, a, sm, dz, dbv, att[layer], layer, lane, tuple(tail), on)
        halves = (keep, send)
        if not on:
            grads[layer]["qk"] = ring.sum(keep, send)
    if on:
        for lane, layer, place in ends:
            grads[layer][place] = lane.value
        grads[0]["qk"] = jnp.concatenate([grads[0]["qk0"], grads[0]["qk1"]], axis=1)
        total = late.value
    else:
        total = ring.total(jnp.concatenate([sums.T[:SMALL], total[:, D:]], axis=1))
    gbias, ggain, ginb, gtaps = small_outputs(ring, total, size, in_b.shape[1])
    first = 2 * QK_HEADS[0][1] * HD
    cut, rest = first // 2, (QK - first) // 2
    stacked = [
        jnp.stack([
            jnp.concatenate([
                g["qk"][:, :cut], g["qk"][:, first : first + rest], g["qk"][:, cut:first], g["qk"][:, first + rest :],
                g["ov"][:, D:]], axis=1) for g in grads]),
        jnp.stack([g["ov"][:, :D] for g in grads]),
        jnp.stack([g["in"] for g in grads]),
        jnp.stack([g["out2"] for g in grads])]
    return (output, dy, stacked[0], stacked[1], stacked[2], ginb, stacked[3], gbias, ggain, gtaps)


def solution(mesh):
    ring = Ring(mesh.shape["wide"], mesh.shape["narrow"])
    rows3 = P(None, AXES, None)
    columns3 = P(None, None, AXES)
    weights = (rows3, rows3, rows3, P(None, AXES), rows3, columns3, columns3, P())
    return jax.shard_map(
        functools.partial(body, ring),
        mesh=mesh,
        in_specs=(P(AXES, None), P(AXES, None)) + weights,
        out_specs=(P(AXES, None), P(AXES, None)) + weights,
        check_vma=False,
    )
```

```python
import functools
import jax
import jax.numpy as jnp
import numpy as np
from jax import lax
from jax.experimental import pallas as pl
from jax.experimental.pallas import tpu as pltpu
from jax.sharding import PartitionSpec as P

D = 768
HEADS = 12
HD = 64
FF = 3072
LM = 64
KSIZE = 33
RADIUS = KSIZE // 2
NS_ITERS = 6
T = 1024
SEG = T // LM
SCALE = HD ** -0.5
EPS = 1e-05
CONV_N = 256
CONV_K = 512
CONV_BLOCKS = T // CONV_N
LEAD = 128
f32 = jnp.float32
bf16 = jnp.bfloat16
AXES = ("wide", "narrow")
NN = (((1,), (0,)), ((), ()))
NT = (((1,), (1,)), ((), ()))
TN = (((0,), (0,)), ((), ()))
VMEM_LIMIT = 60 * 1024 * 1024


def dot(a, b, dims):
    return lax.dot_general(a, b, dims, preferred_element_type=f32)


def split(a):
    high = a.astype(bf16)
    return high, (a - high.astype(f32)).astype(bf16)


def dot3(a, b, dims):
    if dims is NN:
        return dot(a[0], b[0], dims) + (dot(a[0], b[1], dims) + dot(a[1], b[0], dims))
    (i,), (j,) = dims[0]
    return dot(jnp.concatenate([a[0], a[0], a[1]], axis=i), jnp.concatenate([b[0], b[1], b[0]], axis=j), dims)


def rows(start, size):
    if isinstance(start, int):
        return pl.ds(start, size)
    return pl.ds(pl.multiple_of(start, size), size)


def segment_mean():
    token = lax.broadcasted_iota(jnp.int32, (T, LM), 0)
    seg = lax.broadcasted_iota(jnp.int32, (T, LM), 1)
    return jnp.where(token // SEG == seg, 1.0 / SEG, 0.0).astype(bf16)


def segment_spread():
    token = lax.broadcasted_iota(jnp.int32, (LM, T), 1)
    seg = lax.broadcasted_iota(jnp.int32, (LM, T), 0)
    return jnp.where(token // SEG == seg, 1.0, 0.0).astype(bf16)


def eye(value):
    i = lax.broadcasted_iota(jnp.int32, (LM, LM), 0)
    j = lax.broadcasted_iota(jnp.int32, (LM, LM), 1)
    return jnp.where(i == j, value, 0.0).astype(f32)


def toeplitz(row):
    full = jnp.broadcast_to(row, (CONV_N, CONV_K))
    return pltpu.roll(full, 0, 1, stride=1, stride_axis=0).astype(bf16)


def windows(ref, base):
    return jnp.concatenate(
        [ref[rows(base, HD), CONV_N * b : CONV_N * b + CONV_K] for b in range(CONV_BLOCKS)], axis=0
    )


def stack_blocks(value):
    return jnp.concatenate(
        [value[:, CONV_N * b : CONV_N * (b + 1)] for b in range(CONV_BLOCKS)], axis=0
    )


def unstack_blocks(value):
    return jnp.concatenate(
        [value[HD * b : HD * (b + 1), :] for b in range(CONV_BLOCKS)], axis=1
    )


def norm_forward(r_ref, xhat_ref, rstd_ref, width=128):
    for c in range(0, T, width):
        r = r_ref[:, c : c + width]
        center = r - jnp.mean(r, axis=0, keepdims=True)
        rstd = lax.rsqrt(jnp.mean(center * center, axis=0, keepdims=True) + EPS)
        xhat_ref[:, c : c + width] = center * rstd
        rstd_ref[:, c : c + width] = jnp.broadcast_to(rstd, (8, width))


def vm():
    return pl.BlockSpec(memory_space=pltpu.VMEM)


def anywhere(n):
    return [pl.BlockSpec(memory_space=pl.ANY)] * n


def whole(*s):
    return pl.BlockSpec(s, lambda *_: (0,) * len(s))


def sd(*s, t=f32):
    return jax.ShapeDtypeStruct(s, t)


def loader(pieces, dst, sem, columns=None):
    r = pieces[0].shape[0]
    order = Order(len(pieces))
    out = []
    for i, piece in enumerate(pieces):
        src = piece if columns is None else piece.at[:, pl.ds(*columns)]
        at = rows(order.target(i) * r, r)
        out.append(pltpu.make_async_copy(src, dst.at[at, :], sem.at[i]))
    return out


def sizes_of(groups, layer):
    return [(len(g), g[0].shape[1] - (128 if layer == 0 and i == 0 else 0)) for i, g in enumerate(groups)]


def grouped(refs, sizes):
    groups = []
    for n, _ in sizes:
        groups.append(refs[:n])
        refs = refs[n:]
    return groups, refs


def column_loader(groups, sizes, dst, sem, low, high):
    out = []
    at = 0
    for g, (n, width) in enumerate(sizes):
        a, b = max(low, at), min(high, at + width)
        if b > a:
            out += loader(groups[g], dst.at[:, pl.ds(a - low, b - a)], sem.at[g], (a - at, b - a))
        at += width
    return out


def call(kernel, name, out_shape, in_specs, out_specs, scratch, args, lanes, flops, size, grid=None, trans=0):
    identity, lanes = lanes
    ins, outs = len(args), len(out_shape)
    lane_args = [a for lane in lanes for a in lane.args]
    lane_outs = [o for lane in lanes for o in lane.outs]
    lane_scratch = [o for lane in lanes for o in lane.scratch]

    def run(*refs):
        refs = list(refs)

        def take(n):
            got = refs[:n]
            del refs[:n]
            return got

        own = take(ins)
        lane_in = [take(len(lane.args)) for lane in lanes]
        own += take(outs)
        lane_out = [take(len(lane.outs)) for lane in lanes]
        own += take(len(scratch))
        for lane, a, o in zip(lanes, lane_in, lane_out):
            lane.bind(a, o, take(len(lane.scratch)))

        def hook(i):
            if lanes and i == 0:
                near = Near()
                names = sorted({p for lane in lanes for p in lane.partners})
                barrier = pltpu.get_barrier_semaphore()
                for p in names:
                    pl.semaphore_signal(barrier, inc=1, device_id=near.at(p), device_id_type=pl.DeviceIdType.MESH)
                pl.semaphore_wait(barrier, len(names))
            for lane in lanes:
                lane.turn(i)

        kernel(*own, hook=hook)

    params = {"collective_id": identity, "has_side_effects": True} if lanes else {}
    got = pl.pallas_call(
        run,
        out_shape=list(out_shape) + [o for o, _ in lane_outs],
        in_specs=list(in_specs) + [spec for lane in lanes for spec in lane.specs],
        out_specs=list(out_specs) + [spec for _, spec in lane_outs],
        scratch_shapes=list(scratch) + lane_scratch,
        **({} if grid is None else {"grid": grid}),
        compiler_params=pltpu.CompilerParams(vmem_limit_bytes=VMEM_LIMIT, **params),
        cost_estimate=pl.CostEstimate(flops=flops, bytes_accessed=size, transcendentals=trans),
        name=name,
    )(*args, *lane_args)
    own, rest = list(got[:outs]), list(got[outs:])
    for lane in lanes:
        n = len(lane.outs)
        lane.done(rest[:n])
        rest = rest[n:]
    return own


class Near:
    def __init__(self):
        self.w, self.z = lax.axis_index("wide"), lax.axis_index("narrow")

    def over(self, k):
        z = self.z
        if k == 1:
            return z + 1 - 2 * (z % 2)
        if k == 2:
            return z + 2 - 4 * (z // 2)
        return 3 - z

    def at(self, name):
        w, core = self.w, self.w % 2
        if name[0] == "z":
            return (w, self.over(int(name[1])))
        if name == "core":
            return (w + 1 - 2 * core, self.z)
        step = {"a": 2 + 2 * core, "b": 4 - 2 * core, "x": 2, "y": 4}[name]
        return (w + step - 2 * step * ((w // step) % 2), self.z)


def remote(src, dst, send, recv, name):
    return pltpu.make_async_remote_copy(
        src_ref=src, dst_ref=dst, send_sem=send, recv_sem=recv, device_id=Near().at(name),
        device_id_type=pl.DeviceIdType.MESH)


DMA = pltpu.SemaphoreType.DMA
ANY = pl.BlockSpec(memory_space=pl.ANY)


class Move:
    def __init__(self, source, name, start, wait):
        self.chained = not hasattr(source, "dtype")
        self.source, self.name, self.start, self.wait = source, name, start, wait
        self.shape = source.shape
        self.args = [] if self.chained else [source]
        self.specs = [ANY] * len(self.args)
        self.outs = [(sd(*self.shape, t=bf16), ANY)]
        self.scratch = [DMA((2,))]
        self.partners = [name]

    def bind(self, args, outs, scratch):
        self.src = self.source.dst if self.chained else args[0]
        self.dst, self.sem = outs[0], scratch[0]

    def copy(self):
        return remote(self.src, self.dst, self.sem.at[0], self.sem.at[1], self.name)

    def turn(self, i):
        if i == self.wait:
            self.copy().wait()
        if i == self.start:
            self.copy().start()

    def done(self, got):
        self.value = got[0].reshape(-1, self.shape[-1])


class Spread:
    def __init__(self, shard, start, wait):
        self.start, self.wait = start, wait
        self.shape = (4, *shard.shape)
        self.args, self.specs = [shard], [ANY]
        self.outs = [(sd(*self.shape, t=bf16), ANY)]
        self.scratch = [DMA((7,))]
        self.partners = ["z1", "z2", "z3"]

    def bind(self, args, outs, scratch):
        self.src, self.dst, self.sem = args[0], outs[0], scratch[0]

    def copies(self):
        z = lax.axis_index("narrow")
        out = [pltpu.make_async_copy(self.src, self.dst.at[z], self.sem.at[6])]
        for k in (1, 2, 3):
            out.append(remote(self.src, self.dst.at[z], self.sem.at[2 * k - 2], self.sem.at[2 * k - 1], f"z{k}"))
        return out

    def turn(self, i):
        if i == self.wait:
            for copy in self.copies():
                copy.wait()
        if i == self.start:
            for copy in self.copies():
                copy.start()

    def done(self, got):
        self.value = got[0].reshape(-1, self.shape[-1])


class Gather:
    def __init__(self, block):
        self.block, self.moves = block, {}

    def at(self, name):
        if name == "own":
            return self.block
        return self.moves[name]

    def go(self, apart=0, **turns):
        out = []
        fresh = {}
        value = lambda k: fresh[k] if k in fresh else (
            self.moves[k].value if k in self.moves else
            self.block.value if hasattr(self.block, "value") else self.block)
        for key, turn in turns.items():
            if key == "a":
                todo = [("a", "own", "a")]
            elif key == "b":
                todo = [("b0", "own", "b"), ("b1", "a", "b")]
            else:
                todo = {"core0": [("c0", "own", "core")], "core1": [("c1", "a", "core")],
                        "core2": [("c2", "b0", "core"), ("c3", "b1", "core")]}[key]
            for name, source, partner in todo:
                start, wait = turn
                if name == "b1":
                    wait += apart
                if name == "c3":
                    start += apart
                fresh[name] = Move(value(source), partner, start, wait)
                out.append(fresh[name])
        self.moves.update(fresh)
        return sorted(out, key=lambda m: m.start)

    def pieces(self):
        block = self.block.value if hasattr(self.block, "value") else self.block
        return [block] + [self.moves[k].value for k in ("a", "b0", "b1", "c0", "c1", "c2", "c3")]


def strips(columns):
    width = 384 if columns % 384 == 0 else 512 if columns % 512 == 0 else columns
    return [slice(c, c + width) for c in range(0, columns, width)]


class ReduceFirst:
    def __init__(self, keep, send, turns, chained=False, columns=None):
        self.turns, self.chained, self.at = turns, chained, columns
        rows4 = D // 2 if columns is not None else send.shape[0]
        self.columns = columns.stop - columns.start if columns is not None else send.shape[1]
        self.r = r = rows4 // 4
        self.partners = ["core", "b"]
        shape = (r, self.columns)
        self.args = [] if columns is not None else [keep, send]
        self.specs = [ANY] * len(self.args)
        self.outs = [] if chained else [(sd(*shape, t=bf16), whole(*shape)), (sd(*shape), whole(*shape))]
        self.scratch = [pltpu.VMEM((2 * r, self.columns), bf16), pltpu.VMEM((2 * r, self.columns), bf16),
                        pltpu.VMEM((4 * r, self.columns), bf16), DMA((7,))]
        if chained:
            self.scratch += [pltpu.VMEM(shape, bf16), pltpu.VMEM(shape, f32)]
        if columns is None:
            self.scratch += [pltpu.VMEM((4 * r, self.columns), bf16)]

    def bind(self, args, outs, scratch):
        self.away1, self.got1, self.got0, self.sem = scratch[:4]
        rest = scratch[4:]
        if self.chained:
            self.away2, self.own2 = rest[:2]
            rest = rest[2:]
        else:
            self.away2, self.own2 = outs
        if self.at is None:
            self.keep_from, self.send = args
            self.keep = rest[0]

    def use(self, keep, send, sums):
        self.keep, self.send = keep.at[:, self.at], send.at[:, self.at]

    def load(self):
        return pltpu.make_async_copy(self.keep_from, self.keep, self.sem.at[4])

    def first(self, half):
        at = pl.ds(2 * self.r * half, 2 * self.r)
        k = 5 if half == 0 else 0
        return remote(self.send.at[at, :], self.got0.at[at, :], self.sem.at[k], self.sem.at[k + 1], "core")

    def second(self):
        return remote(self.away1, self.got1, self.sem.at[2], self.sem.at[3], "b")

    def turn(self, i):
        r = self.r
        if i == self.turns[0]:
            self.first(1).start()
            if self.at is None:
                self.load().start()
            self.first(0).start()
        if i == self.turns[1]:
            if self.at is None:
                self.load().wait()
            self.first(1).wait()
            for at in strips(self.columns):
                self.away1[:, at] = self.keep[2 * r :, at] + self.got0[2 * r :, at]
            self.second().start()
        if i == self.turns[2]:
            self.first(0).wait()
            self.second().wait()
            for at in strips(self.columns):
                for k, out in ((0, self.own2), (1, self.away2)):
                    block = slice(k * r, (k + 1) * r)
                    value = self.keep[block, at].astype(f32) + self.got0[block, at].astype(f32)
                    out[:, at] = (value + self.got1[block, at].astype(f32)).astype(out.dtype)

    def done(self, got):
        self.value = got


class ReduceLast:
    def __init__(self, away, own, turns, inside=None):
        self.turns, self.inside = turns, inside
        r, columns = (inside.r, inside.columns) if inside else away.shape
        size = r // 4
        self.r, self.columns, self.size = r, columns, size
        self.partners = ["a", "z1", "z2", "z3"]
        self.args = [] if inside else [away, own]
        self.specs = [] if inside else [ANY, whole(r, columns)]
        self.outs = [(sd(size, columns), whole(size, columns))]
        self.scratch = [pltpu.VMEM((r, columns), bf16), pltpu.VMEM((4, size, columns), bf16),
                        pltpu.VMEM((4, size, columns), bf16), pltpu.VMEM((4, size, columns), f32), DMA((8,))]

    def bind(self, args, outs, scratch):
        self.got2, self.parts, self.got3, self.sums, self.sem = scratch
        self.out = outs[0]
        self.away, self.own = (self.inside.away2, self.inside.own2) if self.inside else args

    def third(self):
        return remote(self.away, self.got2, self.sem.at[0], self.sem.at[1], "a")

    def last(self):
        near = Near()
        return [
            remote(self.parts.at[near.over(k)], self.got3.at[near.z], self.sem.at[2 * k], self.sem.at[2 * k + 1], f"z{k}")
            for k in (1, 2, 3)]

    def turn(self, i):
        if i == self.turns[0]:
            self.third().start()
        if i == self.turns[1]:
            self.third().wait()
            for at in strips(self.columns):
                value = self.own[:, at] + self.got2[:, at].astype(f32)
                for k in range(4):
                    block = value[k * self.size : (k + 1) * self.size]
                    self.sums[k, :, at] = block
                    self.parts[k, :, at] = block.astype(bf16)
            for copy in self.last():
                copy.start()
        if i == self.turns[2]:
            for copy in self.last():
                copy.wait()
            near = Near()
            for at in strips(self.columns):
                value = self.sums[near.z, :, at]
                for k in (1, 2, 3):
                    value = value + self.got3[near.over(k), :, at].astype(f32)
                self.out[:, at] = value

    def done(self, got):
        self.value = got[0]


class Core:
    def __init__(self, keep, send, turns):
        self.turns = turns
        r, columns = send.shape[0] // 2, send.shape[1]
        self.r, self.columns = r, columns
        self.partners = ["core"]
        self.args, self.specs = [keep, send], [ANY, ANY]
        self.outs = [(sd(r, columns, t=bf16), whole(r, columns))] * 2
        self.scratch = [pltpu.VMEM((2 * r, columns), bf16), pltpu.VMEM((2 * r, columns), bf16), DMA((3,))]

    def bind(self, args, outs, scratch):
        self.keep_from, self.send = args
        self.away, self.own = outs
        self.keep, self.got, self.sem = scratch

    def copies(self):
        return [pltpu.make_async_copy(self.keep_from, self.keep, self.sem.at[2]),
                remote(self.send, self.got, self.sem.at[0], self.sem.at[1], "core")]

    def turn(self, i):
        if i == self.turns[0]:
            for copy in self.copies():
                copy.start()
        if i == self.turns[1]:
            for copy in self.copies():
                copy.wait()
            for at in strips(self.columns):
                self.away[:, at] = self.keep[self.r :, at] + self.got[self.r :, at]
                self.own[:, at] = self.keep[: self.r, at] + self.got[: self.r, at]

    def done(self, got):
        self.value = got


class Plane:
    def __init__(self, away, own, turns, chained=False):
        self.turns, self.chained = turns, chained
        rows2, self.columns = away.shape
        self.r = rows2 // 2
        shape = (self.r, self.columns)
        self.partners = ["b"]
        self.args, self.specs = [away, own], [ANY, whole(rows2, self.columns)]
        self.outs = [] if chained else [(sd(*shape, t=bf16), whole(*shape)), (sd(*shape), whole(*shape))]
        self.scratch = [pltpu.VMEM((rows2, self.columns), bf16), DMA((2,))]
        if chained:
            self.scratch += [pltpu.VMEM(shape, bf16), pltpu.VMEM(shape, f32)]

    def bind(self, args, outs, scratch):
        self.away1, self.own1 = args
        self.got, self.sem = scratch[:2]
        self.away2, self.own2 = scratch[2:] if self.chained else outs

    def copy(self):
        return remote(self.away1, self.got, self.sem.at[0], self.sem.at[1], "b")

    def turn(self, i):
        r = self.r
        if i == self.turns[0]:
            self.copy().start()
        if i == self.turns[1]:
            self.copy().wait()
            for at in strips(self.columns):
                for block, out in ((slice(0, r), self.own2), (slice(r, 2 * r), self.away2)):
                    value = self.own1[block, at].astype(f32) + self.got[block, at].astype(f32)
                    out[:, at] = value.astype(out.dtype)

    def done(self, got):
        self.value = got


class Third:
    def __init__(self, away, own, turns, inside=None):
        self.turns, self.inside = turns, inside
        r, columns = (inside.r, inside.columns) if inside else away.shape
        self.columns, self.size = columns, r // 4
        self.partners = ["a"]
        self.args = [] if inside else [away, own]
        self.specs = [] if inside else [ANY, whole(r, columns)]
        shape = (4, self.size, columns)
        self.outs = [(sd(*shape, t=bf16), whole(*shape)), (sd(*shape), whole(*shape))]
        self.scratch = [pltpu.VMEM((r, columns), bf16), DMA((2,))]

    def bind(self, args, outs, scratch):
        self.away, self.own = (self.inside.away2, self.inside.own2) if self.inside else args
        self.parts, self.sums = outs
        self.got, self.sem = scratch

    def copy(self):
        return remote(self.away, self.got, self.sem.at[0], self.sem.at[1], "a")

    def turn(self, i):
        if i == self.turns[0]:
            self.copy().start()
        if i == self.turns[1]:
            self.copy().wait()
            for at in strips(self.columns):
                value = self.own[:, at] + self.got[:, at].astype(f32)
                for k in range(4):
                    block = value[k * self.size : (k + 1) * self.size]
                    self.sums[k, :, at] = block
                    self.parts[k, :, at] = block.astype(bf16)

    def done(self, got):
        self.value = got


class Final:
    def __init__(self, parts, sums, turns):
        self.turns = turns
        _, self.size, self.columns = shape = parts.shape
        self.partners = ["z1", "z2", "z3"]
        self.args, self.specs = [parts, sums], [ANY, whole(*shape)]
        self.outs = [(sd(*shape[1:]), whole(*shape[1:]))]
        self.scratch = [pltpu.VMEM(shape, bf16), DMA((8,))]

    def bind(self, args, outs, scratch):
        self.parts, self.sums = args
        self.out = outs[0]
        self.got, self.sem = scratch

    def copies(self):
        near = Near()
        return [
            remote(self.parts.at[near.over(k)], self.got.at[near.z], self.sem.at[2 * k], self.sem.at[2 * k + 1], f"z{k}")
            for k in (1, 2, 3)]

    def turn(self, i):
        if i == self.turns[0]:
            for copy in self.copies():
                copy.start()
        if i == self.turns[1]:
            for copy in self.copies():
                copy.wait()
            near = Near()
            for at in strips(self.columns):
                value = self.sums[near.z, :, at]
                for k in (1, 2, 3):
                    value = value + self.got[near.over(k), :, at].astype(f32)
                self.out[:, at] = value

    def done(self, got):
        self.value = got[0]


SMALL = 24


class Total:
    def __init__(self, packed, turns):
        self.turns = turns
        self.args, self.specs = [packed], [whole(*packed.shape)]
        shape = packed.shape
        self.outs = [(sd(*shape), whole(*shape))]
        self.scratch = [pltpu.VMEM((5, *shape), f32), pltpu.VMEM((5, *shape), f32), DMA((10,))]
        self.partners = ["core", "x", "y", "z1", "z2"]

    def bind(self, args, outs, scratch):
        self.packed, self.out = args[0], outs[0]
        self.held, self.got, self.sem = scratch

    def use(self, keep, send, sums):
        self.sums = sums

    def copy(self, s):
        return remote(self.held.at[s], self.got.at[s], self.sem.at[2 * s], self.sem.at[2 * s + 1], self.partners[s])

    def turn(self, i):
        for s in range(6):
            if i == self.turns[s]:
                if s:
                    self.copy(s - 1).wait()
                    value = self.held[s - 1] + self.got[s - 1]
                    if s < 5:
                        self.held[s] = value
                    else:
                        self.out[...] = value
                else:
                    self.held[0, :, 0:D] = self.sums[...].T[0:SMALL, :]
                    self.held[0, :, D:] = self.packed[:, D:]
                if s < 5:
                    self.copy(s).start()

    def done(self, got):
        self.value = got[0]


CHUNK = 768
STEPS = FF // CHUNK
SUB = 768


def flip(t, stride):
    return t + stride - 2 * stride * ((t // stride) % 2)


class Order:
    def __init__(self, n):
        self.exact = n == 8
        self.core = 0
        if self.exact:
            self.w = lax.axis_index("wide")
            self.core = self.w % 2

    def target(self, i):
        if not self.exact:
            return i
        other, code = i // 4, i % 4
        t = self.w + other * (1 - 2 * self.core)
        core = t % 2
        if code % 2:
            t = flip(t, 2 + 2 * core)
        if code // 2:
            t = flip(t, 4 - 2 * core)
        return t

    def slot(self, j, other):
        if not self.exact:
            return j
        plane = self.w // 2
        core = self.core if other == 0 else 1 - self.core
        dx, dy = (j + plane) % 2, (j // 2 + plane // 2) % 2
        return dx * (1 + core) + dy * (2 - core)


def exchange(tokens, lanes, turns):
    def kernel(tokens_from, x_out, tokens_ref, x_ref, sem, hook):
        load = pltpu.make_async_copy(tokens_from, tokens_ref, sem.at[0])
        load.start()
        hook(0)
        load.wait()
        x_ref[...] = tokens_ref[...].astype(f32).T
        leave = pltpu.make_async_copy(x_ref, x_out, sem.at[1])
        leave.start()
        for i in range(1, turns):
            hook(i)
        leave.wait()

    return call(
        kernel, "exchange", [sd(D, T)], [ANY], [ANY],
        [pltpu.VMEM((T, D), bf16), pltpu.VMEM((D, T), f32), DMA((2,))], (tokens,), lanes, 0, 10_000_000)[0]


def attention_kernel(sizes, p, x_ref, *rest, hook):
    if p:
        par_ref, *rest = rest
    conv_ref, *rest = rest
    groups, rest = grouped(rest, sizes)
    xl_out, mix_out, lm_ref, *rest = rest
    if not p:
        par_ref, *rest = rest
    (ctx_out, f_out, b_out, a_ref, ns_out, small_ref, xhat_ref, rstd_ref,
     w_ref, vpad_ref, z_ref, sem, xl_ref, mix_ref, ctx_ref, f_ref, b_ref, ns_ref, out_sem, ns_sem, *rest) = rest
    leaving = []

    def leave(src, dst):
        copy = pltpu.make_async_copy(src, dst, out_sem.at[len(leaving)])
        copy.start()
        leaving.append(copy)

    loads = column_loader(groups, sizes, w_ref, sem, 0, 4 * D)
    if not p:
        low_ref, low_sem = rest
        loads += loader(groups[0], low_ref, low_sem, (sizes[0][1], 128))
    for copy in loads:
        copy.start()
    xl_ref[...] = x_ref[...].astype(bf16)
    leave(xl_ref, xl_out)
    vpad_ref[:, 0:LEAD] = jnp.zeros((D, LEAD), bf16)
    vpad_ref[:, LEAD + T :] = jnp.zeros((D, LEAD), bf16)
    hook(0)
    for copy in loads:
        copy.wait()
    if not p:
        par_ref[...] = low_ref[...].astype(f32)
    for part, column in ((0, p), (1, None), (2, p + 1)):

        def mix_step(i, _):
            at = rows(part * D + i * 384, 384)
            got = dot(w_ref[:, at], xl_ref[...], TN)
            if column is not None:
                got = got + par_ref[rows(i * 384, 384), column : column + 1]
            mix_ref[at, :] = got.astype(bf16)
            return 0

        lax.fori_loop(0, 2, mix_step, 0)
        leave(mix_ref.at[pl.ds(part * D, D), :], mix_out.at[pl.ds(part * D, D), :])
        hook(part + 1)
    vpad_ref[:, LEAD : LEAD + T] = mix_ref[2 * D :, :]
    lm_ref[...] = dot(mix_ref[0 : 2 * D, :], segment_mean(), NN).astype(bf16)

    for h in range(HEADS):
        ql = lm_ref[h * HD : (h + 1) * HD, :]
        kl = lm_ref[D + h * HD : D + (h + 1) * HD, :]
        s = dot(ql, kl, TN) * SCALE
        e = jnp.exp(s - jnp.max(s, axis=1, keepdims=True))
        a = e / jnp.sum(e, axis=1, keepdims=True)
        a_ref[h] = a
        z_ref[h] = a.T / jnp.sum(a * a)

    def ns_step(k, _):
        ps, rs = [], []
        for h in range(HEADS):
            z = z_ref[h]
            ns_ref[k, 0, h] = z
            p = dot3(split(a_ref[h]), split(z), NN)
            ns_ref[k, 1, h] = p
            ps.append(split(p))
            rs.append(split(eye(7.0) - p))
        for h in range(HEADS):
            r2 = eye(15.0) - dot3(ps[h], rs[h], NN)
            ns_ref[k, 2, h] = r2
            rs[h] = split(r2)
        for h in range(HEADS):
            r3 = eye(13.0) - dot3(ps[h], rs[h], NN)
            ns_ref[k, 3, h] = r3
            rs[h] = split(r3)
        for h in range(HEADS):
            z_ref[h] = 0.25 * dot3(split(z_ref[h]), rs[h], NN)
        pltpu.make_async_copy(ns_ref.at[k], ns_out.at[k], ns_sem.at[k]).start()
        return 0

    lax.fori_loop(0, NS_ITERS // 2, ns_step, 0)
    hook(4)
    lax.fori_loop(NS_ITERS // 2, NS_ITERS, ns_step, 0)
    hook(5)

    def head_step(h, _):
        base = h * HD
        q = mix_ref[rows(base, HD), :]
        k = mix_ref[rows(D + base, HD), :]
        v = mix_ref[rows(2 * D + base, HD), :]
        ql = lm_ref[rows(base, HD), :]
        kl = lm_ref[rows(D + base, HD), :]
        s = dot(kl, q, TN) * SCALE
        e = jnp.exp(s - jnp.max(s, axis=0, keepdims=True))
        f = (e / jnp.sum(e, axis=0, keepdims=True)).astype(bf16)
        f_ref[rows(base, HD), :] = f
        s = dot(ql, k, TN) * SCALE
        e = jnp.exp(s - jnp.max(s, axis=1, keepdims=True))
        b = (e / jnp.sum(e, axis=1, keepdims=True)).astype(bf16)
        b_ref[rows(base, HD), :] = b
        bv = dot(b, v, NT)
        z = z_ref[h]
        w = dot3(split(z), split(bv), NN)
        small_ref[0, h] = z
        small_ref[1, h] = bv
        small_ref[2, h] = w
        attended = dot(w.astype(bf16), f, TN)
        conv = dot(windows(vpad_ref, base), toeplitz(conv_ref[h, 0:1]), NT)
        ctx_ref[rows(base, HD), :] = (attended + unstack_blocks(conv)).astype(bf16)
        return 0

    for third in range(3):
        lax.fori_loop(third * 4, third * 4 + 4, head_step, 0, unroll=4)
        at = pl.ds(third * 4 * HD, 4 * HD)
        for src, dst in ((f_ref, f_out), (b_ref, b_out), (ctx_ref, ctx_out)):
            leave(src.at[at, :], dst.at[at, :])
        hook(6 + third)

    def out_step(i, _):
        at = rows(i * 384, 384)
        got = dot(w_ref[:, rows(3 * D + i * 384, 384)], ctx_ref[...], TN)
        xhat_ref[at, :] = got + par_ref[at, p + 2 : p + 3] + x_ref[at, :]
        return 0

    lax.fori_loop(0, 2, out_step, 0)
    norm_forward(xhat_ref, xhat_ref, rstd_ref)
    for copy in leaving:
        copy.wait()
    for k in range(NS_ITERS):
        pltpu.make_async_copy(ns_ref.at[k], ns_out.at[k], ns_sem.at[k]).wait()
    for i in range(9, 13):
        hook(i)


def attention(x, groups, par, conv, layer, lanes=(None, ())):
    first = layer == 0
    sizes = sizes_of(groups, layer)
    n = sizes[0][0]
    got = call(
        functools.partial(attention_kernel, sizes, 8 * layer), "attention",
        [sd(D, T, t=bf16), sd(3 * D, T, t=bf16), sd(2 * D, LM, t=bf16)] + [sd(D, 128)] * first
        + [
            sd(D, T, t=bf16), sd(D, T, t=bf16), sd(D, T, t=bf16), sd(HEADS, LM, LM),
            sd(NS_ITERS, 4, HEADS, LM, LM), sd(3, HEADS, LM, LM), sd(D, T), sd(8, T),
        ],
        [vm()] * (2 if first else 3) + anywhere(n * len(groups)),
        [ANY, ANY, vm()] + [vm()] * first + [ANY, ANY, ANY, vm(), ANY, vm(), vm(), vm()],
        [
            pltpu.VMEM((D, 4 * D), bf16), pltpu.VMEM((D, T + 2 * LEAD), bf16), pltpu.VMEM((HEADS, LM, LM), f32),
            DMA((len(groups), n)), pltpu.VMEM((D, T), bf16), pltpu.VMEM((3 * D, T), bf16), pltpu.VMEM((D, T), bf16),
            pltpu.VMEM((D, T), bf16), pltpu.VMEM((D, T), bf16), pltpu.VMEM((NS_ITERS, 4, HEADS, LM, LM), f32),
            DMA((16,)), DMA((NS_ITERS,)),
        ] + [pltpu.VMEM((D, 128), bf16), DMA((n,))] * first,
        (x, *([] if first else [par]), conv, *[piece for g in groups for piece in g]), lanes,
        6_800_000_000, 40_000_000, trans=2_000_000)
    return got if first else [*got[:3], par, *got[3:]]


def feed_kernel(n, p, last, xhat_ref, par_ref, inb_ref, *rest, hook):
    pieces1, pieces2, rest = rest[:n], rest[n : 2 * n], rest[2 * n :]
    a_ref, g_ref, xhat2_ref, rstd2_ref, next_ref, w1_ref, w2_ref, hl_ref, sem = rest
    j = pl.program_id(0)

    @pl.when(j == 0)
    def _():
        loads = loader(pieces1, w1_ref, sem.at[0])
        for copy in loads:
            copy.start()
        later = loader(pieces2, w2_ref, sem.at[1])
        for copy in later:
            copy.start()
        hook(0)
        h = xhat_ref[...] * par_ref[:, p + 6 : p + 7] + par_ref[:, p + 3 : p + 4]
        hl_ref[...] = h.astype(bf16)
        xhat2_ref[...] = h + par_ref[:, p + 4 : p + 5]
        for copy in loads + later:
            copy.wait()

    u = dot(w1_ref[:, rows(j * CHUNK, CHUNK)], hl_ref[...], TN)
    u = u + inb_ref[rows(j * CHUNK, CHUNK), 0:1]
    cdf = 0.5 + 0.5 * lax.erf(u * (2.0 ** -0.5))
    pdf = jnp.exp(-0.5 * u * u) * ((2.0 * np.pi) ** -0.5)
    a_ref[...] = (u * cdf).astype(bf16)
    g_ref[...] = (cdf + u * pdf).astype(bf16)
    xhat2_ref[...] += dot(w2_ref[rows(j * CHUNK, CHUNK), :], a_ref[...], TN)

    @pl.when(j == STEPS - 1)
    def _():
        norm_forward(xhat2_ref, xhat2_ref, rstd2_ref)
        y = xhat2_ref[...] * par_ref[:, p + 7 : p + 8] + par_ref[:, p + 5 : p + 6]
        if last:
            next_ref[...] = y.T.astype(bf16)
        else:
            next_ref[...] = y

    for i in range(STEPS):

        @pl.when(j == i)
        def _():
            hook(i + 1)

    @pl.when(j == STEPS - 1)
    def _():
        hook(STEPS + 1)


def feed(xhat, pieces1, pieces2, par, inb, layer, last, lanes=(None, ())):
    n = len(pieces1)
    chunk = pl.BlockSpec((CHUNK, T), lambda j: (j, 0))
    next_shape = (T, D) if last else (D, T)
    return call(
        functools.partial(feed_kernel, n, 8 * layer, last), "feed",
        [sd(FF, T, t=bf16), sd(FF, T, t=bf16), sd(D, T), sd(8, T), sd(*next_shape, t=bf16 if last else f32)],
        [whole(D, T), whole(D, 128), whole(FF, 1)] + anywhere(2 * n),
        [chunk, chunk, whole(D, T), whole(8, T), whole(*next_shape)],
        [pltpu.VMEM((D, FF), bf16), pltpu.VMEM((FF, D), bf16), pltpu.VMEM((D, T), bf16), DMA((2, n))],
        (xhat, par, inb, *pieces1, *pieces2), lanes, 9_800_000_000, 40_000_000, (STEPS,), 6_000_000)


def norm_backward(dy_ref, xhat_ref, rstd_ref, gain, out_ref, grads_ref, gain_col, shift_col, width=128):
    total_gain = jnp.zeros((D, width), f32)
    total_shift = jnp.zeros((D, width), f32)
    for c in range(0, T, width):
        dy = dy_ref[:, c : c + width]
        xhat = xhat_ref[:, c : c + width]
        total_shift = total_shift + dy
        total_gain = total_gain + dy * xhat
        dxhat = dy * gain
        m1 = jnp.mean(dxhat, axis=0, keepdims=True)
        m2 = jnp.mean(dxhat * xhat, axis=0, keepdims=True)
        out_ref[:, c : c + width] = rstd_ref[0:1, c : c + width] * (dxhat - m1 - xhat * m2)
    grads_ref[:, gain_col : gain_col + 1] = jnp.sum(total_gain, axis=1, keepdims=True)
    grads_ref[:, shift_col : shift_col + 1] = jnp.sum(total_shift, axis=1, keepdims=True)


def lane_sum(value):
    return jnp.sum(value.astype(f32), axis=1, keepdims=True)


def permute_rows(dst_ref, src_ref, order, block):
    for i in range(D // block):
        dst_ref[i * block : (i + 1) * block, :] = src_ref[
            rows(order.target(i) * block, block), :]


def hidden_kernel(n, p, first, sums_in, dy_ref, xhat_ref, rstd_ref, par_ref, a_ref, g_ref, *rest, hook):
    order = Order(n)
    pieces, (keep_ref, send_ref, du_ref, dr_ref, cols_ref, w_ref, dz_ref, inb_ref, sem) = rest[:n], rest[n:]
    j = pl.program_id(0)

    @pl.when(j == 0)
    def _():
        loads = loader(pieces, w_ref, sem)
        for copy in loads:
            copy.start()
        hook(0)
        if first:
            dr_ref[...] = dy_ref[...].astype(f32).T
            dy = dr_ref
        else:
            dy = dy_ref
        cols_ref[...] = sums_in[...]
        norm_backward(dy, xhat_ref, rstd_ref, par_ref[:, p + 7 : p + 8], dr_ref, cols_ref, p + 7, p + 5)
        dz_ref[...] = dr_ref[...].astype(bf16)
        cols_ref[:, p + 4 : p + 5] = lane_sum(dz_ref[...])
        hook(1)
        for copy in loads:
            copy.wait()

    def du_step(i, _):
        base = i * SUB
        da = dot(w_ref[rows(j * CHUNK + base, SUB), :], dz_ref[...], NN)
        du = (da * g_ref[rows(base, SUB), :].astype(f32)).astype(bf16)
        du_ref[rows(base, SUB), :] = du
        inb_ref[rows(base, SUB), :] = lane_sum(du)
        return 0

    lax.fori_loop(0, CHUNK // SUB, du_step, 0)
    half = CHUNK // 2
    core = order.core

    def own(start):
        return a_ref[rows(start, half), :]

    keep_ref[order.slot(j, 0)] = dot(own(core * half), dz_ref[...], NT).astype(bf16)
    send_ref[order.slot(j, 1)] = dot(own((1 - core) * half), dz_ref[...], NT).astype(bf16)
    for i in range(STEPS):

        @pl.when(j == i)
        def _():
            column = 2 * 8 + p // 2 + i
            cols_ref[:, column : column + 1] = inb_ref[...]
            hook(i + 2)


def hidden(sums, dy, xhat, rstd, par, a, g, pieces, layer, first, lanes=(None, ())):
    n = len(pieces)
    chunk = pl.BlockSpec((CHUNK, T), lambda j: (j, 0))
    half = CHUNK // 2
    return call(
        functools.partial(hidden_kernel, n, 8 * layer, first), "hidden",
        [
            sd(STEPS, half, D, t=bf16), sd(STEPS, half, D, t=bf16), sd(FF, T, t=bf16), sd(D, T), sd(D, 128),
        ],
        [whole(D, 128), whole(*dy.shape), whole(D, T), whole(8, T), whole(D, 128), chunk, chunk] + anywhere(n),
        [
            whole(STEPS, half, D), whole(STEPS, half, D), chunk, whole(D, T), whole(D, 128),
        ],
        [pltpu.VMEM((FF, D), bf16), pltpu.VMEM((D, T), bf16), pltpu.VMEM((CHUNK, 1), f32), pltpu.SemaphoreType.DMA((n,))],
        (sums, dy, xhat, rstd, par, a, g, *pieces), lanes, 9_700_000_000, 40_000_000, (STEPS,))


def inner_kernel(n, p, sums_in, du_ref, dr_ref, xhat_ref, rstd_ref, par_ref, *rest, hook):
    order = Order(n)
    pieces, (keep_ref, send_ref, out_ref, cols_ref, w_ref, hl_ref, acc_ref, sem) = rest[:n], rest[n:]
    j = pl.program_id(0)

    @pl.when(j == 0)
    def _():
        loads = loader(pieces, w_ref, sem)
        for copy in loads:
            copy.start()
        hook(0)
        block = D // 8
        for i in range(8):
            at = rows(order.target(i) * block, block)
            hl_ref[i * block : (i + 1) * block, :] = (
                xhat_ref[at, :] * par_ref[at, p + 6 : p + 7] + par_ref[at, p + 3 : p + 4]).astype(bf16)
        acc_ref[...] = dr_ref[...]
        for copy in loads:
            copy.wait()

    for i, ref in enumerate((keep_ref, send_ref)):
        ref[...] = dot(hl_ref[i * (D // 2) : (i + 1) * (D // 2), :], du_ref[...], NT).astype(bf16)

    def dh_step(i, _):
        acc_ref[rows(i * SUB, SUB), :] += dot(
            w_ref[rows(i * SUB, SUB), rows(j * CHUNK, CHUNK)], du_ref[...], NN)
        return 0

    lax.fori_loop(0, D // SUB, dh_step, 0)

    @pl.when(j == STEPS - 1)
    def _():
        cols_ref[...] = sums_in[...]
        norm_backward(acc_ref, xhat_ref, rstd_ref, par_ref[:, p + 6 : p + 7], out_ref, cols_ref, p + 6, p + 3)
        cols_ref[:, p + 2 : p + 3] = lane_sum(out_ref[...].astype(bf16))
    for i in range(STEPS):

        @pl.when(j == i)
        def _():
            hook(i + 1)


def inner(sums, du, dr, xhat, rstd, par, pieces, layer, lanes=(None, ())):
    n = len(pieces)
    return call(
        functools.partial(inner_kernel, n, 8 * layer), "inner",
        [sd(D // 2, FF, t=bf16), sd(D // 2, FF, t=bf16), sd(D, T), sd(D, 128)],
        [whole(D, 128), pl.BlockSpec((CHUNK, T), lambda j: (j, 0)), whole(D, T), whole(D, T), whole(8, T), whole(D, 128)]
        + anywhere(n),
        [
            pl.BlockSpec((D // 2, CHUNK), lambda j: (0, j)), pl.BlockSpec((D // 2, CHUNK), lambda j: (0, j)),
            whole(D, T), whole(D, 128),
        ],
        [pltpu.VMEM((D, FF), bf16), pltpu.VMEM((D, T), bf16), pltpu.VMEM((D, T), f32), pltpu.SemaphoreType.DMA((n,))],
        (sums, du, dr, xhat, rstd, par, *pieces), lanes, 9_700_000_000, 35_000_000, (STEPS,))


def row_loader(src, dst, order, sem):
    block = D // 8
    return [
        pltpu.make_async_copy(
            src.at[rows(order.target(i) * block, block), :], dst.at[pl.ds(i * block, block), :], sem.at[i])
        for i in range(8)]


def values_kernel(sizes, p, small_in, sums_in, dr1_ref, mix_from, ctx_from, f_from, b_from, xl_from, small_ref, conv_ref,
                  *rest, hook):
    order = Order(sizes[0][0])
    groups, rest = grouped(rest, sizes)
    (keep_ref, send_ref, dctx_out, dv_ref, dz_ref, dbv_ref, small_out, cols_ref,
     w_ref, dp_ref, perm_ref, vpad_ref, dpad_ref, dctx_ref, f_ref, b_ref, v_ref, xperm_ref, taps_ref,
     sem, perm_sem, late_sem) = rest
    early = column_loader(groups, sizes, w_ref, sem, 3 * D, 4 * D)
    perms = row_loader(ctx_from, perm_ref, order, perm_sem.at[0])
    late = [pltpu.make_async_copy(mix_from.at[pl.ds(2 * D, D), :], v_ref, late_sem.at[0]),
            pltpu.make_async_copy(f_from, f_ref, late_sem.at[1]),
            pltpu.make_async_copy(b_from, b_ref, late_sem.at[2])]
    last = row_loader(xl_from, xperm_ref, order, perm_sem.at[1])
    for copy in early + perms + late + last:
        copy.start()
    for ref in (vpad_ref, dpad_ref):
        ref[:, 0:LEAD] = jnp.zeros((D, LEAD), bf16)
        ref[:, LEAD + T :] = jnp.zeros((D, LEAD), bf16)
    dp_ref[...] = dr1_ref[...].astype(bf16)
    hook(0)
    for copy in early:
        copy.wait()

    def dctx_step(i, _):
        at = rows(i * 384, 384)
        got = dot(w_ref[at, :], dp_ref[...], NN).astype(bf16)
        dctx_ref[at, :] = got
        dpad_ref[at, LEAD : LEAD + T] = got
        return 0

    lax.fori_loop(0, 2, dctx_step, 0)
    hook(1)
    leave = pltpu.make_async_copy(dctx_ref, dctx_out, late_sem.at[3])
    leave.start()
    for copy in perms:
        copy.wait()
    for i, ref in enumerate((keep_ref, send_ref)):
        ref[:, 0:D] = dot(perm_ref[i * (D // 2) : (i + 1) * (D // 2), :], dp_ref[...], NT).astype(bf16)
    for copy in late:
        copy.wait()
    vpad_ref[:, LEAD : LEAD + T] = v_ref[...]
    hook(2)
    flip = jnp.where(
        lax.broadcasted_iota(jnp.int32, (CONV_N, CONV_N), 0)
        + lax.broadcasted_iota(jnp.int32, (CONV_N, CONV_N), 1) == CONV_N - 1, 1.0, 0.0).astype(bf16)

    def value_step(h, _):
        base = h * HD
        dctx = dctx_ref[rows(base, HD), :]
        f = f_ref[rows(base, HD), :]
        dw = split(dot(f, dctx, NT))
        dz_ref[h] = dot3(dw, split(small_ref[1, h]), NT)
        dbv = dot3(split(small_ref[0, h]), dw, TN).astype(bf16)
        dbv_ref[h] = dbv
        dv = dot(dbv, b_ref[rows(base, HD), :], TN)
        conv = dot(windows(dpad_ref, base), toeplitz(conv_ref[h, 1:2]), NT)
        dv_ref[rows(base, HD), :] = (dv + unstack_blocks(conv)).astype(bf16)
        flipped = dot(stack_blocks(dctx), flip, NN).astype(bf16)
        g = dot(flipped, windows(vpad_ref, base), TN)
        g = pltpu.roll(g, CONV_K - CONV_N + 1 - (LEAD - RADIUS), 1, stride=1, stride_axis=0)
        taps_ref[pl.ds(h, 1), :] = jnp.sum(g[:, 0:128], axis=0, keepdims=True)
        return 0

    lax.fori_loop(0, HEADS // 2, value_step, 0, unroll=2)
    hook(3)
    lax.fori_loop(HEADS // 2, HEADS, value_step, 0, unroll=2)
    hook(4)
    for copy in last:
        copy.wait()
    for i, ref in enumerate((keep_ref, send_ref)):
        ref[:, D:] = dot(xperm_ref[i * (D // 2) : (i + 1) * (D // 2), :], dv_ref[...], NT).astype(bf16)
    cols_ref[...] = sums_in[...]
    cols_ref[:, p + 1 : p + 2] = lane_sum(dv_ref[...])
    first = p // 8 * HEADS
    small_out[...] = small_in[...]
    small_out[:, 0:D] = cols_ref[...].T[0:SMALL, :]
    small_out[first : first + HEADS, D:] = taps_ref[...]
    leave.wait()
    hook(5)


def values(total, sums, dr1, mix, ctx, f, b, xl, small, conv, groups, layer, lanes=(None, ())):
    sizes = sizes_of(groups, layer)
    n = sizes[0][0]
    return call(
        functools.partial(values_kernel, sizes, 8 * layer), "values",
        [
            sd(D // 2, 2 * D, t=bf16), sd(D // 2, 2 * D, t=bf16), sd(D, T, t=bf16), sd(D, T, t=bf16),
            sd(HEADS, LM, LM), sd(HEADS, LM, LM, t=bf16), sd(SMALL, D + 128), sd(D, 128),
        ],
        [vm(), vm(), vm()] + [ANY] * 5 + [vm(), vm()] + anywhere(n * len(groups)),
        [vm(), vm(), ANY] + [vm()] * 5,
        [
            pltpu.VMEM((D, D), bf16), pltpu.VMEM((D, T), bf16), pltpu.VMEM((D, T), bf16),
            pltpu.VMEM((D, T + 2 * LEAD), bf16), pltpu.VMEM((D, T + 2 * LEAD), bf16),
        ] + [pltpu.VMEM((D, T), bf16)] * 5 + [pltpu.VMEM((HEADS, 128), f32), DMA((len(groups), n)), DMA((2, 8)), DMA((4,))],
        (total, sums, dr1, mix, ctx, f, b, xl, small, conv, *[piece for g in groups for piece in g]), lanes,
        6_200_000_000, 25_000_000)


QK = 2 * D
QK_HEADS = ((0, 8), (8, 4))
TURNS = 20


def back_kernel(sizes, p, out, tail, sums_in, ns_from, mix_from, dctx_from, f_from, b_from, dv_from, xl_from, dr1_from,
                lm_ref, a_ref, small_ref, dz0_ref, dbv_ref, *rest, hook):
    order = Order(sizes[0][0])
    groups, rest = grouped(rest, sizes)
    if out:
        keep_ref, send_ref, *rest = rest
    dx_ref, cols_ref, *rest = rest
    if not out:
        keep_ref, send_ref, *rest = rest
    (w_ref, ns_ref, mix_ref, dctx_ref, f_ref, b_ref, dv_ref, perm_ref, dr1_ref, dz_ref, da_ref,
     sem, ns_sem, late_sem, perm_sem) = rest

    def load_ns(i):
        return pltpu.make_async_copy(
            ns_from.at[NS_ITERS - 1 - i], ns_ref.at[lax.rem(i, 2)], ns_sem.at[lax.rem(i, 2)])

    load_ns(0).start()
    late = [
        pltpu.make_async_copy(src, dst, late_sem.at[i]) for i, (src, dst) in enumerate((
            (mix_from, mix_ref), (dctx_from, dctx_ref), (f_from, f_ref), (b_from, b_ref), (dv_from, dv_ref),
            (dr1_from, dr1_ref)))]
    late += row_loader(xl_from, perm_ref, order, perm_sem)
    late += column_loader(groups, sizes, w_ref, sem, 0, 3 * D)
    for lane in tail:
        lane.use(keep_ref, send_ref, cols_ref)
    for copy in late:
        copy.start()
    hook(0)
    for h in range(HEADS):
        da_ref[h] = jnp.zeros((LM, LM), f32)
        dz_ref[h] = dz0_ref[h]

    def ns_step(i, _):
        k = lax.rem(i, 2)
        load_ns(i).wait()

        @pl.when(i + 1 < NS_ITERS)
        def _():
            load_ns(i + 1).start()

        d3, dzs, dps, d2 = [], [], [], []
        for h in range(HEADS):
            dzn = split(0.25 * dz_ref[h])
            d3.append(split(dot3(split(ns_ref[k, 0, h]), dzn, TN)))
            dz_ref[h] = dot3(dzn, split(ns_ref[k, 3, h]), NT)
        for h in range(HEADS):
            p = split(ns_ref[k, 1, h])
            d2.append(split(-dot3(p, d3[h], TN)))
            dps.append(dot3(d3[h], split(ns_ref[k, 2, h]), NT))
        for h in range(HEADS):
            p = ns_ref[k, 1, h]
            d1 = dot3(split(p), d2[h], TN)
            dp = d1 - dps[h] - dot3(d2[h], split(eye(7.0) - p), NT)
            dps[h] = split(dp)
        for h in range(HEADS):
            da_ref[h] += dot3(dps[h], split(ns_ref[k, 0, h]), NT)
            dz_ref[h] += dot3(split(a_ref[h]), dps[h], TN)
        return 0

    lax.fori_loop(0, NS_ITERS // 2, ns_step, 0)
    hook(1)
    lax.fori_loop(NS_ITERS // 2, NS_ITERS, ns_step, 0)
    for copy in late:
        copy.wait()
    hook(2)
    spread = segment_spread()

    def score_step(h, _):
        base = h * HD
        a = a_ref[h]
        dz0 = dz_ref[h].T
        s = 1.0 / jnp.sum(a * a)
        da = da_ref[h] + s * dz0 - (2.0 * s * s * jnp.sum(dz0 * a)) * a
        dsa = (SCALE * a * (da - jnp.sum(a * da, axis=1, keepdims=True))).astype(bf16)
        ql = lm_ref[rows(base, HD), :]
        kl = lm_ref[rows(D + base, HD), :]
        q = mix_ref[rows(base, HD), :]
        k = mix_ref[rows(D + base, HD), :]
        f = f_ref[rows(base, HD), :].astype(f32)
        df = dot(small_ref[2, h].astype(bf16), dctx_ref[rows(base, HD), :], NN)
        dsf = (SCALE * f * (df - jnp.sum(f * df, axis=0, keepdims=True))).astype(bf16)
        b = b_ref[rows(base, HD), :].astype(f32)
        db = dot(dbv_ref[h], mix_ref[rows(2 * D + base, HD), :], NN)
        dsb = (SCALE * b * (db - jnp.sum(b * db, axis=1, keepdims=True))).astype(bf16)
        dkl = dot(q, dsf, NT) + dot(ql, dsa, NN)
        dql = dot(kl, dsa, NT) + dot(k, dsb, NT)
        dq = dot(kl, dsf, NN) + dot((dql * (1.0 / SEG)).astype(bf16), spread, NN)
        dk = dot(ql, dsb, NN) + dot((dkl * (1.0 / SEG)).astype(bf16), spread, NN)
        mix_ref[rows(base, HD), :] = dq.astype(bf16)
        mix_ref[rows(D + base, HD), :] = dk.astype(bf16)
        return 0

    half = D // 2
    at = 0
    for part, (head, heads) in enumerate(QK_HEADS):
        middle = head + heads // 2
        lax.fori_loop(head, middle, score_step, 0, unroll=heads // 2)
        hook(3 + 2 * part)
        lax.fori_loop(middle, head + heads, score_step, 0, unroll=heads // 2)
        if head + heads == HEADS:
            cols_ref[...] = sums_in[...]
            cols_ref[:, p : p + 1] = lane_sum(mix_ref[0:D, :])
        width = heads * HD
        for k in range(2):
            d = mix_ref[k * D + head * HD : k * D + head * HD + width, :]
            for side, ref in ((1, send_ref), (0, keep_ref)):
                mine = perm_ref[side * half : (side + 1) * half, :]
                ref[:, at : at + width] = dot(mine, d, NT).astype(bf16)
            at += width
        hook(4 + 2 * part)
    for i in range(3):
        at = slice(i * 256, (i + 1) * 256)
        got = dr1_ref[at, :] + dot(w_ref[at, 0:QK], mix_ref[0:QK, :], NN) + dot(w_ref[at, QK:], dv_ref[...], NN)
        if p:
            dx_ref[at, :] = got
        else:
            dx_ref[:, at] = got.T
        hook(7 + i)
    for i in range(10, TURNS):
        hook(i)


def back(sums, ns, mix, dctx, f, b, dv, xl, dr1, lm, a, small, dz0, dbv, groups, layer, lanes=(None, ()), tail=(), on=False):
    sizes = sizes_of(groups, layer)
    n = sizes[0][0]
    halves = [(D // 2, QK)] * 2
    out = 0 if on and layer == 0 else 1
    got = call(
        functools.partial(back_kernel, sizes, 8 * layer, out, tail), "back",
        [sd(*h, t=bf16) for h in halves] * out + [sd(*((D, T) if layer else (T, D))), sd(D, 128)],
        [vm()] + [ANY] * 8 + [vm()] * 5 + anywhere(n * len(groups)), [vm()] * (2 + 2 * out),
        [pltpu.VMEM(h, bf16) for h in halves] * (1 - out) + [
            pltpu.VMEM((D, 3 * D), bf16), pltpu.VMEM((2, 4, HEADS, LM, LM), f32), pltpu.VMEM((3 * D, T), bf16),
        ] + [pltpu.VMEM((D, T), bf16)] * 5 + [
            pltpu.VMEM((D, T), f32), pltpu.VMEM((HEADS, LM, LM), f32), pltpu.VMEM((HEADS, LM, LM), f32),
            DMA((len(groups), n)), DMA((2,)), DMA((6,)), DMA((8,)),
        ],
        (sums, ns, mix, dctx, f, b, dv, xl, dr1, lm, a, small, dz0, dbv, *[piece for g in groups for piece in g]),
        lanes, 10_000_000_000, 50_000_000)
    return got if out else [None, None, *got]


class Ring:
    def __init__(self, wide, narrow):
        self.wide, self.narrow = wide, narrow
        self.bits = wide.bit_length() - 1
        up = list(range(1, self.bits))
        self.gather_order = (up, up[::-1])
        self.scatter_order = (up[::-1], up)
        self.exact = wide == 8 and narrow == 4

    def pairs(self, flip):
        n = self.narrow
        out = []
        for w in range(self.wide):
            for z in range(n):
                to_w, to_z = flip(w, z)
                out.append((w * n + z, to_w * n + to_z))
        return out

    def narrow_pairs(self, k):
        return self.pairs(lambda w, z: (w, z ^ k))

    def step_pairs(self, order, s):
        return self.pairs(lambda w, z: (w ^ (1 << order[w & 1][s]), z))

    def core_pairs(self):
        return self.pairs(lambda w, z: (w ^ 1, z))

    def gathered(self, w):
        out = []
        for other in (0, 1):
            v = w ^ other
            for code in range(self.wide // 2):
                t = v
                for s in range(self.bits - 1):
                    if code >> s & 1:
                        t ^= 1 << self.gather_order[v & 1][s]
                out.append(t)
        return out

    def slots(self, w):
        out = []
        for other in (0, 1):
            v = w ^ other
            for code in range(self.wide // 2):
                t = v
                for s in range(self.bits - 1):
                    if code >> (self.bits - 2 - s) & 1:
                        t ^= 1 << self.scatter_order[v & 1][s]
                out.append(t)
        return out

    def mine(self, table):
        return lax.dynamic_index_in_dim(jnp.asarray(table), lax.axis_index("wide"), 0, keepdims=False)

    def gather(self, shard):
        z = lax.axis_index("narrow")
        parts = [shard] + [lax.ppermute(shard, AXES, self.narrow_pairs(k)) for k in range(1, self.narrow)]
        yield []
        bit = 1
        while bit < self.narrow:
            swap = (z & bit) != 0
            parts = [jnp.where(swap, parts[k ^ bit], parts[k]) for k in range(self.narrow)]
            bit *= 2
        held = [jnp.concatenate(parts, axis=0)]
        got = held
        for s in range(self.bits - 1):
            pairs = self.step_pairs(self.gather_order, s)
            fresh, got = got, [lax.ppermute(h, AXES, pairs) for h in held]
            held = held + got
            yield fresh
        other = [lax.ppermute(h, AXES, self.core_pairs()) for h in held]
        yield got
        held = held + other
        return held if self.exact else [self.join(held)]

    def join(self, pieces):
        inverse = np.stack([np.argsort(self.gathered(w)) for w in range(self.wide)]).astype(np.int32)
        stacked = jnp.stack(pieces)
        return jnp.take(stacked, self.mine(inverse), axis=0).reshape(-1, stacked.shape[-1])

    def scatter(self, keep, send):
        half = self.wide // 2
        if not self.exact:
            slots = np.stack([self.slots(w) for w in range(self.wide)]).astype(np.int32)
            whole = jnp.concatenate([keep, send], axis=0)
            whole = whole.reshape(self.wide, -1, whole.shape[-1])
            whole = jnp.take(whole, self.mine(slots), axis=0)
            keep, send = whole[:half], whole[half:]
        got = lax.ppermute(send, AXES, self.core_pairs())
        yield [send]
        total = keep.astype(f32) + got.astype(f32)
        for s in range(self.bits - 1):
            half //= 2
            away = total[half:].astype(bf16)
            got = lax.ppermute(away, AXES, self.step_pairs(self.scatter_order, s))
            yield [away]
            total = total[:half] + got.astype(f32)
        total = total[0]
        size = total.shape[0] // self.narrow
        z = lax.axis_index("narrow")
        own = lax.dynamic_slice_in_dim(total, z * size, size, axis=0)
        low = total.astype(bf16)
        parts = [lax.dynamic_slice_in_dim(low, (z ^ k) * size, size, axis=0) for k in range(1, self.narrow)]
        got = [lax.ppermute(parts[k - 1], AXES, self.narrow_pairs(k)) for k in range(1, self.narrow)]
        yield parts
        for part in got:
            own = own + part.astype(f32)
        return own

    def sum(self, keep, send):
        blocks = self.wide // 2
        return finish(self.scatter(
            keep.reshape(blocks, -1, keep.shape[-1]), send.reshape(blocks, -1, send.shape[-1])))

    def total(self, value):
        bit = 1
        while bit < self.narrow:
            value = value + lax.ppermute(value, AXES, self.narrow_pairs(bit))
            bit *= 2
        for s in range(self.bits - 1):
            value = value + lax.ppermute(value, AXES, self.pairs(lambda w, z: (w ^ (2 << s), z)))
        return value + lax.ppermute(value, AXES, self.core_pairs())


def natural_halves(keep, send):
    both = jnp.stack([keep, send], axis=1)
    both = both.reshape(2, -1, both.shape[-1])
    return both[0], both[1]


def conv_rows(conv):
    at = LEAD - RADIUS
    tail = CONV_K - at - KSIZE
    both = jnp.stack([conv, conv[:, ::-1]], axis=1)
    return jnp.pad(both.astype(f32), ((0, 0), (0, 0), (at, tail)))


def finish(steps):
    while True:
        try:
            next(steps)
        except StopIteration as end:
            return end.value


def small_outputs(ring, total, size, hidden_size):
    layers = total.shape[0] // (8 + STEPS)
    here = lax.axis_index("wide") * ring.narrow + lax.axis_index("narrow")
    lines = total[: 8 * layers, :D].reshape(layers, 8, D)
    lines = lax.dynamic_slice_in_dim(lines, here * size, size, axis=2)
    inb = total[8 * layers :, :D].reshape(layers, FF)
    inb = lax.dynamic_slice_in_dim(inb, here * hidden_size, hidden_size, axis=1)
    taps = total[:, D : D + KSIZE].reshape(layers, HEADS, KSIZE)
    return lines[:, :6], lines[:, 6:], inb, taps


def small_shard(in_b, bias_rows, gain_rows):
    layers, size = bias_rows.shape[0], bias_rows.shape[2]
    columns = jnp.concatenate([bias_rows, gain_rows], axis=1).transpose(2, 0, 1).reshape(size, 8 * layers)
    inner_bias = in_b.reshape(layers, size, -1).transpose(1, 0, 2).reshape(size, -1)
    small = jnp.concatenate([columns, inner_bias], axis=1)
    return jnp.pad(small, ((0, 0), (0, 128 - small.shape[1])))


def gather_all(ring, attention_shards, in_w, out2_w):
    layers = in_w.shape[0]
    return (
        [finish(ring.gather(shard)) for shard in attention_shards],
        [finish(ring.gather(in_w[layer])) for layer in range(layers)],
        [finish(ring.gather(out2_w[layer])) for layer in range(layers)],
    )


class Plan:
    def __init__(self):
        self.count = 0

    def lanes(self, *lanes):
        self.count += 1
        return (self.count, list(lanes))


def body(ring, tokens, cotangent, qkv_w, out_w, in_w, in_b, out2_w, bias_rows, gain_rows, conv_w):
    layers = qkv_w.shape[0]
    size = qkv_w.shape[1]
    small = small_shard(in_b, bias_rows, gain_rows)
    plan = Plan()
    none = (None, ())
    on = ring.exact and layers == 2
    conv = [conv_rows(conv_w[layer]) for layer in range(layers)]
    on_attention, on_feed = [none] * layers, [none] * layers
    qkvo = [jnp.concatenate([qkv_w[layer], out_w[layer]], axis=1) for layer in range(layers)]
    if on:
        s1 = Spread(jnp.concatenate([qkvo[0][:, : 2 * D], small], axis=1), 0, 1)
        s2 = Spread(qkvo[0][:, 2 * D :], 1, 3)
        g1, g2 = Gather(s1), Gather(s2)
        s3 = Spread(in_w[0], 3, 8)
        g3 = Gather(s3)
        m1 = g1.go(a=(1, 2), b=(2, 4), core0=(1, 8), core1=(2, 8), core2=(4, 8))
        m2 = g2.go(apart=1, a=(3, 5), b=(5, 7), core0=(3, 9), core1=(5, 9), core2=(7, 9))
        x = exchange(tokens, plan.lanes(s1, s2, *m1, *m2, s3), 10)
        att = [[g1.pieces(), g2.pieces()], None]
        win, wout = [None] * 2, [None] * 2
        s4, s5 = Spread(out2_w[0], 0, 6), Spread(qkvo[1], 6, 10)
        g4 = Gather(s4)
        m3 = g3.go(a=(0, 4), b=(4, 9), core0=(0, 4), core1=(4, 9), core2=(9, 11))
        m4 = g4.go(apart=1, a=(6, 8), b=(8, 10), core0=(6, 9), core1=(8, 10), core2=(10, 12))
        g5 = Gather(s5)
        m5 = g5.go(a=(10, 12))
        on_attention[0] = plan.lanes(s4, *m3, *m4, s5, *m5)
    else:
        x = tokens.T.astype(f32)
        shards = [jnp.concatenate([qkvo[0], small], axis=1)] + qkvo[1:]
        att, win, wout = gather_all(ring, shards, in_w, out2_w)
        att = [[pieces] for pieces in att]

    kept = []
    par = None
    for layer in range(layers):
        final = layer == layers - 1
        xl, mix, lm, par, ctx, f, b, a, ns, sm, xhat1, rstd1 = attention(
            x, att[layer], par, conv[layer], layer, on_attention[layer])
        if on and layer == 0:
            win[0], wout[0] = g3.pieces(), g4.pieces()
            s6, s7 = Spread(in_w[1], 0, 3), Spread(out2_w[1], 3, 5)
            g6, g7 = Gather(s6), Gather(s7)
            m5 = g5.go(apart=1, b=(0, 3), core0=(0, 3), core1=(0, 3), core2=(3, 5))
            m6 = g6.go(a=(3, 5))
            on_feed[0] = plan.lanes(*m5, s6, s7, *m6)
        if on and layer == 1:
            win[1], wout[1] = g6.pieces(), g7.pieces()
        at = 8 * layers + FF // D * layer
        inb = par[:, at : at + FF // D].reshape(FF, 1)
        act, slope, xhat2, rstd2, x = feed(
            xhat1, win[layer], wout[layer], par, inb, layer, final, on_feed[layer])
        if on and layer == 0:
            att[1] = [g5.pieces()]
            m6 = g6.go(b=(0, 6), core0=(0, 6), core1=(0, 6), core2=(6, 11))
            m7 = g7.go(apart=1, a=(0, 6), b=(6, 10), core0=(0, 6), core1=(6, 10), core2=(10, 12))
            on_attention[1] = plan.lanes(*m6, *m7)
        kept.append((xl, mix, lm, ctx, f, b, a, ns, sm, xhat1, rstd1, act, slope, xhat2, rstd2))
    output = x

    dy = cotangent
    sums = jnp.zeros((D, 128), f32)
    total = jnp.zeros((SMALL, D + 128), f32)
    grads = [{} for _ in range(layers)]
    firsts, thirds, ends = {}, {}, []

    def sum_first(keep, send, turns, layer, place):
        firsts[layer, place] = ReduceFirst(keep, send, turns)
        return firsts[layer, place]

    def sum_third(layer, place, turns):
        thirds[layer, place] = Third(*firsts[layer, place].value, turns)
        return thirds[layer, place]

    def ending(lane, layer, place):
        ends.append((lane, layer, place))
        return lane

    def sum_final(layer, place, turns):
        return ending(Final(*thirds[layer, place].value, turns), layer, place)

    def sum_last(layer, place, turns):
        return ending(ReduceLast(*firsts[layer, place].value, turns), layer, place)

    halves = None
    for layer in reversed(range(layers)):
        xl, mix, lm, ctx, f, b, a, ns, sm, xhat1, rstd1, act, slope, xhat2, rstd2 = kept[layer]
        above = layer + 1 < layers
        lane = none
        if on and above:
            firsts[layer + 1, "ov"] = Plane(*core_ov.value, (0, 5))
            lane = plan.lanes(
                sum_first(*halves, (0, 1, 5), layer + 1, "qk"), firsts[layer + 1, "ov"],
                sum_final(layer + 1, "in", (0, 5)))
        keep, send, du, dr2, sums = hidden(
            sums, dy, xhat2, rstd2, par, act, slope, wout[layer], layer, not above, lane)
        if on:
            out2 = (keep.reshape(-1, D), send.reshape(-1, D))
            if above:
                lane = [
                    sum_first(*out2, (0, 1, 4), layer, "out2"),
                    sum_third(layer + 1, "qk", (0, 3)), sum_third(layer + 1, "ov", (0, 3))]
            else:
                core2 = Core(*out2, (0, 2))
                lane = [core2]
            lane = plan.lanes(*lane)
        else:
            grads[layer]["out2"] = ring.sum(*natural_halves(keep, send))
        keep, send, dr1, sums = inner(sums, du, dr2, xhat1, rstd1, par, win[layer], layer, lane)
        if on:
            core1 = Core(keep, send, (0, 3))
            if above:
                lane = [
                    sum_third(layer, "out2", (0, 5)), sum_first(keep, send, (0, 1, 5), layer, "in"),
                    sum_final(layer + 1, "qk", (0, 5)), sum_final(layer + 1, "ov", (0, 5))]
            else:
                core1 = Core(keep, send, (0, 3))
                firsts[layer, "out2"] = Plane(*core2.value, (0, 5))
                lane = [firsts[layer, "out2"], core1]
            lane = plan.lanes(*lane)
        else:
            grads[layer]["in"] = ring.sum(keep, send)
        keep, send, dctx, dv, dz, dbv, total, sums = values(
            total, sums, dr1, mix, ctx, f, b, xl, sm, conv[layer], att[layer], layer, lane)
        tail = []
        if on:
            if layer:
                core_ov = Core(keep, send, (0, 2))
                lead = Plane(*core1.value, (0, 4), chained=True)
                thirds[layer, "in"] = Third(None, None, (4, 10), inside=lead)
                lane = [sum_last(layer, "out2", (0, 3, 10)), lead, thirds[layer, "in"], core_ov]
            else:
                late = Total(total, (6, 8, 10, 11, 13, 15))
                lane, tail = [late], [late]
                starts = (0, 2 * QK_HEADS[0][1] * HD, QK)
                for part, (go, end) in enumerate((((4, 5, 8), (8, 11, 14)), ((6, 9, 11), (11, 13, 15)))):
                    lead = ReduceFirst(None, None, go, chained=True, columns=slice(starts[part], starts[part + 1]))
                    tail.append(lead)
                    lane = [lead, ending(ReduceLast(None, None, end, inside=lead), 0, f"qk{part}")] + lane
                lead = ReduceFirst(keep, send, (0, 1, 3), chained=True)
                lane += [
                    sum_final(0, "out2", (0, 4)), sum_last(0, "in", (0, 2, 6)), lead,
                    ending(ReduceLast(None, None, (3, 4, 10), inside=lead), 0, "ov")]
            lane = plan.lanes(*lane)
        else:
            grads[layer]["ov"] = ring.sum(keep, send)
        keep, send, dy, sums = back(
            sums, ns, mix, dctx, f, b, dv, xl, dr1, lm, a, sm, dz, dbv, att[layer], layer, lane, tuple(tail), on)
        halves = (keep, send)
        if not on:
            grads[layer]["qk"] = ring.sum(keep, send)
    if on:
        for lane, layer, place in ends:
            grads[layer][place] = lane.value
        grads[0]["qk"] = jnp.concatenate([grads[0]["qk0"], grads[0]["qk1"]], axis=1)
        total = late.value
    else:
        total = ring.total(jnp.concatenate([sums.T[:SMALL], total[:, D:]], axis=1))
    gbias, ggain, ginb, gtaps = small_outputs(ring, total, size, in_b.shape[1])
    first = 2 * QK_HEADS[0][1] * HD
    cut, rest = first // 2, (QK - first) // 2
    stacked = [
        jnp.stack([
            jnp.concatenate([
                g["qk"][:, :cut], g["qk"][:, first : first + rest], g["qk"][:, cut:first], g["qk"][:, first + rest :],
                g["ov"][:, D:]], axis=1) for g in grads]),
        jnp.stack([g["ov"][:, :D] for g in grads]),
        jnp.stack([g["in"] for g in grads]),
        jnp.stack([g["out2"] for g in grads])]
    return (output, dy, stacked[0], stacked[1], stacked[2], ginb, stacked[3], gbias, ggain, gtaps)


def solution(mesh):
    ring = Ring(mesh.shape["wide"], mesh.shape["narrow"])
    rows3 = P(None, AXES, None)
    columns3 = P(None, None, AXES)
    weights = (rows3, rows3, rows3, P(None, AXES), rows3, columns3, columns3, P())
    return jax.shard_map(
        functools.partial(body, ring),
        mesh=mesh,
        in_specs=(P(AXES, None), P(AXES, None)) + weights,
        out_specs=(P(AXES, None), P(AXES, None)) + weights,
        check_vma=False,
    )
```
